128 devices in a mesh: dp: 16 (over y, x_hi, core), group: 8 (over z, x_lo).
Axes of the slice: x: 4 (x_hi: 2, x_lo: 2; x = x_hi * 2 + x_lo), y: 4, z: 4, core: 2. Of those that a mesh axis runs over, the one named last changes fastest.
Arguments:
- tokens: bfloat16 [32, 1024, 1024], P('dp', 'group'), may hold values from -6 to 6
- cotangent: bfloat16 [32, 1024, 1024], P('dp', 'group'), may hold values from -6 to 6
- lengths: int32 [32], P('dp'), may hold values from 256 to 1024, as said below
- step_rate: float32 [1], replicated, may hold values from 0.1 to 0.4
- in_weight: float32 [1024, 3072], P('group'), may hold values from -0.1875 to 0.1875
- out_weight: float32 [1024, 1024], P('group'), may hold values from -0.1875 to 0.1875
- conv_weight: float32 [3, 1024], P(None, 'group'), may hold values from -3.5 to 3.5
- gain_mixer: float32 [1024], P('group'), may hold values from 0.5 to 1.5
- gain_feed: float32 [1024], P('group'), may hold values from 0.5 to 1.5
- gate_weight: float32 [1024, 4608], P('group'), may hold values from -0.1875 to 0.1875
- up_weight: float32 [1024, 4608], P('group'), may hold values from -0.1875 to 0.1875
- down_weight: float32 [4608, 1024], P('group'), may hold values from -0.1875 to 0.1875
- in_moment: float32 [1024, 3072], P('group'), may hold values from -0.011048543 to 0.011048543
- out_moment: float32 [1024, 1024], P('group'), may hold values from -0.011048543 to 0.011048543
- conv_moment: float32 [3, 1024], P(None, 'group'), may hold values from -0.011048543 to 0.011048543
- mixer_moment: float32 [1024], P('group'), may hold values from -0.011048543 to 0.011048543
- feed_moment: float32 [1024], P('group'), may hold values from -0.011048543 to 0.011048543
- gate_moment: float32 [1024, 4608], P('group'), may hold values from -0.011048543 to 0.011048543
- up_moment: float32 [1024, 4608], P('group'), may hold values from -0.011048543 to 0.011048543
- down_moment: float32 [4608, 1024], P('group'), may hold values from -0.011048543 to 0.011048543
Outputs:
- block_out: bfloat16 [32, 1024, 1024], P('dp', 'group')
- grad_tokens: bfloat16 [32, 1024, 1024], P('dp', 'group')
- in_updated: float32 [1024, 3072], P('group')
- out_updated: float32 [1024, 1024], P('group')
- conv_updated: float32 [3, 1024], P(None, 'group')
- mixer_updated: float32 [1024], P('group')
- feed_updated: float32 [1024], P('group')
- gate_updated: float32 [1024, 4608], P('group')
- up_updated: float32 [1024, 4608], P('group')
- down_updated: float32 [4608, 1024], P('group')
- in_momentum: float32 [1024, 3072], P('group')
- out_momentum: float32 [1024, 1024], P('group')
- conv_momentum: float32 [3, 1024], P(None, 'group')
- mixer_momentum: float32 [1024], P('group')
- feed_momentum: float32 [1024], P('group')
- gate_momentum: float32 [1024, 4608], P('group')
- up_momentum: float32 [1024, 4608], P('group')
- down_momentum: float32 [4608, 1024], P('group')
The draws below stay inside these ranges and needn't reach their ends.
Inputs may be any that keep to these rules, and one draw needn't show every extreme that they name: `lengths`: among the 2 slots of each index of dp, at least one has length 1024.
All inputs are finite; a program needn't handle non-finite values.
Results may differ from the reference program's by a relative error of at most 0.009.
The reference program's roundings to bfloat16 on the way count: a program that leaves them out, or rounds other values in their place, can miss the bound.
Values may be sent and summed in bfloat16 or wider, within the bound.
No kernel may reach another device: no remote copies, remote signals or barrier semaphores. Data moves between devices by JAX's collectives and lax.ppermute only.
A program may use at most 320 MiB of HBM per device.

```python
import math
import jax
import jax.numpy as jnp
from jax import lax

D = 1024
FF = 4608
K = 3
LEN = 1024
SLOTS = 2
SLOTS_ALL = 32


def moment_field(key, rows, cols, along):
    noise_key = jax.random.fold_in(key, 0)
    cross_key = jax.random.fold_in(key, 2)
    gauss = jnp.clip(jax.random.normal(noise_key, (rows, cols), jnp.float32), -4.0, 4.0)
    noise = gauss
    if along == 0:
        rise = (10.0 ** (jnp.arange(rows, dtype=jnp.float32) / rows))[:, None]
        cross = jnp.exp(jax.random.uniform(cross_key, (1, cols), jnp.float32, 0.0, math.log(10.0)))
    else:
        rise = (10.0 ** (jnp.arange(cols, dtype=jnp.float32) / cols))[None, :]
        cross = jnp.exp(jax.random.uniform(cross_key, (rows, 1), jnp.float32, 0.0, math.log(10.0)))
    magnitude = 0.004 / math.sqrt(SLOTS_ALL * LEN)
    return magnitude * noise * rise * cross


def draw_lengths(key, part):
    key = jax.random.fold_in(key, 3)
    base_key, pick_key = jax.random.split(key)
    groups = SLOTS_ALL // SLOTS
    base = jax.random.randint(base_key, (groups, SLOTS), LEN // 4, LEN + 1)
    pick = jax.random.randint(pick_key, (groups, 1), 0, SLOTS)
    full = jnp.arange(SLOTS, dtype=jnp.int32)[None, :] == pick
    return jnp.where(full, LEN, base).reshape(SLOTS_ALL).astype(jnp.int32)


def draw_in_moment(key, part):
    key = jax.random.fold_in(key, 11)
    return moment_field(key, D, 3 * D, 0)


def draw_out_moment(key, part):
    key = jax.random.fold_in(key, 12)
    return moment_field(key, D, D, 0)


def draw_conv_moment(key, part):
    key = jax.random.fold_in(key, 13)
    return moment_field(key, K, D, 1)


def draw_mixer_moment(key, part):
    key = jax.random.fold_in(key, 14)
    return moment_field(key, D, 1, 0).reshape(D)


def draw_feed_moment(key, part):
    key = jax.random.fold_in(key, 15)
    return moment_field(key, D, 1, 0).reshape(D)


def draw_gate_moment(key, part):
    key = jax.random.fold_in(key, 16)
    return moment_field(key, D, FF, 0)


def draw_up_moment(key, part):
    key = jax.random.fold_in(key, 17)
    return moment_field(key, D, FF, 0)


def draw_down_moment(key, part):
    key = jax.random.fold_in(key, 18)
    return moment_field(key, FF, D, 0)


def level_of(key, extent, cuts, low, largest):
    factor_of = 1.0
    for position, blocks in cuts:
        steps = jax.random.uniform(jax.random.fold_in(jax.random.fold_in(key, 6), position), (blocks,), jnp.float32, low / len(cuts), largest / len(cuts))
        factor_of = factor_of * jnp.repeat(jnp.exp(steps), extent[position] // blocks).reshape((-1,) + (1,) * (len(extent) - 1 - position))
    return factor_of


def scatter_about(stream_key, dims, scale, bound, cuts=(), kind=jnp.bfloat16):
    array = jax.random.normal(stream_key, dims, jnp.float32) * scale
    if len(cuts) > 0:
        array = level_of(stream_key, dims, cuts, -0.22, 0.18) * array
    return jnp.clip(array, min=-bound, max=bound).astype(kind)


def setup_inputs(seed: int = 0) -> dict:
    keys = jax.random.split(jax.random.key(seed), 21)
    return {
        "tokens": scatter_about(keys[0], (SLOTS_ALL, LEN, D), 1.0, 6.0, ((0, 16), (1, 8))),
        "cotangent": scatter_about(keys[1], (SLOTS_ALL, LEN, D), 1.0, 6.0, ((0, 16), (1, 8))),
        "lengths": draw_lengths(jax.random.fold_in(keys[20], 71), 0),
        "step_rate": jnp.clip(jnp.exp(jax.random.uniform(keys[3], (1,), jnp.float32, math.log(0.1), math.log(0.4))), 0.1, 0.4),
        "in_weight": scatter_about(keys[4], (D, 3 * D), D ** -0.5, 0.1875, ((0, 8),), jnp.float32),
        "out_weight": scatter_about(keys[5], (D, D), D ** -0.5, 0.1875, ((0, 8),), jnp.float32),
        "conv_weight": scatter_about(keys[6], (K, D), K ** -0.5, 3.5, ((1, 8),), jnp.float32),
        "gain_mixer": jnp.clip(1.0 + 0.1 * jax.random.normal(keys[7], (D,), jnp.float32), 0.5, 1.5),
        "gain_feed": jnp.clip(1.0 + 0.1 * jax.random.normal(keys[8], (D,), jnp.float32), 0.5, 1.5),
        "gate_weight": scatter_about(keys[9], (D, FF), D ** -0.5, 0.1875, ((0, 8),), jnp.float32),
        "up_weight": scatter_about(keys[10], (D, FF), D ** -0.5, 0.1875, ((0, 8),), jnp.float32),
        "down_weight": scatter_about(keys[11], (FF, D), (FF // 4) ** -0.5, 0.1875, ((0, 8),), jnp.float32),
        "in_moment": draw_in_moment(jax.random.fold_in(keys[20], 71), 0),
        "out_moment": draw_out_moment(jax.random.fold_in(keys[20], 71), 0),
        "conv_moment": draw_conv_moment(jax.random.fold_in(keys[20], 71), 0),
        "mixer_moment": draw_mixer_moment(jax.random.fold_in(keys[20], 71), 0),
        "feed_moment": draw_feed_moment(jax.random.fold_in(keys[20], 71), 0),
        "gate_moment": draw_gate_moment(jax.random.fold_in(keys[20], 71), 0),
        "up_moment": draw_up_moment(jax.random.fold_in(keys[20], 71), 0),
        "down_moment": draw_down_moment(jax.random.fold_in(keys[20], 71), 0),
    }


@jax.custom_vjp
def low(v):
    return lax.optimization_barrier(v.astype(jnp.bfloat16)).astype(jnp.float32)

@jax.custom_vjp
def low_back(v):
    return v

def low_keep(v):
    return (low(v), None)

def low_pass(kept, grad):
    return (grad,)

def back_keep(v):
    return (v, None)

def back_low(kept, grad):
    return (low(grad),)
low.defvjp(low_keep, low_pass)
low_back.defvjp(back_keep, back_low)

def matmul(left, right):
    return jnp.dot(left, right, precision=lax.Precision.HIGHEST, preferred_element_type=jnp.float32)

def root_scale(values, gain):
    return values * lax.rsqrt(lax.optimization_barrier(jnp.mean(values * values, axis=-1, keepdims=True)) + 1e-05) * gain

def block_forward(inputs, weights):
    in_weight, out_weight, conv_weight, gain_mixer, gain_feed, gate_weight, up_weight, down_weight = weights
    width = inputs.shape[-1]
    count = inputs.shape[0]
    normed_in = low(root_scale(inputs, low(gain_mixer)))
    projected = low_back(matmul(normed_in, low(in_weight)))
    b_block = projected[:, :width]
    c_block = projected[:, width:2 * width]
    x_block = projected[:, 2 * width:]
    product = low(b_block * x_block)
    kernel = low(conv_weight)
    taps = kernel.shape[0]
    padded = jnp.concatenate([jnp.zeros((taps - 1, width), jnp.float32), product], 0)
    conv_sum = jnp.zeros((count, width), jnp.float32)
    for j in range(taps):
        conv_sum = conv_sum + kernel[j] * padded[j:j + count]
    conv_sum = low_back(conv_sum)
    gated = low(c_block * conv_sum)
    middle = inputs + low_back(matmul(gated, low(out_weight)))
    normed_feed = low(root_scale(middle, low(gain_feed)))
    gate_pre = low_back(matmul(normed_feed, low(gate_weight)))
    up_pre = low_back(matmul(normed_feed, low(up_weight)))
    hidden = low(jax.nn.silu(gate_pre) * up_pre)
    return middle + low_back(matmul(hidden, low(down_weight)))

def reference(tokens, cotangent, lengths, step_rate, in_weight, out_weight, conv_weight, gain_mixer, gain_feed, gate_weight, up_weight, down_weight, in_moment, out_moment, conv_moment, mixer_moment, feed_moment, gate_moment, up_moment, down_moment):
    weights = (in_weight, out_weight, conv_weight, gain_mixer, gain_feed, gate_weight, up_weight, down_weight)
    moments = (in_moment, out_moment, conv_moment, mixer_moment, feed_moment, gate_moment, up_moment, down_moment)
    positions = jnp.arange(LEN, dtype=jnp.int32)

    def one_slot(totals, item):
        slot_tokens, slot_cotangent, slot_length = item
        valid = (positions < slot_length).astype(jnp.float32)[:, None]
        output, backward = jax.vjp(block_forward, slot_tokens.astype(jnp.float32), weights)
        grad_inputs, grad_weights = backward(slot_cotangent.astype(jnp.float32) * valid)
        totals = tuple((total + grad for total, grad in zip(totals, grad_weights)))
        return (totals, (output.astype(jnp.bfloat16), grad_inputs.astype(jnp.bfloat16)))
    zeros = tuple((jnp.zeros(weight.shape, jnp.float32) for weight in weights))
    sums, (block_out, grad_tokens) = lax.scan(one_slot, zeros, (tokens, cotangent, lengths))
    count = jnp.sum(lengths).astype(jnp.float32)
    updated = []
    momenta = []
    for weight, moment, total in zip(weights, moments, sums):
        grad_mean = total / count
        blend = 0.9 * moment + 0.1 * grad_mean
        scale = lax.rsqrt(jnp.mean(blend * blend) + 1e-06)
        updated.append(weight - step_rate[0] * (jnp.tanh(2.0 * blend * scale) + 0.1 * weight))
        momenta.append(0.5 * moment + 0.5 * grad_mean)
    return (block_out, grad_tokens, updated[0], updated[1], updated[2], updated[3], updated[4], updated[5], updated[6], updated[7], momenta[0], momenta[1], momenta[2], momenta[3], momenta[4], momenta[5], momenta[6], momenta[7])
```

```python
import functools

import jax
import jax.numpy as jnp
from jax import lax
from jax.experimental import pallas as pl
from jax.experimental.pallas import tpu as pltpu
from jax.sharding import Mesh
from jax.sharding import PartitionSpec as P

BF16 = jnp.bfloat16
F32 = jnp.float32
X = ("xh", "xl")
G = ("z", "xl")
DP = ("y", "xh", "core")
CHIPS = ("y", "xh")
VMEM = pl.BlockSpec(memory_space=pltpu.VMEM)
SMEM = pl.BlockSpec(memory_space=pltpu.SMEM)
ANY = pl.BlockSpec(memory_space=pl.ANY)
PARAMS = pltpu.CompilerParams(vmem_limit_bytes=48 * 1024 * 1024)
WIDE = pltpu.CompilerParams(vmem_limit_bytes=58 * 1024 * 1024)


def ring(value, axis, by):
    return lax.ppermute(value, axis, [(i, (i + by) % 4) for i in range(4)])


def swap(value):
    return lax.ppermute(value, "core", [(0, 1), (1, 0)])


def from_behind(value, by):
    pairs = [(i, i + by) for i in range(8) if 0 <= i + by < 8]
    return lax.ppermute(value, G, pairs)


def pick(value, index, axis):
    return lax.dynamic_index_in_dim(value, index, axis, keepdims=False)


def after(value, *others):
    return lax.optimization_barrier((value, *others))[0]


def share_kernel(widths, *refs):
    sources, target = refs[:-1], refs[-1]
    for core in range(2):

        @pl.when(lax.axis_index("core") == core)
        def _():
            at = 0
            for source, width in zip(sources, widths):
                for j in range(source.shape[1] // (2 * width)):
                    columns = source[:, (2 * j + core) * width : (2 * j + core + 1) * width]
                    target[:, at : at + width] = columns.astype(BF16)
                    at += width


def share(width, source):
    rows, columns = source.shape
    return pl.pallas_call(
        functools.partial(share_kernel, (width,)),
        out_shape=jax.ShapeDtypeStruct((rows, columns // 2), BF16),
        in_specs=[VMEM],
        out_specs=VMEM,
        compiler_params=PARAMS,
    )(source)


def mix_kernel(in_ref, out_ref, small_ref, target):
    for core in range(2):

        @pl.when(lax.axis_index("core") == core)
        def _():
            for j in range(24):
                columns = in_ref[:, (2 * j + core) * 64 : (2 * j + core + 1) * 64]
                target[:, j * 64 : (j + 1) * 64] = columns.astype(BF16)
            rows = out_ref[core * 64 : (core + 1) * 64, :].astype(BF16)
            target[:64, 1536:2048] = rows[:, :512]
            target[64:, 1536:2048] = rows[:, 512:]
            target[:, 2048:] = small_ref[...].astype(BF16)


def mix_share(in_weight, out_weight, small):
    return pl.pallas_call(
        mix_kernel,
        out_shape=jax.ShapeDtypeStruct((128, 2176), BF16),
        in_specs=[VMEM] * 3,
        out_specs=VMEM,
        compiler_params=PARAMS,
    )(in_weight, out_weight, small)


def place_kernel(n_in, n_out, moves, *refs):
    parts, wholes, sems = refs[:n_in], refs[n_in : n_in + n_out], refs[-1]
    z, x = lax.axis_index("z"), lax.axis_index("xl")
    copies = []
    for number, (part, source, whole, where) in enumerate(moves):
        target = wholes[whole].at[where(z, x)]
        copies.append(
            pltpu.make_async_copy(parts[part].at[source], target, sems.at[number])
        )
    for copy in copies:
        copy.start()
    for copy in copies:
        copy.wait()


def place(parts, shapes, moves):
    return pl.pallas_call(
        functools.partial(place_kernel, len(parts), len(shapes), moves),
        out_shape=[jax.ShapeDtypeStruct(shape, BF16) for shape in shapes],
        in_specs=[ANY] * len(parts),
        out_specs=[VMEM] * len(shapes),
        scratch_shapes=[pltpu.SemaphoreType.DMA((len(moves),))],
        compiler_params=PARAMS,
    )(*parts)


def block(dz, dx, *rest):
    def where(z, x):
        return (lax.rem(z + dz, 4), x if dx == 0 else 1 - x) + rest

    return where


def around(part, axis):
    return [ring(part, axis, by) for by in (1, -1, 2)]


def x_pairs(part, left, right, far):
    shape = (2,) + part.shape
    moves = [(i, (), i // 2, (lambda z, x, i=i: (i % 2,))) for i in range(4)]
    low, high = place((part, left, right, far), [shape, shape], moves)
    return ring(low, X, -1), ring(high, X, 1)


BLOCKS = (
    (0, (), 0, 0),
    (1, (), 3, 0),
    (2, (), 1, 0),
    (3, (), 2, 0),
    (4, (0,), 0, 1),
    (4, (1,), 3, 1),
    (5, (0,), 1, 1),
    (5, (1,), 2, 1),
)


def place_whole(pieces):
    rows, columns = pieces[0].shape
    moves = [(part, lead, 0, block(dz, dx)) for part, lead, dz, dx in BLOCKS]
    (whole,) = place(pieces, [(4, 2, rows, columns)], moves)
    return whole.reshape(8 * rows, columns)


def place_mix(pieces):
    moves = []
    ins, outs, smalls = pl.ds(0, 1536), pl.ds(1536, 512), pl.ds(2048, 128)
    top, bottom, full = pl.ds(0, 64), pl.ds(64, 64), pl.ds(0, 128)
    for part, lead, dz, dx in BLOCKS:
        moves.append((part, lead + (full, ins), 0, block(dz, dx)))
        moves.append((part, lead + (top, outs), 1, block(dz, dx, top, pl.ds(0, 512))))
        moves.append((part, lead + (bottom, outs), 1, block(dz, dx, top, pl.ds(512, 512))))
        moves.append((part, lead + (full, smalls), 2, block(dz, dx)))
    shapes = [(4, 2, 128, 1536), (4, 2, 64, 1024), (4, 2, 128, 128)]
    in_full, out_full, small = place(pieces, shapes, moves)
    return in_full.reshape(1024, 1536), out_full.reshape(512, 1024), small.reshape(8, 128, 128)


def place_quarters(pieces):
    _, _, rows, columns = pieces.shape
    moves = [(0, (y,), 0, (lambda z, x, y=y: (slice(None), pl.ds(y * rows, rows)))) for y in range(4)]
    (whole,) = place((pieces,), [(8, 4 * rows, columns)], moves)
    return whole.reshape(32 * rows, columns)


def add(first, *others):
    total = first.astype(F32)
    for other in others:
        total = total + other.astype(F32)
    return total.astype(BF16)


def turned(value):
    return lax.optimization_barrier(value.T)


def ring_first(blocks, axis):
    on, back, low, high, here = blocks
    half = low.shape[0]
    on = jnp.concatenate([add(on[:half], ring(low, axis, 1)), on[half:]], 0)
    back = jnp.concatenate([back[:half], add(back[half:], ring(high, axis, -1))], 0)
    return on, back, here


def ring_second(on, back, here, axis):
    return add(here, ring(on, axis, 1), ring(back, axis, -1))


def ring_scatter(blocks, axis):
    return ring_second(*ring_first(ring_blocks(blocks, axis), axis), axis)


def ring_blocks(blocks, axis):
    me = lax.axis_index(axis)
    on, back, far, here = [pick(blocks, (me + by) % 4, 0) for by in (1, 3, 2, 0)]
    half = far.shape[0] // 2
    return on, back, far[:half], far[half:], here


def x_scatter(low, high, here):
    half = here.shape[0] // 2
    low, high = ring(low, X, -1), ring(high, X, 1)
    return jnp.concatenate([add(here[:half], low), add(here[half:], high)], 0)


def pair_sum(part, axis, by):
    return add(part, lax.ppermute(part, axis, [(i, i ^ by) for i in range(lax.axis_size(axis))]))


def to_owners(blocks):
    return lax.all_to_all(blocks, ("z", "xl", "y"), 0, 0, tiled=True)


def owner_sum(pieces):
    return pair_sum(jnp.sum(pieces.astype(F32), axis=0).astype(BF16), "xh", 1)


def piece_sum(part, rows):
    pieces = lax.all_to_all(part.reshape(8, rows, -1), CHIPS, 0, 0, tiled=True)
    return jnp.sum(pieces.astype(F32), axis=0).astype(BF16)


def spread(part, axes, count):
    return lax.all_to_all(jnp.broadcast_to(part[None], (count,) + part.shape), axes, 0, 0, tiled=True)


def chip_sum(part):
    return pair_sum(pair_sum(pair_sum(part, "y", 1), "y", 2), "xh", 1)


def shifted(product, slot):
    main = product[slot * 128 : (slot + 1) * 128]
    rim = product[512 + 2 * slot : 514 + 2 * slot]
    row = lax.broadcasted_iota(jnp.int32, main.shape, 0)
    one = jnp.where(row == 0, rim[1:2], pltpu.roll(main, 1, 0))
    two = pltpu.roll(main, 2, 0)
    two = jnp.where(row == 0, rim[0:1], jnp.where(row == 1, rim[1:2], two))
    return main, one, two


def conv_kernel(chip, in_ref, gain, taps, out_ref, normed, projected, conv_sum, gated, partial):
    inputs = chip[...].astype(F32)
    normed[...] = (inputs * root(inputs) * gain[...]).astype(BF16)
    for j in range(3):
        columns = slice(j * 512, (j + 1) * 512)
        projected[:, columns] = dot(normed[...], in_ref[:, columns])
    product = (projected[:, :512] * projected[:, 1024:]).astype(BF16).astype(F32)
    for slot in range(4):
        rows = slice(slot * 128, (slot + 1) * 128)
        main, one, two = shifted(product, slot)
        conv = taps[0:1] * two + taps[1:2] * one + taps[2:3] * main
        conv_sum[rows, :] = conv
        gated[rows, :] = (projected[rows, 512:1024] * conv).astype(BF16)
    partial[...] = dot(gated[...], out_ref[...])


def conv_forward(*args):
    return pl.pallas_call(
        conv_kernel,
        out_shape=[
            jax.ShapeDtypeStruct((528, 1024), BF16),
            jax.ShapeDtypeStruct((528, 1536), F32),
            jax.ShapeDtypeStruct((512, 512), F32),
            jax.ShapeDtypeStruct((512, 512), BF16),
            jax.ShapeDtypeStruct((512, 1024), F32),
        ],
        in_specs=[VMEM] * 5,
        out_specs=[VMEM] * 5,
        compiler_params=PARAMS,
    )(*args)


def conv_back_kernel(
    grad_out, out_ref, projected, conv_sum, gated, normed, chip, in_ref, taps, sum_feed,
    partial, low, high, own, grad, block,
):
    gated_back = dot_t(grad_out[...], out_ref[...])
    grad_conv = (gated_back * projected[:512, 512:1024]).astype(BF16).astype(F32)
    grad[:512, 512:1024] = (gated_back * conv_sum[...]).astype(BF16)
    product = (projected[:, :512] * projected[:, 1024:]).astype(BF16).astype(F32)
    sums = [jnp.zeros((1, 512), F32)] * 3
    rim = []
    for slot in range(4):
        rows = slice(slot * 128, (slot + 1) * 128)
        back = grad_conv[rows]
        row = lax.broadcasted_iota(jnp.int32, back.shape, 0)
        one = jnp.where(row == 127, 0.0, pltpu.roll(back, 127, 0))
        two = jnp.where(row >= 126, 0.0, pltpu.roll(back, 126, 0))
        grad_product = taps[0:1] * two + taps[1:2] * one + taps[2:3] * back
        grad[rows, :512] = (grad_product * projected[rows, 1024:]).astype(BF16)
        grad[rows, 1024:] = (grad_product * projected[rows, :512]).astype(BF16)
        rim.append(taps[0:1] * back[0:1])
        rim.append(taps[0:1] * back[1:2] + taps[1:2] * back[0:1])
        main, behind, further = shifted(product, slot)
        for j, value in enumerate((further, behind, main)):
            sums[j] = sums[j] + jnp.sum(back * value, axis=0, keepdims=True)
    rim = jnp.concatenate(rim + [jnp.zeros((8, 512), F32)], 0)
    grad[512:, :512] = (rim * projected[512:, 1024:]).astype(BF16)
    grad[512:, 512:1024] = jnp.zeros((16, 512), BF16)
    grad[512:, 1024:] = (rim * projected[512:, :512]).astype(BF16)
    partial[...] = dot_t(grad[...], in_ref[...])
    inputs = chip[...].astype(F32)
    sum_mixer = jnp.sum(partial[...] * inputs * root(inputs), axis=0, keepdims=True)
    zeros = jnp.zeros((1, 64), F32)
    wide = [
        jnp.concatenate([part for g in range(8) for part in (total[:, g * 64 : (g + 1) * 64], zeros)], 1)
        for total in sums
    ]
    small = jnp.concatenate([sum_mixer, sum_feed[...], *wide, jnp.zeros((123, 1024), F32)], 0).T
    x = lax.axis_index("xl")
    for z in range(4):
        columns = slice(z * 256, (z + 1) * 256)
        block[:, :1536] = t_dot(normed[:, columns], grad[...]).astype(BF16)
        total = t_dot(gated[:, z * 128 : (z + 1) * 128], grad_out[...]).astype(BF16)
        for part in range(4):
            corner = total[(part // 2) * 64 : (part // 2 + 1) * 64, (part % 2) * 512 : (part % 2 + 1) * 512]
            block[part * 64 : (part + 1) * 64, 1536:2048] = corner
        block[:, 2048:] = small[columns].astype(BF16)
        cut(block, x, 128, z, low, high, own)


def conv_back(*args):
    return pl.pallas_call(
        conv_back_kernel,
        out_shape=[
            jax.ShapeDtypeStruct((528, 1024), F32),
            jax.ShapeDtypeStruct((256, 2176), BF16),
            jax.ShapeDtypeStruct((256, 2176), BF16),
            jax.ShapeDtypeStruct((512, 2176), BF16),
        ],
        in_specs=[VMEM] * 10,
        out_specs=[VMEM] * 4,
        scratch_shapes=[pltpu.VMEM((528, 1536), BF16), pltpu.VMEM((256, 2176), BF16)],
        compiler_params=WIDE,
    )(*args)


def cut(block, x, rows, z, low, high, own):
    far = low if z < 2 else high
    other = pl.multiple_of((1 - x) * rows, rows)
    mine = pl.multiple_of(x * rows, rows)
    far[(z % 2) * rows : (z % 2 + 1) * rows, :] = block[pl.ds(other, rows), :]
    own[z * rows : (z + 1) * rows, :] = block[pl.ds(mine, rows), :]


def feed_kernel(
    normed, turned_ref, branch, gate, up, down,
    partial_out, partial_in, on, back, low, high, here, up_low, up_high, up_own, down_low, down_high, down_own,
    hidden, grad_gate, grad_up, block, tall,
):
    step = pl.program_id(0)
    y, x = lax.axis_index("y"), lax.axis_index("xl")

    @pl.when(step == 0)
    def _():
        partial_out[...] = jnp.zeros_like(partial_out)
        partial_in[...] = jnp.zeros_like(partial_in)

    for part in range(2):
        rows = slice(part * 256, (part + 1) * 256)
        gate_pre = dot(normed[rows, :], gate[...])
        up_pre = dot(normed[rows, :], up[...])
        sigmoid = jax.nn.sigmoid(gate_pre)
        silu = gate_pre * sigmoid
        hidden[rows, :] = (silu * up_pre).astype(BF16)
        grad_hidden = dot_t(branch[rows, :], down[...])
        grad_up[rows, :] = (grad_hidden * silu).astype(BF16)
        slope = grad_hidden * up_pre * sigmoid * (1.0 + gate_pre * (1.0 - sigmoid))
        grad_gate[rows, :] = slope.astype(BF16)
        partial_out[rows, :] += dot(hidden[rows, :], down[...])
        partial_in[rows, :] += dot_t(grad_gate[rows, :], gate[...]) + dot_t(grad_up[rows, :], up[...])
    tall[...] = t_dot(hidden[...], branch[...]).astype(BF16)
    for part in range(2):
        mine = pl.multiple_of((2 * part + x) * 288, 32)
        other = pl.multiple_of((2 * part + 1 - x) * 288, 32)
        rows = slice(part * 288, (part + 1) * 288)
        down_own[rows, :] = tall[pl.ds(mine, 288), :]

        @pl.when(step == 0)
        def _():
            down_low[rows, :] = tall[pl.ds(other, 288), :]

        @pl.when(step == 1)
        def _():
            down_high[rows, :] = tall[pl.ds(other, 288), :]

    def quarter(by, source):
        at = pl.multiple_of(lax.rem(y + by, 4) * 32 + source * 128, 32)
        return block[pl.ds(at, 32), :]

    for z in range(4):
        rows = turned_ref[z * 256 : (z + 1) * 256, :]
        block[...] = dot(rows, grad_gate[...]).astype(BF16)
        for source in range(2):
            at = z * 64 + source * 32
            on[at : at + 32, :] = quarter(1, source)
            back[at : at + 32, :] = quarter(3, source)
            here[at : at + 32, :] = quarter(0, source)
            far = low if z < 2 else high
            far[at % 128 : at % 128 + 32, :] = quarter(2, source)
        block[...] = dot(rows, grad_up[...]).astype(BF16)
        cut(block, x, 128, z, up_low, up_high, up_own)


def feed_forward(normed, turned_ref, branch, gate, up, down):
    whole = lambda *shape: pl.BlockSpec(shape, lambda i: (0, 0))
    columns = lambda rows: pl.BlockSpec((rows, 1152), lambda i: (0, i))
    gate_rows, up_rows = (256, 256, 128, 128, 256), (256, 256, 512)
    outs = pl.pallas_call(
        feed_kernel,
        grid=(2,),
        out_shape=[
            jax.ShapeDtypeStruct((512, 1024), F32),
            jax.ShapeDtypeStruct((512, 1024), F32),
            *[jax.ShapeDtypeStruct((n, 2304), BF16) for n in gate_rows + up_rows],
            *[jax.ShapeDtypeStruct((n, 1024), BF16) for n in (576, 576, 1152)],
        ],
        in_specs=[
            whole(512, 1024),
            whole(1024, 512),
            whole(512, 1024),
            columns(1024),
            columns(1024),
            pl.BlockSpec((1152, 1024), lambda i: (i, 0)),
        ],
        out_specs=[
            whole(512, 1024),
            whole(512, 1024),
            *[columns(n) for n in gate_rows + up_rows],
            whole(576, 1024),
            whole(576, 1024),
            pl.BlockSpec((576, 1024), lambda i: (i, 0)),
        ],
        scratch_shapes=[
            pltpu.VMEM((512, 1152), BF16),
            pltpu.VMEM((512, 1152), BF16),
            pltpu.VMEM((512, 1152), BF16),
            pltpu.VMEM((256, 1152), BF16),
            pltpu.VMEM((1152, 1024), BF16),
        ],
        compiler_params=WIDE,
    )(normed, turned_ref, branch, gate, up, down)
    return outs[0], outs[1], outs[2:7], outs[7:10], outs[10:13]


def norm_back_kernel(middle, here, there, gain, branch, grad_total, grad_out, sum_gain):
    values, grad = middle[...], here[...] + there[...]
    back, total = root_back(values, gain[...], grad)
    total_grad = branch[...].astype(F32) + back
    grad_total[...] = total_grad
    grad_out[...] = total_grad.astype(BF16)
    sum_gain[...] = total[None]


def norm_back(*args):
    return pl.pallas_call(
        norm_back_kernel,
        out_shape=[
            jax.ShapeDtypeStruct((256, 1024), F32),
            jax.ShapeDtypeStruct((256, 1024), BF16),
            jax.ShapeDtypeStruct((1, 1024), F32),
        ],
        in_specs=[VMEM] * 5,
        out_specs=[VMEM] * 3,
        compiler_params=PARAMS,
    )(*args)


def moment_kernel(kind, ordered, inverse, m_ref, mine_ref, other_ref, new_ref, square_ref, grad):
    halves = mine_ref[...].astype(F32), other_ref[...].astype(F32)
    if not ordered:
        zero = lax.axis_index("core") == 0
        mine, other = halves
        halves = (jnp.where(zero, mine, other), jnp.where(zero, other, mine))
    for core in range(2):
        share = halves[core]
        if kind == "rows":
            grad[core * 288 : (core + 1) * 288, :] = share
        elif kind == "out":
            grad[core * 64 : (core + 1) * 64, :512] = share[:64]
            grad[core * 64 : (core + 1) * 64, 512:] = share[64:]
        else:
            for j in range(share.shape[1] // kind):
                grad[:, (2 * j + core) * kind : (2 * j + core + 1) * kind] = share[
                    :, j * kind : (j + 1) * kind
                ]
    mean = grad[...] * inverse[0]
    m = m_ref[...]
    new_ref[...] = 0.5 * m + 0.5 * mean
    blend = 0.9 * m + 0.1 * mean
    square = jnp.sum(blend * blend, axis=0, keepdims=True)
    total = square[:, :128]
    for j in range(1, square.shape[1] // 128):
        total = total + square[:, j * 128 : (j + 1) * 128]
    square_ref[...] = total


def new_moment(kind, ordered, inverse, moment, mine, other):
    rows, columns = moment.shape
    return pl.pallas_call(
        functools.partial(moment_kernel, kind, ordered),
        out_shape=[
            jax.ShapeDtypeStruct((rows, columns), F32),
            jax.ShapeDtypeStruct((1, 128), F32),
        ],
        in_specs=[SMEM, VMEM, VMEM, VMEM],
        out_specs=[VMEM, VMEM],
        scratch_shapes=[pltpu.VMEM((rows, columns), F32)],
        compiler_params=PARAMS,
    )(inverse, moment, mine, other)


def dot(left, right):
    return jnp.dot(left, right, preferred_element_type=F32)


def dot_t(left, right):
    return lax.dot_general(left, right, (((1,), (1,)), ((), ())), preferred_element_type=F32)


def t_dot(left, right):
    return lax.dot_general(left, right, (((0,), (0,)), ((), ())), preferred_element_type=F32)


def root(values):
    return lax.rsqrt(jnp.mean(values * values, axis=-1, keepdims=True) + 1e-05)


def root_back(values, gain, grad):
    r = root(values)
    inner = jnp.mean(grad * gain * values, axis=-1, keepdims=True)
    back = r * grad * gain - values * (r * r * r) * inner
    return back, jnp.sum(grad * values * r, axis=0)


def shards(
    tokens,
    cotangent,
    lengths,
    step_rate,
    in_weight,
    out_weight,
    conv_weight,
    gain_mixer,
    gain_feed,
    gate_weight,
    up_weight,
    down_weight,
    in_moment,
    out_moment,
    conv_moment,
    mixer_moment,
    feed_moment,
    gate_moment,
    up_moment,
    down_moment,
):
    core = lax.axis_index("core")
    group = lax.axis_index(G)
    rate = step_rate[0]
    slots, length, width = tokens.shape
    rows = slots * length
    half = width // 2

    taps = lax.dynamic_slice_in_dim(conv_weight, core * 64, 64, 1)
    taps = jnp.pad(taps, ((0, 0), (0, 64)))
    small = jnp.concatenate([gain_mixer[None], gain_feed[None], taps], 0).T
    small = jnp.pad(small, ((0, 0), (0, 123)))
    mix_part = mix_share(in_weight, out_weight, small)
    gate_part = share(288, gate_weight)
    up_part = share(288, up_weight)
    down_part = lax.dynamic_slice_in_dim(down_weight, core * 288, 288, 0).astype(BF16)

    own = tokens.reshape(rows, width)
    rim = from_behind(tokens[:, length - 2 :], 1).reshape(2 * slots, width)
    pad = jnp.zeros((8, width), BF16)
    chip = jnp.concatenate([own, swap(own), rim, swap(rim), pad], 0)
    positions = group * length + jnp.arange(length, dtype=jnp.int32)
    valid = (positions[None, :] < lengths[:, None]).reshape(rows, 1)
    branch_own = jnp.where(valid, cotangent.reshape(rows, width), 0).astype(BF16)
    branch = jnp.concatenate([branch_own, swap(branch_own)], 0)
    up_quarter = lax.dynamic_slice_in_dim(up_part, lax.axis_index("y") * 32, 32, 0)
    up_quarters = spread(up_quarter, G, 8).reshape(8, 32, 2304)
    mix_z = around(mix_part, "z")
    gate_part, up_quarters, chip, branch, *mix_z = lax.optimization_barrier(
        (gate_part, up_quarters, chip, branch, *mix_z)
    )
    total_length = after(jnp.sum(lengths).astype(F32), mix_z[0])
    counts = jnp.broadcast_to(total_length, (16, 128))
    count = jnp.sum(lax.all_to_all(counts, DP, 0, 0, tiled=True)[:, 0])
    inverse = jnp.reshape(1.0 / count, (1,))
    mix_x = x_pairs(mix_part, *mix_z)
    gate_z = around(gate_part, "z")
    up_pieces = lax.all_gather(up_quarters, "y", axis=0)
    down_part, *both_x = lax.optimization_barrier((down_part, *mix_x, *gate_z))
    mix_x, gate_z = both_x[:2], both_x[2:]
    gate_x = x_pairs(gate_part, *gate_z)
    down_z = around(down_part, "z")
    both_x = lax.optimization_barrier((*gate_x, *down_z, up_pieces))
    gate_x, down_z, up_pieces = both_x[:2], both_x[2:5], both_x[5]
    down_x = x_pairs(down_part, *down_z)
    up_full = place_quarters(up_pieces)
    in_full, out_full, small_full = place_mix((mix_part, *mix_z, *mix_x))
    gate_full = place_whole((gate_part, *gate_z, *gate_x))
    down_full = place_whole((down_part, *down_z, *down_x))

    gains = small_full[:, :, :2].reshape(width, 2).astype(F32)
    mixer_gain, feed_gain = gains[:, 0][None], gains[:, 1][None]
    kernel = small_full[:, :64, 2:5].reshape(half, 3).astype(F32).T

    normed_in, projected, conv_sum, gated, partial = conv_forward(
        chip, in_full, mixer_gain, kernel, out_full
    )
    inputs_own = own.astype(F32)
    middle = inputs_own + (partial[:rows] + swap(partial[rows:]))
    normed_own = (middle * root(middle) * feed_gain).astype(BF16)
    normed_feed = jnp.concatenate([normed_own, swap(normed_own)], 0)
    partial_out, partial_feed, gate_dots, up_dots, down_dots = feed_forward(
        normed_feed, turned(normed_feed), branch, gate_full, up_full, down_full
    )

    grad_total, grad_out_own, sum_feed = norm_back(
        middle, partial_feed[:rows], swap(partial_feed[rows:]), feed_gain, branch[:rows]
    )
    grad_out = jnp.concatenate([grad_out_own, swap(grad_out_own)], 0)
    partial_in, *mix_dots = conv_back(
        grad_out, out_full, projected, conv_sum, gated, normed_in, chip, in_full, kernel, sum_feed
    )
    output = middle + (partial_out[:rows] + swap(partial_out[rows:]))
    block_out = output.astype(BF16).reshape(slots, length, width)
    split = 2 * rows + 2 * slots
    here_in = jnp.concatenate([partial_in[:rows], partial_in[2 * rows : split]], 0)
    there_in = jnp.concatenate([partial_in[rows : 2 * rows], partial_in[split : split + 2 * slots]], 0)
    grad_normed = here_in + swap(there_in)
    inputs_rim = jnp.concatenate([inputs_own, rim.astype(F32)], 0)
    grad_inputs, _ = root_back(inputs_rim, mixer_gain, grad_normed)
    rim_inputs = from_behind(grad_inputs[rows:].reshape(slots, 2, width), -1)
    grad_tokens = (grad_total + grad_inputs[:rows]).reshape(slots, length, width)
    grad_tokens = grad_tokens + jnp.pad(rim_inputs, ((0, 0), (length - 2, 0), (0, 0)))
    grad_tokens = grad_tokens.astype(BF16)

    mine = lax.axis_index("xl")
    down_here = x_scatter(*down_dots)
    up_dots = [after(part, down_here) for part in up_dots]
    up_here = x_scatter(*up_dots)
    mix_here = x_scatter(*mix_dots)
    gate_here = ring_second(*ring_first(gate_dots, "y"), "y")
    down_mine = chip_sum(ring_scatter(down_here.reshape(4, 288, width), "z"))
    up_mine = chip_sum(ring_scatter(up_here.reshape(4, 128, 2304), "z"))
    mix_piece = piece_sum(ring_scatter(mix_here.reshape(4, 128, 2176), "z"), 16)
    mix_both = spread(mix_piece, DP, 16).reshape(8, 2, 16, 2176)
    mix_first = mix_both[:, 0].reshape(128, 2176)
    mix_second = mix_both[:, 1].reshape(128, 2176)

    gate_blocks = gate_here.reshape(4, 2, 32, 2304)
    gate_other = pick(gate_blocks, 1 - mine, 1)
    gate_here = x_scatter(
        gate_other[:2].reshape(64, 2304),
        gate_other[2:].reshape(64, 2304),
        pick(gate_blocks, mine, 1).reshape(128, 2304),
    )
    gate_quarter = pair_sum(ring_scatter(gate_here.reshape(4, 32, 2304), "z"), "xh", 1)
    gate_mine = spread(gate_quarter, "y", 4).reshape(128, 2304)
    down_other, up_other, gate_other = swap(down_mine), swap(up_mine), swap(gate_mine)

    down_new, down_square = new_moment("rows", False, inverse, down_moment, down_mine, down_other)
    gate_new, gate_square = new_moment(288, False, inverse, gate_moment, gate_mine, gate_other)
    up_new, up_square = new_moment(288, False, inverse, up_moment, up_mine, up_other)
    in_new, in_square = new_moment(
        64, True, inverse, in_moment, mix_first[:, :1536], mix_second[:, :1536]
    )
    out_new, out_square = new_moment(
        "out", True, inverse, out_moment, mix_first[:, 1536:2048], mix_second[:, 1536:2048]
    )
    small_first = mix_first[:, 2048:2056].astype(F32).T
    small_second = mix_second[:, 2048:2056].astype(F32).T
    small_sum = (small_first + small_second) * inverse
    conv_mean = jnp.concatenate([small_first[2:5, :64], small_second[2:5, :64]], 1) * inverse
    conv_new = 0.5 * conv_moment + 0.5 * conv_mean
    mixer_new = 0.5 * mixer_moment + 0.5 * small_sum[0]
    feed_new = 0.5 * feed_moment + 0.5 * small_sum[1]

    conv_blend = 0.9 * conv_moment + 0.1 * conv_mean
    mixer_blend = 0.9 * mixer_moment + 0.1 * small_sum[0]
    feed_blend = 0.9 * feed_moment + 0.1 * small_sum[1]
    own_squares = jnp.concatenate(
        [
            in_square,
            out_square,
            jnp.sum(conv_blend * conv_blend, axis=0, keepdims=True),
            (mixer_blend * mixer_blend)[None],
            (feed_blend * feed_blend)[None],
            gate_square,
            up_square,
            down_square,
        ]
    )
    squares = jnp.sum(spread(own_squares, G, 8), axis=(0, 2))
    params = (
        in_weight,
        out_weight,
        conv_weight,
        gain_mixer,
        gain_feed,
        gate_weight,
        up_weight,
        down_weight,
    )
    moments = (
        in_moment,
        out_moment,
        conv_moment,
        mixer_moment,
        feed_moment,
        gate_moment,
        up_moment,
        down_moment,
    )
    momenta = (in_new, out_new, conv_new, mixer_new, feed_new, gate_new, up_new, down_new)
    updated = []
    for param, moment, new, squared in zip(params, moments, momenta, squares):
        scale = lax.rsqrt(squared / (param.size * 8) + 1e-06)
        blend = 0.8 * moment + 0.2 * new
        updated.append(param - rate * (jnp.tanh(2.0 * blend * scale) + 0.1 * param))
    return (block_out, grad_tokens, *updated, *momenta)


def solution(mesh):
    fine = Mesh(mesh.devices.reshape(4, 2, 2, 4, 2), ("y", "xh", "core", "z", "xl"))
    rows = P(G, None)
    flat = P(G)
    taps = P(None, G)
    slots = P(DP, G, None)
    weights = (rows, rows, taps, flat, flat, rows, rows, rows)
    return jax.shard_map(
        shards,
        mesh=fine,
        in_specs=(slots, slots, P(DP), P(), *weights, *weights),
        out_specs=(slots, slots, *weights, *weights),
        check_vma=False,
    )
```

```python
import functools

import jax
import jax.numpy as jnp
from jax import lax
from jax.experimental import pallas as pl
from jax.experimental.pallas import tpu as pltpu
from jax.sharding import Mesh
from jax.sharding import PartitionSpec as P

BF16 = jnp.bfloat16
F32 = jnp.float32
X = ("xh", "xl")
G = ("z", "xl")
DP = ("y", "xh", "core")
CHIPS = ("y", "xh")
VMEM = pl.BlockSpec(memory_space=pltpu.VMEM)
SMEM = pl.BlockSpec(memory_space=pltpu.SMEM)
ANY = pl.BlockSpec(memory_space=pl.ANY)
PARAMS = pltpu.CompilerParams(vmem_limit_bytes=48 * 1024 * 1024)
WIDE = pltpu.CompilerParams(vmem_limit_bytes=58 * 1024 * 1024)


def ring(value, axis, by):
    return lax.ppermute(value, axis, [(i, (i + by) % 4) for i in range(4)])


def swap(value):
    return lax.ppermute(value, "core", [(0, 1), (1, 0)])


def across(value):
    at = lambda x, core: (x % 4 // 2) * 4 + core * 2 + x % 2
    pairs = [(at(x, core), at(x + 2 * core - 1, core)) for x in range(4) for core in range(2)]
    return lax.ppermute(value, ("xh", "core", "xl"), pairs)


def from_behind(value, by):
    pairs = [(i, i + by) for i in range(8) if 0 <= i + by < 8]
    return lax.ppermute(value, G, pairs)


def pick(value, index, axis):
    return lax.dynamic_index_in_dim(value, index, axis, keepdims=False)


def after(value, *others):
    return lax.optimization_barrier((value, *others))[0]


def share_kernel(widths, *refs):
    sources, target = refs[:-1], refs[-1]
    for core in range(2):

        @pl.when(lax.axis_index("core") == core)
        def _():
            at = 0
            for source, width in zip(sources, widths):
                for j in range(source.shape[1] // (2 * width)):
                    columns = source[:, (2 * j + core) * width : (2 * j + core + 1) * width]
                    target[:, at : at + width] = columns.astype(BF16)
                    at += width


def share(width, source):
    rows, columns = source.shape
    return pl.pallas_call(
        functools.partial(share_kernel, (width,)),
        out_shape=jax.ShapeDtypeStruct((rows, columns // 2), BF16),
        in_specs=[VMEM],
        out_specs=VMEM,
        compiler_params=PARAMS,
    )(source)


def mix_kernel(in_ref, out_ref, small_ref, target):
    for core in range(2):

        @pl.when(lax.axis_index("core") == core)
        def _():
            for j in range(24):
                columns = in_ref[:, (2 * j + core) * 64 : (2 * j + core + 1) * 64]
                target[:, j * 64 : (j + 1) * 64] = columns.astype(BF16)
            rows = out_ref[core * 64 : (core + 1) * 64, :].astype(BF16)
            target[:64, 1536:2048] = rows[:, :512]
            target[64:, 1536:2048] = rows[:, 512:]
            target[:, 2048:] = small_ref[...].astype(BF16)


def mix_share(in_weight, out_weight, small):
    return pl.pallas_call(
        mix_kernel,
        out_shape=jax.ShapeDtypeStruct((128, 2176), BF16),
        in_specs=[VMEM] * 3,
        out_specs=VMEM,
        compiler_params=PARAMS,
    )(in_weight, out_weight, small)


def place_kernel(n_in, n_out, moves, *refs):
    parts, wholes, sems = refs[:n_in], refs[n_in : n_in + n_out], refs[-1]
    z, x = lax.axis_index("z"), lax.axis_index("xl")
    copies = []
    for number, (part, source, whole, where) in enumerate(moves):
        target = wholes[whole].at[where(z, x)]
        copies.append(
            pltpu.make_async_copy(parts[part].at[source], target, sems.at[number])
        )
    for copy in copies:
        copy.start()
    for copy in copies:
        copy.wait()


def place(parts, shapes, moves):
    return pl.pallas_call(
        functools.partial(place_kernel, len(parts), len(shapes), moves),
        out_shape=[jax.ShapeDtypeStruct(shape, BF16) for shape in shapes],
        in_specs=[ANY] * len(parts),
        out_specs=[VMEM] * len(shapes),
        scratch_shapes=[pltpu.SemaphoreType.DMA((len(moves),))],
        compiler_params=PARAMS,
    )(*parts)


def block(dz, dx, *rest):
    def where(z, x):
        return (lax.rem(z + dz, 4), x if dx == 0 else 1 - x) + rest

    return where


def around(part, axis):
    return [ring(part, axis, by) for by in (1, -1, 2)]


def other_x(pieces):
    shape = (4,) + pieces[0].shape
    (stack,) = place(pieces, [shape], [(i, (), 0, (lambda z, x, i=i: (i,))) for i in range(4)])
    return across(stack)


BLOCKS = (
    (0, (), 0, 0),
    (1, (), 3, 0),
    (2, (), 1, 0),
    (3, (), 2, 0),
    (4, (0,), 0, 1),
    (4, (1,), 3, 1),
    (4, (2,), 1, 1),
    (4, (3,), 2, 1),
)


def place_whole(pieces):
    rows, columns = pieces[0].shape
    moves = [(part, lead, 0, block(dz, dx)) for part, lead, dz, dx in BLOCKS]
    (whole,) = place(pieces, [(4, 2, rows, columns)], moves)
    return whole.reshape(8 * rows, columns)


def place_pair(pair, left, right, low, high):
    rows, columns = low.shape
    here, there = pl.ds(0, rows), pl.ds(rows, rows)
    moves = [(part, (here,), 0, block(dz, 0)) for part, dz in ((0, 0), (1, 3), (2, 1))]
    moves += [(part, (there,), 0, block(dz, 1)) for part, dz in ((0, 0), (1, 3), (2, 1))]
    moves += [(3, (), 0, block(2, 0)), (4, (), 0, block(2, 1))]
    (whole,) = place((pair, left, right, low, high), [(4, 2, rows, columns)], moves)
    return whole.reshape(8 * rows, columns)


def place_mix(pieces):
    moves = []
    ins, outs, smalls = pl.ds(0, 1536), pl.ds(1536, 512), pl.ds(2048, 128)
    top, bottom, full = pl.ds(0, 64), pl.ds(64, 64), pl.ds(0, 128)
    for part, lead, dz, dx in BLOCKS:
        moves.append((part, lead + (full, ins), 0, block(dz, dx)))
        moves.append((part, lead + (top, outs), 1, block(dz, dx, top, pl.ds(0, 512))))
        moves.append((part, lead + (bottom, outs), 1, block(dz, dx, top, pl.ds(512, 512))))
        moves.append((part, lead + (full, smalls), 2, block(dz, dx)))
    shapes = [(4, 2, 128, 1536), (4, 2, 64, 1024), (4, 2, 128, 128)]
    in_full, out_full, small = place(pieces, shapes, moves)
    return in_full.reshape(1024, 1536), out_full.reshape(512, 1024), small.reshape(8, 128, 128)


def place_quarters(pieces):
    _, _, rows, columns = pieces.shape
    moves = [(0, (y,), 0, (lambda z, x, y=y: (slice(None), pl.ds(y * rows, rows)))) for y in range(4)]
    (whole,) = place((pieces,), [(8, 4 * rows, columns)], moves)
    return whole.reshape(32 * rows, columns)


def add(first, *others):
    total = first.astype(F32)
    for other in others:
        total = total + other.astype(F32)
    return total.astype(BF16)


def turned(value):
    return lax.optimization_barrier(value.T)


def ring_sum(blocks, axis, *pins):
    me = lax.axis_index(axis)
    here, on, back, far = [pick(blocks, (me + by) % 4, 0) for by in (0, 1, 3, 2)]
    arrived = (ring(on, axis, 1), ring(back, axis, -1), ring(far, axis, 2))
    return add(here, *[after(part, *pins) for part in arrived])


def one_way_sum(blocks):
    core, me = lax.axis_index("core"), lax.axis_index("z")
    pairs = [(z, (z + 1) % 4) for z in range(4)] + [(4 + z, 4 + (z + 3) % 4) for z in range(4)]
    step = 1 - 2 * core
    total = pick(blocks, (me + 4 - step) % 4, 0)
    for hop in (2, 3, 4):
        total = add(pick(blocks, (me + 8 - hop * step) % 4, 0), lax.ppermute(total, ("core", "z"), pairs))
    return total


def x_sum(away, here, *pins):
    return add(here, after(across(away), *pins))


def pair_sum(part, axis, by, *pins):
    pairs = [(i, i ^ by) for i in range(lax.axis_size(axis))]
    return add(part, after(lax.ppermute(part, axis, pairs), *pins))


def to_owners(blocks):
    return lax.all_to_all(blocks, ("z", "xl", "y"), 0, 0, tiled=True)


def owner_sum(pieces):
    return pair_sum(jnp.sum(pieces.astype(F32), axis=0).astype(BF16), "xh", 1)


def piece_sum(part, rows, *pins):
    pieces = after(lax.all_to_all(part.reshape(8, rows, -1), CHIPS, 0, 0, tiled=True), *pins)
    return jnp.sum(pieces.astype(F32), axis=0).astype(BF16)


def spread(part, axes, count):
    return lax.all_to_all(jnp.broadcast_to(part[None], (count,) + part.shape), axes, 0, 0, tiled=True)


def chip_sum(part):
    return pair_sum(pair_sum(pair_sum(part, "y", 1), "y", 2), "xh", 1)


def shifted(product, slot):
    main = product[slot * 128 : (slot + 1) * 128]
    rim = product[512 + 2 * slot : 514 + 2 * slot]
    row = lax.broadcasted_iota(jnp.int32, main.shape, 0)
    one = jnp.where(row == 0, rim[1:2], pltpu.roll(main, 1, 0))
    two = pltpu.roll(main, 2, 0)
    two = jnp.where(row == 0, rim[0:1], jnp.where(row == 1, rim[1:2], two))
    return main, one, two


def conv_kernel(chip, in_ref, gain, taps, out_ref, normed, projected, conv_sum, gated, partial):
    inputs = chip[...].astype(F32)
    normed[...] = (inputs * root(inputs) * gain[...]).astype(BF16)
    for j in range(3):
        columns = slice(j * 512, (j + 1) * 512)
        projected[:, columns] = dot(normed[...], in_ref[:, columns])
    product = (projected[:, :512] * projected[:, 1024:]).astype(BF16).astype(F32)
    for slot in range(4):
        rows = slice(slot * 128, (slot + 1) * 128)
        main, one, two = shifted(product, slot)
        conv = taps[0:1] * two + taps[1:2] * one + taps[2:3] * main
        conv_sum[rows, :] = conv
        gated[rows, :] = (projected[rows, 512:1024] * conv).astype(BF16)
    partial[...] = dot(gated[...], out_ref[...])


def conv_forward(*args):
    return pl.pallas_call(
        conv_kernel,
        out_shape=[
            jax.ShapeDtypeStruct((528, 1024), BF16),
            jax.ShapeDtypeStruct((528, 1536), F32),
            jax.ShapeDtypeStruct((512, 512), F32),
            jax.ShapeDtypeStruct((512, 512), BF16),
            jax.ShapeDtypeStruct((512, 1024), F32),
        ],
        in_specs=[VMEM] * 5,
        out_specs=[VMEM] * 5,
        compiler_params=PARAMS,
    )(*args)


def conv_back_kernel(
    grad_out, out_ref, projected, conv_sum, gated, normed, chip, in_ref, taps, sum_feed,
    partial, away, own, grad, block,
):
    gated_back = dot_t(grad_out[...], out_ref[...])
    grad_conv = (gated_back * projected[:512, 512:1024]).astype(BF16).astype(F32)
    grad[:512, 512:1024] = (gated_back * conv_sum[...]).astype(BF16)
    product = (projected[:, :512] * projected[:, 1024:]).astype(BF16).astype(F32)
    sums = [jnp.zeros((1, 512), F32)] * 3
    rim = []
    for slot in range(4):
        rows = slice(slot * 128, (slot + 1) * 128)
        back = grad_conv[rows]
        row = lax.broadcasted_iota(jnp.int32, back.shape, 0)
        one = jnp.where(row == 127, 0.0, pltpu.roll(back, 127, 0))
        two = jnp.where(row >= 126, 0.0, pltpu.roll(back, 126, 0))
        grad_product = taps[0:1] * two + taps[1:2] * one + taps[2:3] * back
        grad[rows, :512] = (grad_product * projected[rows, 1024:]).astype(BF16)
        grad[rows, 1024:] = (grad_product * projected[rows, :512]).astype(BF16)
        rim.append(taps[0:1] * back[0:1])
        rim.append(taps[0:1] * back[1:2] + taps[1:2] * back[0:1])
        main, behind, further = shifted(product, slot)
        for j, value in enumerate((further, behind, main)):
            sums[j] = sums[j] + jnp.sum(back * value, axis=0, keepdims=True)
    rim = jnp.concatenate(rim + [jnp.zeros((8, 512), F32)], 0)
    grad[512:, :512] = (rim * projected[512:, 1024:]).astype(BF16)
    grad[512:, 512:1024] = jnp.zeros((16, 512), BF16)
    grad[512:, 1024:] = (rim * projected[512:, :512]).astype(BF16)
    partial[...] = dot_t(grad[...], in_ref[...])
    inputs = chip[...].astype(F32)
    sum_mixer = jnp.sum(partial[...] * inputs * root(inputs), axis=0, keepdims=True)
    zeros = jnp.zeros((1, 64), F32)
    wide = [
        jnp.concatenate([part for g in range(8) for part in (total[:, g * 64 : (g + 1) * 64], zeros)], 1)
        for total in sums
    ]
    small = jnp.concatenate([sum_mixer, sum_feed[...], *wide, jnp.zeros((123, 1024), F32)], 0).T
    x = lax.axis_index("xl")
    for z in range(4):
        columns = slice(z * 256, (z + 1) * 256)
        block[:, :1536] = t_dot(normed[:, columns], grad[...]).astype(BF16)
        total = t_dot(gated[:, z * 128 : (z + 1) * 128], grad_out[...]).astype(BF16)
        for part in range(4):
            corner = total[(part // 2) * 64 : (part // 2 + 1) * 64, (part % 2) * 512 : (part % 2 + 1) * 512]
            block[part * 64 : (part + 1) * 64, 1536:2048] = corner
        block[:, 2048:] = small[columns].astype(BF16)
        cut(block, x, 128, z, away, own)


def conv_back(*args):
    return pl.pallas_call(
        conv_back_kernel,
        out_shape=[
            jax.ShapeDtypeStruct((528, 1024), F32),
            jax.ShapeDtypeStruct((512, 2176), BF16),
            jax.ShapeDtypeStruct((512, 2176), BF16),
        ],
        in_specs=[VMEM] * 10,
        out_specs=[VMEM] * 3,
        scratch_shapes=[pltpu.VMEM((528, 1536), BF16), pltpu.VMEM((256, 2176), BF16)],
        compiler_params=WIDE,
    )(*args)


def cut(block, x, rows, z, away, own):
    other = pl.multiple_of((1 - x) * rows, 32)
    mine = pl.multiple_of(x * rows, 32)
    away[z * rows : (z + 1) * rows, :] = block[pl.ds(other, rows), :]
    own[z * rows : (z + 1) * rows, :] = block[pl.ds(mine, rows), :]


def feed_kernel(
    normed, turned_ref, branch, gate, up, down,
    partial_out, partial_in, gate_rows, up_away, up_own, down_away, down_own,
    hidden, grad_gate, grad_up, block, tall,
):
    step = pl.program_id(0)
    x = lax.axis_index("xl")

    @pl.when(step == 0)
    def _():
        partial_out[...] = jnp.zeros_like(partial_out)
        partial_in[...] = jnp.zeros_like(partial_in)

    for part in range(2):
        rows = slice(part * 256, (part + 1) * 256)
        gate_pre = dot(normed[rows, :], gate[...])
        up_pre = dot(normed[rows, :], up[...])
        sigmoid = jax.nn.sigmoid(gate_pre)
        silu = gate_pre * sigmoid
        hidden[rows, :] = (silu * up_pre).astype(BF16)
        grad_hidden = dot_t(branch[rows, :], down[...])
        grad_up[rows, :] = (grad_hidden * silu).astype(BF16)
        slope = grad_hidden * up_pre * sigmoid * (1.0 + gate_pre * (1.0 - sigmoid))
        grad_gate[rows, :] = slope.astype(BF16)
        partial_out[rows, :] += dot(hidden[rows, :], down[...])
        partial_in[rows, :] += dot_t(grad_gate[rows, :], gate[...]) + dot_t(grad_up[rows, :], up[...])
    tall[...] = t_dot(hidden[...], branch[...]).astype(BF16)
    for part in range(2):
        cut(tall.at[part * 576 : (part + 1) * 576, :], x, 288, part, down_away, down_own)
    for z in range(4):
        rows = turned_ref[z * 256 : (z + 1) * 256, :]
        block[...] = dot(rows, grad_gate[...]).astype(BF16)
        for source in range(2):
            for y in range(4):
                at = z * 64 + source * 32
                gate_rows[y, at : at + 32, :] = block[source * 128 + y * 32 : source * 128 + (y + 1) * 32, :]
        block[...] = dot(rows, grad_up[...]).astype(BF16)
        cut(block, x, 128, z, up_away, up_own)


def feed_forward(normed, turned_ref, branch, gate, up, down):
    whole = lambda *shape: pl.BlockSpec(shape, lambda i: (0, 0))
    columns = lambda rows: pl.BlockSpec((rows, 1152), lambda i: (0, i))
    outs = pl.pallas_call(
        feed_kernel,
        grid=(2,),
        out_shape=[
            jax.ShapeDtypeStruct((512, 1024), F32),
            jax.ShapeDtypeStruct((512, 1024), F32),
            jax.ShapeDtypeStruct((4, 256, 2304), BF16),
            *[jax.ShapeDtypeStruct((512, 2304), BF16)] * 2,
            *[jax.ShapeDtypeStruct((1152, 1024), BF16)] * 2,
        ],
        in_specs=[
            whole(512, 1024),
            whole(1024, 512),
            whole(512, 1024),
            columns(1024),
            columns(1024),
            pl.BlockSpec((1152, 1024), lambda i: (i, 0)),
        ],
        out_specs=[
            whole(512, 1024),
            whole(512, 1024),
            pl.BlockSpec((4, 256, 1152), lambda i: (0, 0, i)),
            *[columns(512)] * 2,
            *[pl.BlockSpec((576, 1024), lambda i: (i, 0))] * 2,
        ],
        scratch_shapes=[
            pltpu.VMEM((512, 1152), BF16),
            pltpu.VMEM((512, 1152), BF16),
            pltpu.VMEM((512, 1152), BF16),
            pltpu.VMEM((256, 1152), BF16),
            pltpu.VMEM((1152, 1024), BF16),
        ],
        compiler_params=WIDE,
    )(normed, turned_ref, branch, gate, up, down)
    return outs[0], outs[1], outs[2], outs[3:5], outs[5:7]


def norm_back_kernel(middle, here, there, gain, branch, grad_total, grad_out, sum_gain):
    values, grad = middle[...], here[...] + there[...]
    back, total = root_back(values, gain[...], grad)
    total_grad = branch[...].astype(F32) + back
    grad_total[...] = total_grad
    grad_out[...] = total_grad.astype(BF16)
    sum_gain[...] = total[None]


def norm_back(*args):
    return pl.pallas_call(
        norm_back_kernel,
        out_shape=[
            jax.ShapeDtypeStruct((256, 1024), F32),
            jax.ShapeDtypeStruct((256, 1024), BF16),
            jax.ShapeDtypeStruct((1, 1024), F32),
        ],
        in_specs=[VMEM] * 5,
        out_specs=[VMEM] * 3,
        compiler_params=PARAMS,
    )(*args)


def moment_kernel(kind, ordered, inverse, m_ref, mine_ref, other_ref, new_ref, square_ref, grad):
    halves = mine_ref[...].astype(F32), other_ref[...].astype(F32)
    if not ordered:
        zero = lax.axis_index("core") == 0
        mine, other = halves
        halves = (jnp.where(zero, mine, other), jnp.where(zero, other, mine))
    for core in range(2):
        share = halves[core]
        if kind == "rows":
            grad[core * 288 : (core + 1) * 288, :] = share
        elif kind == "out":
            grad[core * 64 : (core + 1) * 64, :512] = share[:64]
            grad[core * 64 : (core + 1) * 64, 512:] = share[64:]
        else:
            for j in range(share.shape[1] // kind):
                grad[:, (2 * j + core) * kind : (2 * j + core + 1) * kind] = share[
                    :, j * kind : (j + 1) * kind
                ]
    mean = grad[...] * inverse[0]
    m = m_ref[...]
    new_ref[...] = 0.5 * m + 0.5 * mean
    blend = 0.9 * m + 0.1 * mean
    square = jnp.sum(blend * blend, axis=0, keepdims=True)
    total = square[:, :128]
    for j in range(1, square.shape[1] // 128):
        total = total + square[:, j * 128 : (j + 1) * 128]
    square_ref[...] = total


def new_moment(kind, ordered, inverse, moment, mine, other):
    rows, columns = moment.shape
    return pl.pallas_call(
        functools.partial(moment_kernel, kind, ordered),
        out_shape=[
            jax.ShapeDtypeStruct((rows, columns), F32),
            jax.ShapeDtypeStruct((1, 128), F32),
        ],
        in_specs=[SMEM, VMEM, VMEM, VMEM],
        out_specs=[VMEM, VMEM],
        scratch_shapes=[pltpu.VMEM((rows, columns), F32)],
        compiler_params=PARAMS,
    )(inverse, moment, mine, other)


def dot(left, right):
    return jnp.dot(left, right, preferred_element_type=F32)


def dot_t(left, right):
    return lax.dot_general(left, right, (((1,), (1,)), ((), ())), preferred_element_type=F32)


def t_dot(left, right):
    return lax.dot_general(left, right, (((0,), (0,)), ((), ())), preferred_element_type=F32)


def root(values):
    return lax.rsqrt(jnp.mean(values * values, axis=-1, keepdims=True) + 1e-05)


def root_back(values, gain, grad):
    r = root(values)
    inner = jnp.mean(grad * gain * values, axis=-1, keepdims=True)
    back = r * grad * gain - values * (r * r * r) * inner
    return back, jnp.sum(grad * values * r, axis=0)


def shards(
    tokens,
    cotangent,
    lengths,
    step_rate,
    in_weight,
    out_weight,
    conv_weight,
    gain_mixer,
    gain_feed,
    gate_weight,
    up_weight,
    down_weight,
    in_moment,
    out_moment,
    conv_moment,
    mixer_moment,
    feed_moment,
    gate_moment,
    up_moment,
    down_moment,
):
    core = lax.axis_index("core")
    group = lax.axis_index(G)
    rate = step_rate[0]
    slots, length, width = tokens.shape
    rows = slots * length
    half = width // 2

    taps = lax.dynamic_slice_in_dim(conv_weight, core * 64, 64, 1)
    taps = jnp.pad(taps, ((0, 0), (0, 64)))
    small = jnp.concatenate([gain_mixer[None], gain_feed[None], taps], 0).T
    small = jnp.pad(small, ((0, 0), (0, 123)))
    mix_part = mix_share(in_weight, out_weight, small)
    gate_part = share(288, gate_weight)
    up_part = share(288, up_weight)
    down_part = lax.dynamic_slice_in_dim(down_weight, core * 288, 288, 0).astype(BF16)

    up_quarter = lax.dynamic_slice_in_dim(up_part, lax.axis_index("y") * 32, 32, 0)
    up_quarters = spread(up_quarter, G, 8).reshape(8, 32, 2304)
    mix_z = around(mix_part, "z")
    own = tokens.reshape(rows, width)
    rim = from_behind(after(tokens[:, length - 2 :], mix_z[0]), 1).reshape(2 * slots, width)
    pad = jnp.zeros((8, width), BF16)
    chip = jnp.concatenate([own, swap(own), rim, swap(rim), pad], 0)
    positions = group * length + jnp.arange(length, dtype=jnp.int32)
    valid = (positions[None, :] < lengths[:, None]).reshape(rows, 1)
    branch_own = jnp.where(valid, cotangent.reshape(rows, width), 0).astype(BF16)
    branch = jnp.concatenate([branch_own, swap(branch_own)], 0)

    down_other = across(down_part)
    gate_part, up_quarters, chip, branch, down_other, *mix_z = lax.optimization_barrier(
        (gate_part, up_quarters, chip, branch, down_other, *mix_z)
    )
    total_length = after(jnp.sum(lengths).astype(F32), mix_z[0])
    counts = jnp.broadcast_to(total_length, (16, 128))
    count = jnp.sum(lax.all_to_all(counts, DP, 0, 0, tiled=True)[:, 0])
    inverse = jnp.reshape(1.0 / count, (1,))
    mix_x = other_x((mix_part, *mix_z))
    gate_z = around(gate_part, "z")
    up_pieces = lax.all_gather(up_quarters, "y", axis=0)
    down_pair = jnp.concatenate([down_part, down_other])
    down_pair, inverse, *both = lax.optimization_barrier((down_pair, inverse, mix_x, *gate_z))
    mix_x, gate_z = both[0], both[1:]
    gate_x = other_x((gate_part, *gate_z))
    down_z = ring(down_pair, "z", 1), ring(down_pair, "z", -1)
    in_full, out_full, small_full = place_mix((mix_part, *mix_z, mix_x))

    gains = small_full[:, :, :2].reshape(width, 2).astype(F32)
    mixer_gain, feed_gain = gains[:, 0][None], gains[:, 1][None]
    kernel = small_full[:, :64, 2:5].reshape(half, 3).astype(F32).T

    normed_in, projected, conv_sum, gated, partial = conv_forward(
        chip, in_full, mixer_gain, kernel, out_full
    )
    partial, gate_x, *down_z = lax.optimization_barrier((partial, gate_x, *down_z))
    down_far = ring(down_z[0][:288], "z", 1), ring(down_z[1][288:], "z", -1)
    up_full = place_quarters(up_pieces)
    gate_full = place_whole((gate_part, *gate_z, gate_x))
    down_full = place_pair(down_pair, *down_z, *down_far)
    inputs_own = own.astype(F32)
    middle = inputs_own + (partial[:rows] + swap(partial[rows:]))
    normed_own = (middle * root(middle) * feed_gain).astype(BF16)
    normed_feed = jnp.concatenate([normed_own, swap(normed_own)], 0)
    partial_out, partial_feed, gate_dots, up_dots, down_dots = feed_forward(
        normed_feed, turned(normed_feed), branch, gate_full, up_full, down_full
    )

    grad_total, grad_out_own, sum_feed = norm_back(
        middle, partial_feed[:rows], swap(partial_feed[rows:]), feed_gain, branch[:rows]
    )
    grad_out = jnp.concatenate([grad_out_own, swap(grad_out_own)], 0)
    partial_in, *mix_dots = conv_back(
        grad_out, out_full, projected, conv_sum, gated, normed_in, chip, in_full, kernel, sum_feed
    )
    output = middle + (partial_out[:rows] + swap(partial_out[rows:]))
    block_out = output.astype(BF16).reshape(slots, length, width)
    split = 2 * rows + 2 * slots
    here_in = jnp.concatenate([partial_in[:rows], partial_in[2 * rows : split]], 0)
    there_in = jnp.concatenate([partial_in[rows : 2 * rows], partial_in[split : split + 2 * slots]], 0)
    grad_normed = here_in + swap(there_in)
    inputs_rim = jnp.concatenate([inputs_own, rim.astype(F32)], 0)
    grad_inputs, _ = root_back(inputs_rim, mixer_gain, grad_normed)
    rim_inputs = from_behind(grad_inputs[rows:].reshape(slots, 2, width), -1)
    grad_tokens = (grad_total + grad_inputs[:rows]).reshape(slots, length, width)
    grad_tokens = grad_tokens + jnp.pad(rim_inputs, ((0, 0), (length - 2, 0), (0, 0)))
    grad_tokens = grad_tokens.astype(BF16)

    mine = lax.axis_index("xl")
    down_here = x_sum(*down_dots, mix_dots[0])
    up_here = x_sum(*up_dots, mix_dots[0])
    mix_here = x_sum(*mix_dots)
    down_mine = chip_sum(one_way_sum(down_here.reshape(4, 288, width)))
    up_mine = chip_sum(ring_sum(up_here.reshape(4, 128, 2304), "z"))
    gate_pieces = after(lax.all_to_all(gate_dots, "y", 0, 0, tiled=True), mix_dots[0])
    gate_here = jnp.sum(gate_pieces.astype(F32), axis=0).astype(BF16)
    mix_piece = piece_sum(ring_sum(mix_here.reshape(4, 128, 2176), "z"), 16)
    mix_both = spread(mix_piece, DP, 16).reshape(8, 2, 16, 2176)
    mix_first = mix_both[:, 0].reshape(128, 2176)
    mix_second = mix_both[:, 1].reshape(128, 2176)
    gate_blocks = gate_here.reshape(4, 2, 32, 2304)
    gate_here = x_sum(pick(gate_blocks, 1 - mine, 1), pick(gate_blocks, mine, 1))
    gate_quarter = pair_sum(ring_sum(gate_here, "z"), "xh", 1)
    gate_mine = spread(gate_quarter, "y", 4).reshape(128, 2304)
    gate_other, down_other, up_other = swap(gate_mine), swap(down_mine), swap(up_mine)

    down_new, down_square = new_moment("rows", False, inverse, down_moment, down_mine, down_other)
    gate_new, gate_square = new_moment(288, False, inverse, gate_moment, gate_mine, gate_other)
    up_new, up_square = new_moment(288, False, inverse, up_moment, up_mine, up_other)
    in_new, in_square = new_moment(
        64, True, inverse, in_moment, mix_first[:, :1536], mix_second[:, :1536]
    )
    out_new, out_square = new_moment(
        "out", True, inverse, out_moment, mix_first[:, 1536:2048], mix_second[:, 1536:2048]
    )
    small_first = mix_first[:, 2048:2056].astype(F32).T
    small_second = mix_second[:, 2048:2056].astype(F32).T
    small_sum = (small_first + small_second) * inverse
    conv_mean = jnp.concatenate([small_first[2:5, :64], small_second[2:5, :64]], 1) * inverse
    conv_new = 0.5 * conv_moment + 0.5 * conv_mean
    mixer_new = 0.5 * mixer_moment + 0.5 * small_sum[0]
    feed_new = 0.5 * feed_moment + 0.5 * small_sum[1]

    conv_blend = 0.9 * conv_moment + 0.1 * conv_mean
    mixer_blend = 0.9 * mixer_moment + 0.1 * small_sum[0]
    feed_blend = 0.9 * feed_moment + 0.1 * small_sum[1]
    own_squares = jnp.concatenate(
        [
            in_square,
            out_square,
            jnp.sum(conv_blend * conv_blend, axis=0, keepdims=True),
            (mixer_blend * mixer_blend)[None],
            (feed_blend * feed_blend)[None],
            up_square,
            jnp.zeros((2, 128), F32),
        ]
    )
    squares = jnp.sum(spread(own_squares, G, 8), axis=(0, 2))
    own_squares = jnp.concatenate([gate_square, down_square, jnp.zeros((6, 128), F32)])
    more = jnp.sum(spread(own_squares, G, 8), axis=(0, 2))
    squares = [squares[i] for i in range(5)] + [more[0], squares[5], more[1]]
    params = (
        in_weight,
        out_weight,
        conv_weight,
        gain_mixer,
        gain_feed,
        gate_weight,
        up_weight,
        down_weight,
    )
    moments = (
        in_moment,
        out_moment,
        conv_moment,
        mixer_moment,
        feed_moment,
        gate_moment,
        up_moment,
        down_moment,
    )
    momenta = (in_new, out_new, conv_new, mixer_new, feed_new, gate_new, up_new, down_new)
    updated = []
    for param, moment, new, squared in zip(params, moments, momenta, squares):
        scale = lax.rsqrt(squared / (param.size * 8) + 1e-06)
        blend = 0.8 * moment + 0.2 * new
        updated.append(param - rate * (jnp.tanh(2.0 * blend * scale) + 0.1 * param))
    return (block_out, grad_tokens, *updated, *momenta)


def solution(mesh):
    fine = Mesh(mesh.devices.reshape(4, 2, 2, 4, 2), ("y", "xh", "core", "z", "xl"))
    rows = P(G, None)
    flat = P(G)
    taps = P(None, G)
    slots = P(DP, G, None)
    weights = (rows, rows, taps, flat, flat, rows, rows, rows)
    return jax.shard_map(
        shards,
        mesh=fine,
        in_specs=(slots, slots, P(DP), P(), *weights, *weights),
        out_specs=(slots, slots, *weights, *weights),
        check_vma=False,
    )
```

```python
import functools

import jax
import jax.numpy as jnp
from jax import lax
from jax.experimental import pallas as pl
from jax.experimental.pallas import tpu as pltpu
from jax.sharding import Mesh
from jax.sharding import PartitionSpec as P

BF16 = jnp.bfloat16
F32 = jnp.float32
X = ("xh", "xl")
G = ("z", "xl")
DP = ("y", "xh", "core")
CHIPS = ("y", "xh")
VMEM = pl.BlockSpec(memory_space=pltpu.VMEM)
SMEM = pl.BlockSpec(memory_space=pltpu.SMEM)
ANY = pl.BlockSpec(memory_space=pl.ANY)
PARAMS = pltpu.CompilerParams(vmem_limit_bytes=48 * 1024 * 1024)
WIDE = pltpu.CompilerParams(vmem_limit_bytes=58 * 1024 * 1024)


def ring(value, axis, by):
    return lax.ppermute(value, axis, [(i, (i + by) % 4) for i in range(4)])


def swap(value):
    return lax.ppermute(value, "core", [(0, 1), (1, 0)])


def across(value):
    at = lambda x, core: (x % 4 // 2) * 4 + core * 2 + x % 2
    pairs = [(at(x, core), at(x + 2 * core - 1, core)) for x in range(4) for core in range(2)]
    return lax.ppermute(value, ("xh", "core", "xl"), pairs)


def from_behind(value, by):
    pairs = [(i, i + by) for i in range(8) if 0 <= i + by < 8]
    return lax.ppermute(value, G, pairs)


def pick(value, index, axis):
    return lax.dynamic_index_in_dim(value, index, axis, keepdims=False)


def after(value, *others):
    return lax.optimization_barrier((value, *others))[0]


def share_kernel(widths, *refs):
    sources, target = refs[:-1], refs[-1]
    for core in range(2):

        @pl.when(lax.axis_index("core") == core)
        def _():
            at = 0
            for source, width in zip(sources, widths):
                for j in range(source.shape[1] // (2 * width)):
                    columns = source[:, (2 * j + core) * width : (2 * j + core + 1) * width]
                    target[:, at : at + width] = columns.astype(target.dtype)
                    at += width


def share(width, source, kind=BF16):
    rows, columns = source.shape
    return pl.pallas_call(
        functools.partial(share_kernel, (width,)),
        out_shape=jax.ShapeDtypeStruct((rows, columns // 2), kind),
        in_specs=[VMEM],
        out_specs=VMEM,
        compiler_params=PARAMS,
    )(source)


def mix_kernel(in_ref, out_ref, small_ref, target):
    for core in range(2):

        @pl.when(lax.axis_index("core") == core)
        def _():
            for j in range(24):
                columns = in_ref[:, (2 * j + core) * 64 : (2 * j + core + 1) * 64]
                target[:, j * 64 : (j + 1) * 64] = columns.astype(BF16)
            rows = out_ref[core * 64 : (core + 1) * 64, :].astype(BF16)
            target[:64, 1536:2048] = rows[:, :512]
            target[64:, 1536:2048] = rows[:, 512:]
            target[:, 2048:] = small_ref[...].astype(BF16)


def mix_share(in_weight, out_weight, small):
    return pl.pallas_call(
        mix_kernel,
        out_shape=jax.ShapeDtypeStruct((128, 2176), BF16),
        in_specs=[VMEM] * 3,
        out_specs=VMEM,
        compiler_params=PARAMS,
    )(in_weight, out_weight, small)


def place_kernel(n_in, n_out, moves, *refs):
    parts, wholes, sems = refs[:n_in], refs[n_in : n_in + n_out], refs[-1]
    z, x = lax.axis_index("z"), lax.axis_index("xl")
    copies = []
    for number, (part, source, whole, where) in enumerate(moves):
        target = wholes[whole].at[where(z, x)]
        copies.append(
            pltpu.make_async_copy(parts[part].at[source], target, sems.at[number])
        )
    for copy in copies:
        copy.start()
    for copy in copies:
        copy.wait()


def place(parts, shapes, moves):
    return pl.pallas_call(
        functools.partial(place_kernel, len(parts), len(shapes), moves),
        out_shape=[jax.ShapeDtypeStruct(shape, BF16) for shape in shapes],
        in_specs=[ANY] * len(parts),
        out_specs=[VMEM] * len(shapes),
        scratch_shapes=[pltpu.SemaphoreType.DMA((len(moves),))],
        compiler_params=PARAMS,
    )(*parts)


def block(dz, dx, *rest):
    def where(z, x):
        return (lax.rem(z + dz, 4), x if dx == 0 else 1 - x) + rest

    return where


def around(part, axis):
    return [ring(part, axis, by) for by in (1, -1, 2)]


def other_x(pieces):
    shape = (4,) + pieces[0].shape
    (stack,) = place(pieces, [shape], [(i, (), 0, (lambda z, x, i=i: (i,))) for i in range(4)])
    return across(stack)


BLOCKS = (
    (0, (), 0, 0),
    (1, (), 3, 0),
    (2, (), 1, 0),
    (3, (), 2, 0),
    (4, (0,), 0, 1),
    (4, (1,), 3, 1),
    (4, (2,), 1, 1),
    (4, (3,), 2, 1),
)


def place_whole(pieces):
    rows, columns = pieces[0].shape
    moves = [(part, lead, 0, block(dz, dx)) for part, lead, dz, dx in BLOCKS]
    (whole,) = place(pieces, [(4, 2, rows, columns)], moves)
    return whole.reshape(8 * rows, columns)


def place_pair(pair, left, right, low, high):
    rows, columns = low.shape
    here, there = pl.ds(0, rows), pl.ds(rows, rows)
    moves = [(part, (here,), 0, block(dz, 0)) for part, dz in ((0, 0), (1, 3), (2, 1))]
    moves += [(part, (there,), 0, block(dz, 1)) for part, dz in ((0, 0), (1, 3), (2, 1))]
    moves += [(3, (), 0, block(2, 0)), (4, (), 0, block(2, 1))]
    (whole,) = place((pair, left, right, low, high), [(4, 2, rows, columns)], moves)
    return whole.reshape(8 * rows, columns)


def place_mix(pieces):
    moves = []
    ins, outs, smalls = pl.ds(0, 1536), pl.ds(1536, 512), pl.ds(2048, 128)
    top, bottom, full = pl.ds(0, 64), pl.ds(64, 64), pl.ds(0, 128)
    for part, lead, dz, dx in BLOCKS:
        moves.append((part, lead + (full, ins), 0, block(dz, dx)))
        moves.append((part, lead + (top, outs), 1, block(dz, dx, top, pl.ds(0, 512))))
        moves.append((part, lead + (bottom, outs), 1, block(dz, dx, top, pl.ds(512, 512))))
        moves.append((part, lead + (full, smalls), 2, block(dz, dx)))
    shapes = [(4, 2, 128, 1536), (4, 2, 64, 1024), (4, 2, 128, 128)]
    in_full, out_full, small = place(pieces, shapes, moves)
    return in_full.reshape(1024, 1536), out_full.reshape(512, 1024), small.reshape(8, 128, 128)


def place_quarters(pieces):
    _, rows, columns = pieces[0].shape

    def quarter(owners, by):
        def where(z, x):
            at = pl.multiple_of(lax.rem(lax.axis_index("y") + by, 4) * rows, rows)
            return owners, pl.ds(at, rows)

        return where

    every, low, high = pl.ds(0, 8), pl.ds(0, 4), pl.ds(4, 4)
    order = ((every, 0), (every, 3), (every, 1), (low, 2), (high, 2))
    moves = [(part, (), 0, quarter(*place)) for part, place in enumerate(order)]
    (whole,) = place(pieces, [(8, 4 * rows, columns)], moves)
    return whole.reshape(32 * rows, columns)


def add(first, *others):
    total = first.astype(F32)
    for other in others:
        total = total + other.astype(F32)
    return total.astype(BF16)


def turned(value):
    return lax.optimization_barrier(value.T)


def ring_sum(blocks, axis, *pins):
    me = lax.axis_index(axis)
    here, on, back, far = [pick(blocks, (me + by) % 4, 0) for by in (0, 1, 3, 2)]
    arrived = (ring(on, axis, 1), ring(back, axis, -1), ring(far, axis, 2))
    return add(here, *[after(part, *pins) for part in arrived])


def near_far_sum(blocks, axis, near_pin, far_pin):
    me = lax.axis_index(axis)
    here, on, back, far = [pick(blocks, (me + by) % 4, 0) for by in (0, 1, 3, 2)]
    near = here.astype(F32) + after(ring(on, axis, 1), near_pin).astype(F32)
    near = near + after(ring(back, axis, -1), near_pin).astype(F32)
    return (near + after(ring(far, axis, 2), far_pin).astype(F32)).astype(BF16)


def one_way_sum(blocks):
    core, me = lax.axis_index("core"), lax.axis_index("z")
    pairs = [(z, (z + 1) % 4) for z in range(4)] + [(4 + z, 4 + (z + 3) % 4) for z in range(4)]
    step = 1 - 2 * core
    total = pick(blocks, (me + 4 - step) % 4, 0)
    for hop in (2, 3, 4):
        total = add(pick(blocks, (me + 8 - hop * step) % 4, 0), lax.ppermute(total, ("core", "z"), pairs))
    return total


def x_sum(away, here, *pins):
    return add(here, after(across(away), *pins))


def pair_sum(part, axis, by, *pins):
    pairs = [(i, i ^ by) for i in range(lax.axis_size(axis))]
    return add(part, after(lax.ppermute(part, axis, pairs), *pins))


def to_owners(blocks):
    return lax.all_to_all(blocks, ("z", "xl", "y"), 0, 0, tiled=True)


def owner_sum(pieces):
    return pair_sum(jnp.sum(pieces.astype(F32), axis=0).astype(BF16), "xh", 1)


def piece_sum(part, count=8):
    pieces = lax.all_to_all(part, CHIPS, 0, 0, tiled=True)
    return jnp.sum(pieces.astype(F32), axis=0).astype(BF16)


def spread(part, axes, count):
    return lax.all_to_all(jnp.broadcast_to(part[None], (count,) + part.shape), axes, 0, 0, tiled=True)


def chip_sum(part):
    return pair_sum(pair_sum(pair_sum(part, "y", 1), "y", 2), "xh", 1)


def shifted(product, slot):
    main = product[slot * 128 : (slot + 1) * 128]
    rim = product[512 + 2 * slot : 514 + 2 * slot]
    row = lax.broadcasted_iota(jnp.int32, main.shape, 0)
    one = jnp.where(row == 0, rim[1:2], pltpu.roll(main, 1, 0))
    two = pltpu.roll(main, 2, 0)
    two = jnp.where(row == 0, rim[0:1], jnp.where(row == 1, rim[1:2], two))
    return main, one, two


def conv_kernel(
    chip, in_ref, gain, taps, out_ref, normed_turned, gated_turned, projected, conv_sum, partial, peer, normed, gated
):
    inputs = chip[...].astype(F32)
    normed[...] = (inputs * root(inputs) * gain[...]).astype(BF16)
    for j in range(3):
        columns = slice(j * 512, (j + 1) * 512)
        projected[:, columns] = dot(normed[...], in_ref[:, columns])
    product = (projected[:, :512] * projected[:, 1024:]).astype(BF16).astype(F32)
    for slot in range(4):
        rows = slice(slot * 128, (slot + 1) * 128)
        main, one, two = shifted(product, slot)
        conv = taps[0:1] * two + taps[1:2] * one + taps[2:3] * main
        conv_sum[rows, :] = conv
        gated[rows, :] = (projected[rows, 512:1024] * conv).astype(BF16)
    partial[...] = dot(gated[:256, :], out_ref[...])
    peer[...] = dot(gated[256:, :], out_ref[...])
    normed_turned[...] = normed[...].T
    gated_turned[...] = gated[...].T


def conv_forward(*args):
    return pl.pallas_call(
        conv_kernel,
        out_shape=[
            jax.ShapeDtypeStruct((1024, 528), BF16),
            jax.ShapeDtypeStruct((512, 512), BF16),
            jax.ShapeDtypeStruct((528, 1536), F32),
            jax.ShapeDtypeStruct((512, 512), F32),
            jax.ShapeDtypeStruct((256, 1024), F32),
            jax.ShapeDtypeStruct((256, 1024), F32),
        ],
        in_specs=[VMEM] * 5,
        out_specs=[VMEM] * 6,
        scratch_shapes=[pltpu.VMEM((528, 1024), BF16), pltpu.VMEM((512, 512), BF16)],
        compiler_params=PARAMS,
    )(*args)


def conv_back_kernel(
    grad_mine, grad_other, out_ref, projected, conv_sum, gated_turned, normed_turned, chip, in_ref, taps, sum_feed,
    partial, away, own, grad, block, grad_out,
):
    grad_out[:256, :] = grad_mine[...]
    grad_out[256:, :] = grad_other[...]
    gated_back = dot_t(grad_out[...], out_ref[...])
    grad_conv = (gated_back * projected[:512, 512:1024]).astype(BF16).astype(F32)
    grad[:512, 512:1024] = (gated_back * conv_sum[...]).astype(BF16)
    product = (projected[:, :512] * projected[:, 1024:]).astype(BF16).astype(F32)
    sums = [jnp.zeros((1, 512), F32)] * 3
    rim = []
    for slot in range(4):
        rows = slice(slot * 128, (slot + 1) * 128)
        back = grad_conv[rows]
        row = lax.broadcasted_iota(jnp.int32, back.shape, 0)
        one = jnp.where(row == 127, 0.0, pltpu.roll(back, 127, 0))
        two = jnp.where(row >= 126, 0.0, pltpu.roll(back, 126, 0))
        grad_product = taps[0:1] * two + taps[1:2] * one + taps[2:3] * back
        grad[rows, :512] = (grad_product * projected[rows, 1024:]).astype(BF16)
        grad[rows, 1024:] = (grad_product * projected[rows, :512]).astype(BF16)
        rim.append(taps[0:1] * back[0:1])
        rim.append(taps[0:1] * back[1:2] + taps[1:2] * back[0:1])
        main, behind, further = shifted(product, slot)
        for j, value in enumerate((further, behind, main)):
            sums[j] = sums[j] + jnp.sum(back * value, axis=0, keepdims=True)
    rim = jnp.concatenate(rim + [jnp.zeros((8, 512), F32)], 0)
    grad[512:, :512] = (rim * projected[512:, 1024:]).astype(BF16)
    grad[512:, 512:1024] = jnp.zeros((16, 512), BF16)
    grad[512:, 1024:] = (rim * projected[512:, :512]).astype(BF16)
    partial[...] = dot_t(grad[...], in_ref[...])
    inputs = chip[...].astype(F32)
    sum_mixer = jnp.sum(partial[...] * inputs * root(inputs), axis=0, keepdims=True)
    zeros = jnp.zeros((1, 64), F32)
    wide = [
        jnp.concatenate([part for g in range(8) for part in (total[:, g * 64 : (g + 1) * 64], zeros)], 1)
        for total in sums
    ]
    small = jnp.concatenate([sum_mixer, sum_feed[...], *wide, jnp.zeros((123, 1024), F32)], 0).T
    x = lax.axis_index("xl")
    for z in range(4):
        columns = slice(z * 256, (z + 1) * 256)
        block[:, :1536] = dot(normed_turned[columns, :], grad[...]).astype(BF16)
        total = dot(gated_turned[z * 128 : (z + 1) * 128, :], grad_out[...]).astype(BF16)
        for part in range(4):
            corner = total[(part // 2) * 64 : (part // 2 + 1) * 64, (part % 2) * 512 : (part % 2 + 1) * 512]
            block[part * 64 : (part + 1) * 64, 1536:2048] = corner
        block[:, 2048:] = small[columns].astype(BF16)
        cut(block, x, 128, z, away, own)


def conv_back(*args):
    return pl.pallas_call(
        conv_back_kernel,
        out_shape=[
            jax.ShapeDtypeStruct((528, 1024), F32),
            jax.ShapeDtypeStruct((512, 2176), BF16),
            jax.ShapeDtypeStruct((512, 2176), BF16),
        ],
        in_specs=[VMEM] * 11,
        out_specs=[VMEM] * 3,
        scratch_shapes=[
            pltpu.VMEM((528, 1536), BF16),
            pltpu.VMEM((256, 2176), BF16),
            pltpu.VMEM((512, 1024), BF16),
        ],
        compiler_params=WIDE,
    )(*args)


def cut(block, x, rows, z, away, own):
    other = pl.multiple_of((1 - x) * rows, 32)
    mine = pl.multiple_of(x * rows, 32)
    away[z * rows : (z + 1) * rows, :] = block[pl.ds(other, rows), :]
    own[z * rows : (z + 1) * rows, :] = block[pl.ds(mine, rows), :]


def feed_kernel(
    mine, other, branch, gate, up, down,
    out_mine, out_other, in_mine, in_other, gate_rows, up_away, up_own, down_away, down_own,
    normed, turned, gate_pre, up_pre, hidden, grad_gate, grad_up, block, tall,
):
    step = pl.program_id(0)
    x = lax.axis_index("xl")

    @pl.when(step == 0)
    def _():
        for ref in (out_mine, out_other, in_mine, in_other):
            ref[...] = jnp.zeros_like(ref)
        normed[:256, :] = mine[...]
        normed[256:, :] = other[...]
        turned[...] = normed[...].T

    gate_pre[...] = dot(normed[...], gate[...])
    up_pre[...] = dot(normed[...], up[...])
    grad_hid = dot_t(branch[...], down[...])
    for part in range(4):
        rows = slice(part * 128, (part + 1) * 128)
        grad_hidden = grad_hid[rows, :]
        sigmoid = jax.nn.sigmoid(gate_pre[rows, :])
        silu = gate_pre[rows, :] * sigmoid
        hidden[rows, :] = (silu * up_pre[rows, :]).astype(BF16)
        grad_up[rows, :] = (grad_hidden * silu).astype(BF16)
        slope = grad_hidden * up_pre[rows, :] * sigmoid * (1.0 + gate_pre[rows, :] * (1.0 - sigmoid))
        grad_gate[rows, :] = slope.astype(BF16)
    for rows, out_part, in_part in ((slice(0, 256), out_mine, in_mine), (slice(256, 512), out_other, in_other)):
        out_part[...] += dot(hidden[rows, :], down[...])
        in_part[...] += dot_t(grad_gate[rows, :], gate[...]) + dot_t(grad_up[rows, :], up[...])
    tall[...] = t_dot(hidden[...], branch[...]).astype(BF16)
    for part in range(2):
        for target, source in ((down_away, 2 * part + 1 - x), (down_own, 2 * part + x)):
            for i in range(18):
                at = pl.multiple_of(source * 288 + i * 16, 16)
                rows = tall[pl.ds(at, 16), :]
                for j in range(8):
                    target[part * 128 + j * 16 : part * 128 + (j + 1) * 16, i * 128 : (i + 1) * 128] = rows[
                        :, j * 128 : (j + 1) * 128
                    ]

    for z in range(4):
        rows = turned[z * 256 : (z + 1) * 256, :]
        block[...] = dot(rows, grad_gate[...]).astype(BF16)
        for source in range(2):
            for y in range(4):
                at = z * 64 + source * 32
                gate_rows[y, at : at + 32, :] = block[source * 128 + y * 32 : source * 128 + (y + 1) * 32, :]
        block[...] = dot(rows, grad_up[...]).astype(BF16)
        cut(block, x, 128, z, up_away, up_own)


def feed_forward(*args):
    whole = lambda *shape: pl.BlockSpec(shape, lambda i: (0, 0), pipeline_mode=pl.Buffered(1))
    total = lambda *shape: pl.BlockSpec(shape, lambda i: (0, 0))
    columns = lambda rows: pl.BlockSpec((rows, 1152), lambda i: (0, i))
    outs = pl.pallas_call(
        feed_kernel,
        grid=(2,),
        out_shape=[
            *[jax.ShapeDtypeStruct((256, 1024), F32)] * 4,
            jax.ShapeDtypeStruct((4, 256, 2304), BF16),
            *[jax.ShapeDtypeStruct((512, 2304), BF16)] * 4,
        ],
        in_specs=[
            whole(256, 1024),
            whole(256, 1024),
            whole(512, 1024),
            columns(1024),
            columns(1024),
            pl.BlockSpec((1152, 1024), lambda i: (i, 0)),
        ],
        out_specs=[
            *[total(256, 1024)] * 4,
            pl.BlockSpec((4, 256, 1152), lambda i: (0, 0, i)),
            *[columns(512)] * 2,
            *[pl.BlockSpec((256, 2304), lambda i: (i, 0))] * 2,
        ],
        scratch_shapes=[
            pltpu.VMEM((512, 1024), BF16),
            pltpu.VMEM((1024, 512), BF16),
            *[pltpu.VMEM((512, 1152), F32)] * 2,
            *[pltpu.VMEM((512, 1152), BF16)] * 3,
            pltpu.VMEM((256, 1152), BF16),
            pltpu.VMEM((1152, 1024), BF16),
        ],
        compiler_params=WIDE,
    )(*args)
    return outs[:4], outs[4], outs[5:7], outs[7:9]


def norm_back_kernel(middle, here, there, gain, branch, grad_total, grad_out, sum_gain):
    values, grad = middle[...], here[...] + there[...]
    back, total = root_back(values, gain[...], grad)
    total_grad = branch[...].astype(F32) + back
    grad_total[...] = total_grad
    grad_out[...] = total_grad.astype(BF16)
    sum_gain[...] = total[None]


def norm_back(*args):
    return pl.pallas_call(
        norm_back_kernel,
        out_shape=[
            jax.ShapeDtypeStruct((256, 1024), F32),
            jax.ShapeDtypeStruct((256, 1024), BF16),
            jax.ShapeDtypeStruct((1, 1024), F32),
        ],
        in_specs=[VMEM] * 5,
        out_specs=[VMEM] * 3,
        compiler_params=PARAMS,
    )(*args)


def square_kernel(inverse, feed, gate, mix, small, feed_moment, mix_moment, target):
    target[...] = jnp.zeros_like(target)

    def fold(row, grad, moment):
        blend = 0.9 * moment + 0.1 * (grad.astype(F32) * inverse[0])
        square = jnp.sum(blend * blend, axis=0, keepdims=True)
        total = square[:, :128]
        for j in range(1, square.shape[1] // 128):
            total = total + square[:, j * 128 : (j + 1) * 128]
        target[row : row + 1, :] = total

    fold(0, mix[:, :1536], mix_moment[:, :1536])
    fold(1, mix[:, 1536:2048], mix_moment[:, 1536:2048])
    fold(3, gate[...], feed_moment[32:, :])
    fold(4, feed[16:, :], feed_moment[16:32, :])
    fold(5, feed[:16, :], feed_moment[:16, :])
    mine, other = mix[:, 2048:].astype(F32), small[...].astype(F32)
    lane = lax.broadcasted_iota(jnp.int32, mine.shape, 1)
    blend = 0.9 * mix_moment[:, 2048:] + 0.1 * (jnp.where(lane < 2, mine + other, mine) * inverse[0])
    once = jnp.where(lane >= 2, 1.0, jnp.where(lax.axis_index("core") == 0, 1.0, 0.0))
    target[2:3, :] = jnp.sum(blend * blend * once, axis=0, keepdims=True)


def piece_squares(*args):
    return pl.pallas_call(
        square_kernel,
        out_shape=jax.ShapeDtypeStruct((8, 128), F32),
        in_specs=[SMEM] + [VMEM] * 6,
        out_specs=VMEM,
        compiler_params=PARAMS,
    )(*args)


def sum_all(value, *pins):
    value = value + swap(value)
    for axis in ("z", X, "y"):
        if axis == X:
            value = after(value, *pins)
        back, on, far = around(value, axis)
        value = (value + far) + (on + back)
    return value


def update_kernel(kind, ordered, row, scalars, totals, w_ref, m_ref, mine_ref, other_ref, w_new, m_new, grad):
    halves = mine_ref[...].astype(F32), other_ref[...].astype(F32)
    if not ordered:
        zero = lax.axis_index("core") == 0
        mine, other = halves
        halves = (jnp.where(zero, mine, other), jnp.where(zero, other, mine))
    for core in range(2):
        share = halves[core]
        if kind == "rows":
            for i in range(18):
                for j in range(8):
                    rows = slice(core * 288 + i * 16, core * 288 + (i + 1) * 16)
                    grad[rows, j * 128 : (j + 1) * 128] = share[
                        j * 16 : (j + 1) * 16, i * 128 : (i + 1) * 128
                    ]
        else:
            for j in range(share.shape[1] // kind):
                grad[:, (2 * j + core) * kind : (2 * j + core + 1) * kind] = share[
                    :, j * kind : (j + 1) * kind
                ]
    m, w = m_ref[...], w_ref[...]
    mean = grad[...] * scalars[0]
    blend = 0.9 * m + 0.1 * mean
    m_new[...] = 0.5 * m + 0.5 * mean
    square = jnp.sum(totals[row : row + 1, :], axis=1, keepdims=True)
    scale = lax.rsqrt(square / (w.size * 8) + 1e-06)
    w_new[...] = w - scalars[1] * (jnp.tanh(2.0 * blend * scale) + 0.1 * w)


def update(kind, ordered, row, scalars, totals, weight, moment, mine, other):
    shape = jax.ShapeDtypeStruct(weight.shape, F32)
    return pl.pallas_call(
        functools.partial(update_kernel, kind, ordered, row),
        out_shape=[shape, shape],
        in_specs=[SMEM] + [VMEM] * 5,
        out_specs=[VMEM, VMEM],
        scratch_shapes=[pltpu.VMEM(weight.shape, F32)],
        compiler_params=PARAMS,
    )(scalars, totals, weight, moment, mine, other)


def mix_update_kernel(
    scalars, totals, first, second, in_w, in_m, out_w, out_m, conv_w, conv_m, mixer_w, mixer_m, feed_w, feed_m,
    in_wn, in_mn, out_wn, out_mn, conv_wn, conv_mn, mixer_wn, mixer_mn, feed_wn, feed_mn, grad, wide,
):
    def step(grad, square, count, w_ref, m_ref, w_new, m_new):
        m, w = m_ref[...], w_ref[...]
        mean = grad * scalars[0]
        scale = lax.rsqrt(square / count + 1e-06)
        m_new[...] = 0.5 * m + 0.5 * mean
        move = jnp.tanh(2.0 * (0.9 * m + 0.1 * mean) * scale) + 0.1 * w
        w_new[...] = w - scalars[1] * move

    for core, half in enumerate((first, second)):
        for j in range(24):
            grad[:, (2 * j + core) * 64 : (2 * j + core + 1) * 64] = half[:, j * 64 : (j + 1) * 64].astype(F32)
        wide[core * 64 : (core + 1) * 64, :512] = half[:64, 1536:2048].astype(F32)
        wide[core * 64 : (core + 1) * 64, 512:] = half[64:, 1536:2048].astype(F32)
    total = lambda row: jnp.sum(totals[row : row + 1, :], axis=1, keepdims=True)
    step(grad[...], total(0), 1024 * 3072, in_w, in_m, in_wn, in_mn)
    step(wide[...], total(1), 1024 * 1024, out_w, out_m, out_wn, out_mn)
    one, two = first[:, 2048:].astype(F32).T, second[:, 2048:].astype(F32).T
    lane = lax.broadcasted_iota(jnp.int32, (1, 128), 1)
    among = lambda low, high: jnp.sum(
        jnp.where((lane >= low) & (lane < high), totals[2:3, :], 0.0), axis=1, keepdims=True
    )
    taps = jnp.where(lane < 64, one[2:5], pltpu.roll(two[2:5], 64, 1))
    step(taps, among(2, 5), 3 * 1024, conv_w, conv_m, conv_wn, conv_mn)
    step(one[0:1] + two[0:1], among(0, 1), 1024, mixer_w, mixer_m, mixer_wn, mixer_mn)
    step(one[1:2] + two[1:2], among(1, 2), 1024, feed_w, feed_m, feed_wn, feed_mn)


def mix_update(scalars, totals, first, second, *arrays):
    shapes = [jax.ShapeDtypeStruct(v.shape, F32) for v in arrays]
    return pl.pallas_call(
        mix_update_kernel,
        out_shape=shapes,
        in_specs=[SMEM] + [VMEM] * (3 + len(arrays)),
        out_specs=[VMEM] * len(arrays),
        scratch_shapes=[pltpu.VMEM((128, 3072), F32), pltpu.VMEM((128, 1024), F32)],
        compiler_params=PARAMS,
    )(scalars, totals, first, second, *arrays)


def dot(left, right):
    return jnp.dot(left, right, preferred_element_type=F32)


def dot_t(left, right):
    return lax.dot_general(left, right, (((1,), (1,)), ((), ())), preferred_element_type=F32)


def t_dot(left, right):
    return lax.dot_general(left, right, (((0,), (0,)), ((), ())), preferred_element_type=F32)


def root(values):
    return lax.rsqrt(jnp.mean(values * values, axis=-1, keepdims=True) + 1e-05)


def root_back(values, gain, grad):
    r = root(values)
    inner = jnp.mean(grad * gain * values, axis=-1, keepdims=True)
    back = r * grad * gain - values * (r * r * r) * inner
    return back, jnp.sum(grad * values * r, axis=0)


def shards(
    tokens,
    cotangent,
    lengths,
    step_rate,
    in_weight,
    out_weight,
    conv_weight,
    gain_mixer,
    gain_feed,
    gate_weight,
    up_weight,
    down_weight,
    in_moment,
    out_moment,
    conv_moment,
    mixer_moment,
    feed_moment,
    gate_moment,
    up_moment,
    down_moment,
):
    core = lax.axis_index("core")
    group = lax.axis_index(G)
    rate = step_rate[0]
    slots, length, width = tokens.shape
    rows = slots * length
    half = width // 2

    taps = lax.dynamic_slice_in_dim(conv_weight, core * 64, 64, 1)
    taps = jnp.pad(taps, ((0, 0), (0, 64)))
    small = jnp.concatenate([gain_mixer[None], gain_feed[None], taps], 0).T
    small = jnp.pad(small, ((0, 0), (0, 123)))
    mix_part = mix_share(in_weight, out_weight, small)
    gate_part = share(288, gate_weight)
    up_part = share(288, up_weight)
    down_part = lax.dynamic_slice_in_dim(down_weight, core * 288, 288, 0).astype(BF16)

    up_quarter = lax.dynamic_slice_in_dim(up_part, lax.axis_index("y") * 32, 32, 0)
    up_quarters = spread(up_quarter, G, 8).reshape(8, 32, 2304)
    piece = lax.axis_index(CHIPS)
    sixteen = lambda value: lax.dynamic_slice_in_dim(value, piece * 16, 16, 0)
    down_moments = lax.dynamic_slice(down_moment, (core * 288, piece * 128), (288, 128))
    down_moments = down_moments.reshape(18, 16, 128).transpose(1, 0, 2).reshape(16, 2304)
    feed_moments = jnp.concatenate(
        [down_moments, share(288, sixteen(up_moment), F32), share(288, sixteen(gate_moment), F32)], 0
    )
    out_moments = lax.dynamic_slice(
        out_moment, (core * 64 + piece % 4 * 16, piece // 4 * half), (16, half)
    )
    tap_moments = lax.dynamic_slice(conv_moment, (0, core * 64 + piece % 4 * 16), (3, 16))
    tap_moments = jnp.where(piece < 4, tap_moments, 0.0)
    small_moments = jnp.concatenate(
        [sixteen(mixer_moment)[None], sixteen(feed_moment)[None], tap_moments], 0
    ).T
    small_moments = jnp.pad(small_moments, ((0, 0), (0, 123)))
    mix_moments = jnp.concatenate(
        [share(64, sixteen(in_moment), F32), out_moments, small_moments], 1
    )
    mix_z = around(mix_part, "z")
    own = tokens.reshape(rows, width)
    rim = from_behind(after(tokens[:, length - 2 :], mix_z[0]), 1).reshape(2 * slots, width)
    pad = jnp.zeros((8, width), BF16)
    chip = jnp.concatenate([own, swap(own), rim, swap(rim), pad], 0)
    positions = group * length + jnp.arange(length, dtype=jnp.int32)
    valid = (positions[None, :] < lengths[:, None]).reshape(rows, 1)
    branch_own = jnp.where(valid, cotangent.reshape(rows, width), 0).astype(BF16)
    branch = jnp.concatenate([branch_own, swap(branch_own)], 0)

    down_other = across(down_part)
    gate_part, up_quarters, chip, branch, down_other, *mix_z = lax.optimization_barrier(
        (gate_part, up_quarters, chip, branch, down_other, *mix_z)
    )
    total_length = after(jnp.sum(lengths).astype(F32), mix_z[0])
    counts = jnp.broadcast_to(total_length, (16, 128))
    count = jnp.sum(lax.all_to_all(counts, DP, 0, 0, tiled=True)[:, 0])
    inverse = jnp.reshape(1.0 / count, (1,))
    mix_x = other_x((mix_part, *mix_z))
    gate_z = around(gate_part, "z")
    down_pair = jnp.concatenate([down_part, down_other])
    down_pair, inverse, up_quarters, *both = lax.optimization_barrier(
        (down_pair, inverse, up_quarters, mix_x, *gate_z)
    )
    mix_x, gate_z = both[0], both[1:]
    gate_x = other_x((gate_part, *gate_z))
    up_near = ring(up_quarters, "y", 1), ring(up_quarters, "y", -1)
    down_z = ring(down_pair, "z", 1), ring(down_pair, "z", -1)
    in_full, out_full, small_full = place_mix((mix_part, *mix_z, mix_x))

    gains = small_full[:, :, :2].reshape(width, 2).astype(F32)
    mixer_gain, feed_gain = gains[:, 0][None], gains[:, 1][None]
    kernel = small_full[:, :64, 2:5].reshape(half, 3).astype(F32).T

    normed_turned, gated_turned, projected, conv_sum, partial, peer = conv_forward(
        chip, in_full, mixer_gain, kernel, out_full
    )
    peer, feed_moments, mix_moments, gate_x, *both = lax.optimization_barrier(
        (peer, feed_moments, mix_moments, gate_x, *down_z, *up_near)
    )
    down_z, up_near = both[:2], both[2:]
    up_far = ring(up_near[0][:4], "y", 1), ring(up_near[1][4:], "y", -1)
    down_far = ring(down_z[0][:288], "z", 1), ring(down_z[1][288:], "z", -1)
    up_full = place_quarters((up_quarters, *up_near, *up_far))
    gate_full = place_whole((gate_part, *gate_z, gate_x))
    down_full = place_pair(down_pair, *down_z, *down_far)
    inputs_own = own.astype(F32)
    middle = inputs_own + (partial + swap(peer))
    normed_own = (middle * root(middle) * feed_gain).astype(BF16)
    partials, gate_dots, up_dots, down_dots = feed_forward(
        normed_own, swap(normed_own), branch, gate_full, up_full, down_full
    )

    grad_total, grad_out, sum_feed = norm_back(
        middle, partials[2], swap(partials[3]), feed_gain, branch[:rows]
    )
    partial_in, *mix_dots = conv_back(
        grad_out,
        swap(grad_out),
        out_full,
        projected,
        conv_sum,
        gated_turned,
        normed_turned,
        chip,
        in_full,
        kernel,
        sum_feed,
    )
    mine = lax.axis_index("xl")
    down_here = x_sum(*down_dots, mix_dots[0])
    up_here = x_sum(*up_dots, mix_dots[0])
    mix_here = x_sum(*mix_dots)
    down_part = ring_sum(down_here.reshape(4, 128, 2304), "z")
    up_part = ring_sum(up_here.reshape(4, 128, 2304), "z", mix_here)
    feed_part = jnp.concatenate([down_part.reshape(8, 16, 2304), up_part.reshape(8, 16, 2304)], 1)
    feed_pieces = lax.all_to_all(feed_part, CHIPS, 0, 0, tiled=True)
    feed_piece = jnp.sum(feed_pieces.astype(F32), axis=0).astype(BF16)
    mix_part = near_far_sum(mix_here.reshape(4, 128, 2176), "z", feed_part, feed_pieces)
    gate_pieces = after(lax.all_to_all(gate_dots, "y", 0, 0, tiled=True), mix_dots[0])
    gate_here = jnp.sum(gate_pieces.astype(F32), axis=0).astype(BF16)
    gate_blocks = gate_here.reshape(4, 2, 32, 2304)
    gate_here = x_sum(pick(gate_blocks, 1 - mine, 1), pick(gate_blocks, mine, 1))
    gate_halves = ring_sum(after(gate_here, mix_part), "z").reshape(2, 16, 2304)
    half_index = lax.axis_index("xh")
    gate_away = lax.ppermute(pick(gate_halves, 1 - half_index, 0), "xh", [(0, 1), (1, 0)])
    gate_piece = add(pick(gate_halves, half_index, 0), gate_away)
    mix_piece = piece_sum(after(mix_part, feed_pieces).reshape(8, 16, 2176))
    output = middle + (partials[0] + swap(after(partials[1], mix_part)))
    block_out = output.astype(BF16).reshape(slots, length, width)
    split = 2 * rows + 2 * slots
    here_in = jnp.concatenate([partial_in[:rows], partial_in[2 * rows : split]], 0)
    there_in = jnp.concatenate([partial_in[rows : 2 * rows], partial_in[split : split + 2 * slots]], 0)
    grad_normed = here_in + swap(after(there_in, mix_part))
    inputs_rim = jnp.concatenate([inputs_own, rim.astype(F32)], 0)
    grad_inputs, _ = root_back(inputs_rim, mixer_gain, grad_normed)
    rim_inputs = from_behind(grad_inputs[rows:].reshape(slots, 2, width), -1)
    grad_tokens = (grad_total + grad_inputs[:rows]).reshape(slots, length, width)
    grad_tokens = grad_tokens + jnp.pad(rim_inputs, ((0, 0), (length - 2, 0), (0, 0)))
    grad_tokens = grad_tokens.astype(BF16)

    feed_mine = spread(jnp.concatenate([feed_piece, gate_piece], 0), CHIPS, 8).reshape(8, 48, 2304)
    feed_other = swap(feed_mine)
    totals = sum_all(
        piece_squares(
            inverse,
            feed_piece,
            gate_piece,
            mix_piece,
            swap(mix_piece[:, 2048:]),
            feed_moments,
            mix_moments,
        ),
        feed_mine,
    )
    mix_both = spread(after(mix_piece, feed_mine), DP, 16).reshape(8, 2, 16, 2176)
    scalars = jnp.stack([inverse[0], rate])
    shares = [
        [v[:, at : at + 16].reshape(128, 2304) for v in (feed_mine, feed_other)] for at in (0, 16, 32)
    ]
    down_new = update("rows", False, 5, scalars, totals, down_weight, down_moment, *shares[0])
    up_new = update(288, False, 4, scalars, totals, up_weight, up_moment, *shares[1])
    gate_new = update(288, False, 3, scalars, totals, gate_weight, gate_moment, *shares[2])
    mix_both = after(mix_both, down_new[1], up_new[1], gate_new[1])
    mix_first = mix_both[:, 0].reshape(128, 2176)
    mix_second = mix_both[:, 1].reshape(128, 2176)
    news = mix_update(
        scalars,
        totals,
        mix_first,
        mix_second,
        in_weight,
        in_moment,
        out_weight,
        out_moment,
        conv_weight,
        conv_moment,
        gain_mixer[None],
        mixer_moment[None],
        gain_feed[None],
        feed_moment[None],
    )
    in_new, out_new, conv_new = news[0:2], news[2:4], news[4:6]
    mixer_new, feed_new = [v[0] for v in news[6:8]], [v[0] for v in news[8:10]]
    news = (in_new, out_new, conv_new, mixer_new, feed_new, gate_new, up_new, down_new)
    return (block_out, grad_tokens, *[new[0] for new in news], *[new[1] for new in news])


def solution(mesh):
    fine = Mesh(mesh.devices.reshape(4, 2, 2, 4, 2), ("y", "xh", "core", "z", "xl"))
    rows = P(G, None)
    flat = P(G)
    taps = P(None, G)
    slots = P(DP, G, None)
    weights = (rows, rows, taps, flat, flat, rows, rows, rows)
    return jax.shard_map(
        shards,
        mesh=fine,
        in_specs=(slots, slots, P(DP), P(), *weights, *weights),
        out_specs=(slots, slots, *weights, *weights),
        check_vma=False,
    )
```

```python
import functools

import jax
import jax.numpy as jnp
from jax import lax
from jax.experimental import pallas as pl
from jax.experimental.pallas import tpu as pltpu
from jax.sharding import Mesh
from jax.sharding import PartitionSpec as P

BF16 = jnp.bfloat16
F32 = jnp.float32
X = ("xh", "xl")
G = ("z", "xl")
DP = ("y", "xh", "core")
CHIPS = ("y", "xh")
VMEM = pl.BlockSpec(memory_space=pltpu.VMEM)
SMEM = pl.BlockSpec(memory_space=pltpu.SMEM)
ANY = pl.BlockSpec(memory_space=pl.ANY)
PARAMS = pltpu.CompilerParams(vmem_limit_bytes=48 * 1024 * 1024)
LIGHT = pltpu.CompilerParams(vmem_limit_bytes=20 * 1024 * 1024)
WIDE = pltpu.CompilerParams(vmem_limit_bytes=58 * 1024 * 1024)


def ring(value, axis, by):
    return lax.ppermute(value, axis, [(i, (i + by) % 4) for i in range(4)])


def swap(value):
    return lax.ppermute(value, "core", [(0, 1), (1, 0)])


def across(value):
    at = lambda x, core: (x % 4 // 2) * 4 + core * 2 + x % 2
    pairs = [(at(x, core), at(x + 2 * core - 1, core)) for x in range(4) for core in range(2)]
    return lax.ppermute(value, ("xh", "core", "xl"), pairs)


def from_behind(value, by):
    pairs = [(i, i + by) for i in range(8) if 0 <= i + by < 8]
    return lax.ppermute(value, G, pairs)


def pick(value, index, axis):
    return lax.dynamic_index_in_dim(value, index, axis, keepdims=False)


def after(value, *others):
    return lax.optimization_barrier((value, *others))[0]


def share_kernel(widths, *refs):
    sources, target = refs[:-1], refs[-1]
    for core in range(2):

        @pl.when(lax.axis_index("core") == core)
        def _():
            at = 0
            for source, width in zip(sources, widths):
                for j in range(source.shape[1] // (2 * width)):
                    columns = source[:, (2 * j + core) * width : (2 * j + core + 1) * width]
                    target[:, at : at + width] = columns.astype(target.dtype)
                    at += width


def share(width, source, kind=BF16):
    rows, columns = source.shape
    return pl.pallas_call(
        functools.partial(share_kernel, (width,)),
        out_shape=jax.ShapeDtypeStruct((rows, columns // 2), kind),
        in_specs=[VMEM],
        out_specs=VMEM,
        compiler_params=PARAMS,
    )(source)


def mix_kernel(in_ref, out_ref, small_ref, target):
    for core in range(2):

        @pl.when(lax.axis_index("core") == core)
        def _():
            for j in range(24):
                columns = in_ref[:, (2 * j + core) * 64 : (2 * j + core + 1) * 64]
                target[:, j * 64 : (j + 1) * 64] = columns.astype(BF16)
            rows = out_ref[core * 64 : (core + 1) * 64, :].astype(BF16)
            target[:64, 1536:2048] = rows[:, :512]
            target[64:, 1536:2048] = rows[:, 512:]
            target[:, 2048:] = small_ref[...].astype(BF16)


def mix_share(in_weight, out_weight, small):
    return pl.pallas_call(
        mix_kernel,
        out_shape=jax.ShapeDtypeStruct((128, 2176), BF16),
        in_specs=[VMEM] * 3,
        out_specs=VMEM,
        compiler_params=PARAMS,
    )(in_weight, out_weight, small)


def copies_of(parts, wholes, sems, moves):
    z, x = lax.axis_index("z"), lax.axis_index("xl")
    return [
        pltpu.make_async_copy(parts[part].at[source], wholes[whole].at[where(z, x)], sems.at[number])
        for number, (part, source, whole, where) in enumerate(moves)
    ]


def place_kernel(n_in, n_out, moves, *refs):
    parts, wholes, sems = refs[:n_in], refs[n_in : n_in + n_out], refs[-1]
    copies = copies_of(parts, wholes, sems, moves)
    for copy in copies:
        copy.start()
    for copy in copies:
        copy.wait()


def place(parts, shapes, moves):
    return pl.pallas_call(
        functools.partial(place_kernel, len(parts), len(shapes), moves),
        out_shape=[jax.ShapeDtypeStruct(shape, BF16) for shape in shapes],
        in_specs=[ANY] * len(parts),
        out_specs=[VMEM] * len(shapes),
        scratch_shapes=[pltpu.SemaphoreType.DMA((len(moves),))],
        compiler_params=PARAMS,
    )(*parts)


def block(dz, dx, *rest):
    def where(z, x):
        return (lax.rem(z + dz, 4), x if dx == 0 else 1 - x) + rest

    return where


def around(part, axis):
    return [ring(part, axis, by) for by in (1, -1, 2)]


def other_x(pieces):
    shape = (4,) + pieces[0].shape
    (stack,) = place(pieces, [shape], [(i, (), 0, (lambda z, x, i=i: (i,))) for i in range(4)])
    return across(stack)


BLOCKS = (
    (0, (), 0, 0),
    (1, (), 3, 0),
    (2, (), 1, 0),
    (3, (), 2, 0),
    (4, (0,), 0, 1),
    (4, (1,), 3, 1),
    (4, (2,), 1, 1),
    (4, (3,), 2, 1),
)


def place_whole(pieces):
    rows, columns = pieces[0].shape
    moves = [(part, lead, 0, block(dz, dx)) for part, lead, dz, dx in BLOCKS]
    return pieces, (4, 2, rows, columns), moves


def place_pair(pair, left, right, low, high):
    rows, columns = low.shape
    here, there = pl.ds(0, rows), pl.ds(rows, rows)
    moves = [(part, (here,), 0, block(dz, 0)) for part, dz in ((0, 0), (1, 3), (2, 1))]
    moves += [(part, (there,), 0, block(dz, 1)) for part, dz in ((0, 0), (1, 3), (2, 1))]
    moves += [(3, (), 0, block(2, 0)), (4, (), 0, block(2, 1))]
    return (pair, left, right, low, high), (4, 2, rows, columns), moves


def place_mix(pieces):
    moves = []
    ins, outs, smalls = pl.ds(0, 1536), pl.ds(1536, 512), pl.ds(2048, 128)
    top, bottom, full = pl.ds(0, 64), pl.ds(64, 64), pl.ds(0, 128)
    for part, lead, dz, dx in BLOCKS:
        moves.append((part, lead + (full, ins), 0, block(dz, dx)))
        moves.append((part, lead + (top, outs), 1, block(dz, dx, top, pl.ds(0, 512))))
        moves.append((part, lead + (bottom, outs), 1, block(dz, dx, top, pl.ds(512, 512))))
        moves.append((part, lead + (full, smalls), 2, block(dz, dx)))
    shapes = [(4, 2, 128, 1536), (4, 2, 64, 1024), (4, 2, 128, 128)]
    in_full, out_full, small = place(pieces, shapes, moves)
    return in_full.reshape(1024, 1536), out_full.reshape(512, 1024), small.reshape(8, 128, 128)


def place_quarters(pieces):
    _, rows, columns = pieces[0].shape

    def quarter(owners, by):
        def where(z, x):
            at = pl.multiple_of(lax.rem(lax.axis_index("y") + by, 4) * rows, rows)
            return owners, pl.ds(at, rows)

        return where

    every, low, high = pl.ds(0, 8), pl.ds(0, 4), pl.ds(4, 4)
    order = ((every, 0), (every, 3), (every, 1), (low, 2), (high, 2))
    moves = [(part, (), 0, quarter(*place)) for part, place in enumerate(order)]
    return pieces, (8, 4 * rows, columns), moves


def add(first, *others):
    total = first.astype(F32)
    for other in others:
        total = total + other.astype(F32)
    return total.astype(BF16)


def turned(value):
    return lax.optimization_barrier(value.T)


def ring_sum(blocks, axis, *pins):
    me = lax.axis_index(axis)
    here, on, back, far = [pick(blocks, (me + by) % 4, 0) for by in (0, 1, 3, 2)]
    arrived = (ring(on, axis, 1), ring(back, axis, -1), ring(far, axis, 2))
    return add(here, *[after(part, *pins) for part in arrived])


def ring_picks(blocks, axis):
    me = lax.axis_index(axis)
    return [pick(blocks, (me + by) % 4, 0) for by in (0, 1, 3, 2)]


def near_far_sum(picks, axis, near_pin, far_pin):
    here, on, back, far = picks
    near = here.astype(F32) + after(ring(on, axis, 1), near_pin).astype(F32)
    near = near + after(ring(back, axis, -1), near_pin).astype(F32)
    far = after(ring(far, axis, 2), far_pin).astype(F32)
    return lambda rows: (near[rows] + far[rows]).astype(BF16)


def x_sum(away, here, *pins):
    return add(here, after(across(away), *pins))


def pair_sum(part, axis, by, *pins):
    pairs = [(i, i ^ by) for i in range(lax.axis_size(axis))]
    return add(part, after(lax.ppermute(part, axis, pairs), *pins))


def to_owners(blocks):
    return lax.all_to_all(blocks, ("z", "xl", "y"), 0, 0, tiled=True)


def owner_sum(pieces):
    return pair_sum(jnp.sum(pieces.astype(F32), axis=0).astype(BF16), "xh", 1)


def piece_sum(part, *pins):
    pieces = after(lax.all_to_all(part, CHIPS, 0, 0, tiled=True), *pins)
    return jnp.sum(pieces.astype(F32), axis=0).astype(BF16)


def spread(part, axes, count):
    return lax.all_to_all(jnp.broadcast_to(part[None], (count,) + part.shape), axes, 0, 0, tiled=True)


def chip_sum(part):
    return pair_sum(pair_sum(pair_sum(part, "y", 1), "y", 2), "xh", 1)


def shifted(product, slot):
    main = product[slot * 128 : (slot + 1) * 128]
    rim = product[512 + 2 * slot : 514 + 2 * slot]
    row = lax.broadcasted_iota(jnp.int32, main.shape, 0)
    one = jnp.where(row == 0, rim[1:2], pltpu.roll(main, 1, 0))
    two = pltpu.roll(main, 2, 0)
    two = jnp.where(row == 0, rim[0:1], jnp.where(row == 1, rim[1:2], two))
    return main, one, two


def conv_kernel(
    chip, in_ref, gain, taps, out_ref, normed_turned, gated_turned, projected, conv_sum, partial, peer, normed, gated
):
    inputs = chip[...].astype(F32)
    normed[...] = (inputs * root(inputs) * gain[...]).astype(BF16)
    for j in range(3):
        columns = slice(j * 512, (j + 1) * 512)
        projected[:, columns] = dot(normed[...], in_ref[:, columns])
    product = (projected[:, :512] * projected[:, 1024:]).astype(BF16).astype(F32)
    for slot in range(4):
        rows = slice(slot * 128, (slot + 1) * 128)
        main, one, two = shifted(product, slot)
        conv = taps[0:1] * two + taps[1:2] * one + taps[2:3] * main
        conv_sum[rows, :] = conv
        gated[rows, :] = (projected[rows, 512:1024] * conv).astype(BF16)
    partial[...] = dot(gated[:256, :], out_ref[...])
    peer[...] = dot(gated[256:, :], out_ref[...])
    normed_turned[...] = normed[...].T
    gated_turned[...] = gated[...].T


def conv_forward(*args):
    return pl.pallas_call(
        conv_kernel,
        out_shape=[
            jax.ShapeDtypeStruct((1024, 528), BF16),
            jax.ShapeDtypeStruct((512, 512), BF16),
            jax.ShapeDtypeStruct((528, 1536), F32),
            jax.ShapeDtypeStruct((512, 512), F32),
            jax.ShapeDtypeStruct((256, 1024), F32),
            jax.ShapeDtypeStruct((256, 1024), F32),
        ],
        in_specs=[VMEM] * 5,
        out_specs=[VMEM] * 6,
        scratch_shapes=[pltpu.VMEM((528, 1024), BF16), pltpu.VMEM((512, 512), BF16)],
        compiler_params=PARAMS,
    )(*args)


def conv_back_kernel(
    grad_mine, grad_other, out_ref, projected, conv_sum, gated_turned, normed_turned, chip, in_ref, taps, sum_feed,
    partial, away, own, grad, block, grad_out,
):
    grad_out[:256, :] = grad_mine[...]
    grad_out[256:, :] = grad_other[...]
    gated_back = dot_t(grad_out[...], out_ref[...])
    grad_conv = (gated_back * projected[:512, 512:1024]).astype(BF16).astype(F32)
    grad[:512, 512:1024] = (gated_back * conv_sum[...]).astype(BF16)
    product = (projected[:, :512] * projected[:, 1024:]).astype(BF16).astype(F32)
    sums = [jnp.zeros((1, 512), F32)] * 3
    rim = []
    for slot in range(4):
        rows = slice(slot * 128, (slot + 1) * 128)
        back = grad_conv[rows]
        row = lax.broadcasted_iota(jnp.int32, back.shape, 0)
        one = jnp.where(row == 127, 0.0, pltpu.roll(back, 127, 0))
        two = jnp.where(row >= 126, 0.0, pltpu.roll(back, 126, 0))
        grad_product = taps[0:1] * two + taps[1:2] * one + taps[2:3] * back
        grad[rows, :512] = (grad_product * projected[rows, 1024:]).astype(BF16)
        grad[rows, 1024:] = (grad_product * projected[rows, :512]).astype(BF16)
        rim.append(taps[0:1] * back[0:1])
        rim.append(taps[0:1] * back[1:2] + taps[1:2] * back[0:1])
        main, behind, further = shifted(product, slot)
        for j, value in enumerate((further, behind, main)):
            sums[j] = sums[j] + jnp.sum(back * value, axis=0, keepdims=True)
    rim = jnp.concatenate(rim + [jnp.zeros((8, 512), F32)], 0)
    grad[512:, :512] = (rim * projected[512:, 1024:]).astype(BF16)
    grad[512:, 512:1024] = jnp.zeros((16, 512), BF16)
    grad[512:, 1024:] = (rim * projected[512:, :512]).astype(BF16)
    partial[...] = dot_t(grad[...], in_ref[...])
    inputs = chip[...].astype(F32)
    sum_mixer = jnp.sum(partial[...] * inputs * root(inputs), axis=0, keepdims=True)
    zeros = jnp.zeros((1, 64), F32)
    wide = [
        jnp.concatenate([part for g in range(8) for part in (total[:, g * 64 : (g + 1) * 64], zeros)], 1)
        for total in sums
    ]
    small = jnp.concatenate([sum_mixer, sum_feed[...], *wide, jnp.zeros((123, 1024), F32)], 0).T
    x = lax.axis_index("xl")
    for z in range(4):
        columns = slice(z * 256, (z + 1) * 256)
        block[:, :1536] = dot(normed_turned[columns, :], grad[...]).astype(BF16)
        total = dot(gated_turned[z * 128 : (z + 1) * 128, :], grad_out[...]).astype(BF16)
        for part in range(4):
            corner = total[(part // 2) * 64 : (part // 2 + 1) * 64, (part % 2) * 512 : (part % 2 + 1) * 512]
            block[part * 64 : (part + 1) * 64, 1536:2048] = corner
        block[:, 2048:] = small[columns].astype(BF16)
        cut(block, x, 128, z, away, own)


def conv_back(*args):
    return pl.pallas_call(
        conv_back_kernel,
        out_shape=[
            jax.ShapeDtypeStruct((528, 1024), F32),
            jax.ShapeDtypeStruct((512, 2176), BF16),
            jax.ShapeDtypeStruct((512, 2176), BF16),
        ],
        in_specs=[VMEM] * 11,
        out_specs=[VMEM] * 3,
        scratch_shapes=[
            pltpu.VMEM((528, 1536), BF16),
            pltpu.VMEM((256, 2176), BF16),
            pltpu.VMEM((512, 1024), BF16),
        ],
        compiler_params=WIDE,
    )(*args)


def cut(block, x, rows, z, away, own):
    other = pl.multiple_of((1 - x) * rows, 32)
    mine = pl.multiple_of(x * rows, 32)
    away[z * rows : (z + 1) * rows, :] = block[pl.ds(other, rows), :]
    own[z * rows : (z + 1) * rows, :] = block[pl.ds(mine, rows), :]


def feed_kernel(sets, mine, other, branch, *refs):
    n_in = sum(count for count, _ in sets)
    parts, refs = refs[:n_in], refs[n_in:]
    out_mine, out_other, in_mine, in_other, gate_rows, up_away, up_own, down_away, down_own = refs[:9]
    normed, turned, gate_pre, up_pre, hidden, grad_gate, grad_up, block, tall = refs[9:18]
    wholes, sems = refs[18:21], refs[21:24]
    step = pl.program_id(0)
    x = lax.axis_index("xl")
    copies, at = [], 0
    for (count, moves), whole, sem in zip(sets, wholes, sems):
        copies.append(copies_of(parts[at : at + count], (whole,), sem, moves))
        at += count

    def arrived(which):
        @pl.when(step == 0)
        def _():
            for copy in copies[which]:
                copy.wait()

    columns = pl.ds(pl.multiple_of(step * 1152, 128), 1152)

    @pl.when(step == 0)
    def _():
        for which in copies:
            for copy in which:
                copy.start()
        for ref in (out_mine, out_other, in_mine, in_other):
            ref[...] = jnp.zeros_like(ref)
        normed[:256, :] = mine[...]
        normed[256:, :] = other[...]
        turned[...] = normed[...].T

    arrived(0)
    gate = wholes[0][:, :, :, columns].reshape(1024, 1152)
    gate_pre[...] = dot(normed[...], gate)
    arrived(1)
    up = wholes[1][:, :, columns].reshape(1024, 1152)
    up_pre[...] = dot(normed[...], up)
    arrived(2)
    down = wholes[2][pl.ds(2 * step, 2)].reshape(1152, 1024)
    grad_hid = dot_t(branch[...], down)
    for part in range(4):
        rows = slice(part * 128, (part + 1) * 128)
        grad_hidden = grad_hid[rows, :]
        sigmoid = jax.nn.sigmoid(gate_pre[rows, :])
        silu = gate_pre[rows, :] * sigmoid
        hidden[rows, :] = (silu * up_pre[rows, :]).astype(BF16)
        grad_up[rows, :] = (grad_hidden * silu).astype(BF16)
        slope = grad_hidden * up_pre[rows, :] * sigmoid * (1.0 + gate_pre[rows, :] * (1.0 - sigmoid))
        grad_gate[rows, :] = slope.astype(BF16)
    for rows, out_part, in_part in ((slice(0, 256), out_mine, in_mine), (slice(256, 512), out_other, in_other)):
        out_part[...] += dot(hidden[rows, :], down)
        in_part[...] += dot_t(grad_gate[rows, :], gate) + dot_t(grad_up[rows, :], up)
    tall[...] = t_dot(hidden[...], branch[...]).astype(BF16)
    for part in range(2):
        for target, source in ((down_away, 2 * part + 1 - x), (down_own, 2 * part + x)):
            for i in range(18):
                at = pl.multiple_of(source * 288 + i * 16, 16)
                rows = tall[pl.ds(at, 16), :]
                for j in range(8):
                    target[part * 128 + j * 16 : part * 128 + (j + 1) * 16, i * 128 : (i + 1) * 128] = rows[
                        :, j * 128 : (j + 1) * 128
                    ]

    for z in range(4):
        rows = turned[z * 256 : (z + 1) * 256, :]
        block[...] = dot(rows, grad_gate[...]).astype(BF16)
        for source in range(2):
            for y in range(4):
                at = z * 64 + source * 32
                gate_rows[y, at : at + 32, :] = block[source * 128 + y * 32 : source * 128 + (y + 1) * 32, :]
        block[...] = dot(rows, grad_up[...]).astype(BF16)
        cut(block, x, 128, z, up_away, up_own)


def feed_forward(mine, other, branch, *weights):
    sets = [(len(pieces), moves) for pieces, _, moves in weights]
    parts = [piece for pieces, _, _ in weights for piece in pieces]
    whole = lambda *shape: pl.BlockSpec(shape, lambda i: (0, 0), pipeline_mode=pl.Buffered(1))
    total = lambda *shape: pl.BlockSpec(shape, lambda i: (0, 0))
    columns = lambda rows: pl.BlockSpec((rows, 1152), lambda i: (0, i))
    outs = pl.pallas_call(
        functools.partial(feed_kernel, sets),
        grid=(2,),
        out_shape=[
            *[jax.ShapeDtypeStruct((256, 1024), F32)] * 4,
            jax.ShapeDtypeStruct((4, 256, 2304), BF16),
            *[jax.ShapeDtypeStruct((512, 2304), BF16)] * 4,
        ],
        in_specs=[
            whole(256, 1024),
            whole(256, 1024),
            whole(512, 1024),
            *[ANY] * len(parts),
        ],
        out_specs=[
            *[total(256, 1024)] * 4,
            pl.BlockSpec((4, 256, 1152), lambda i: (0, 0, i)),
            *[columns(512)] * 2,
            *[pl.BlockSpec((256, 2304), lambda i: (i, 0))] * 2,
        ],
        scratch_shapes=[
            pltpu.VMEM((512, 1024), BF16),
            pltpu.VMEM((1024, 512), BF16),
            *[pltpu.VMEM((512, 1152), F32)] * 2,
            *[pltpu.VMEM((512, 1152), BF16)] * 3,
            pltpu.VMEM((256, 1152), BF16),
            pltpu.VMEM((1152, 1024), BF16),
            *[pltpu.VMEM(shape, BF16) for _, shape, _ in weights],
            *[pltpu.SemaphoreType.DMA((len(moves),)) for _, _, moves in weights],
        ],
        compiler_params=WIDE,
    )(mine, other, branch, *parts)
    return outs[:4], outs[4], outs[5:7], outs[7:9]


def norm_back_kernel(middle, here, there, gain, branch, grad_total, grad_out, sum_gain):
    values, grad = middle[...], here[...] + there[...]
    back, total = root_back(values, gain[...], grad)
    total_grad = branch[...].astype(F32) + back
    grad_total[...] = total_grad
    grad_out[...] = total_grad.astype(BF16)
    sum_gain[...] = total[None]


def norm_back(*args):
    return pl.pallas_call(
        norm_back_kernel,
        out_shape=[
            jax.ShapeDtypeStruct((256, 1024), F32),
            jax.ShapeDtypeStruct((256, 1024), BF16),
            jax.ShapeDtypeStruct((1, 1024), F32),
        ],
        in_specs=[VMEM] * 5,
        out_specs=[VMEM] * 3,
        compiler_params=PARAMS,
    )(*args)


def square_kernel(inverse, feed, gate, mix, small, feed_moment, mix_moment, target):
    target[...] = jnp.zeros_like(target)

    def fold(row, grad, moment):
        blend = 0.9 * moment + 0.1 * (grad.astype(F32) * inverse[0])
        square = jnp.sum(blend * blend, axis=0, keepdims=True)
        total = square[:, :128]
        for j in range(1, square.shape[1] // 128):
            total = total + square[:, j * 128 : (j + 1) * 128]
        target[row : row + 1, :] = total

    fold(0, mix[:, :1536], mix_moment[:, :1536])
    fold(1, mix[:, 1536:2048], mix_moment[:, 1536:2048])
    fold(3, gate[...], feed_moment[32:, :])
    fold(4, feed[16:, :], feed_moment[16:32, :])
    fold(5, feed[:16, :], feed_moment[:16, :])
    mine, other = mix[:, 2048:2176].astype(F32), small[...].astype(F32)
    lane = lax.broadcasted_iota(jnp.int32, mine.shape, 1)
    blend = 0.9 * mix_moment[:, 2048:] + 0.1 * (jnp.where(lane < 2, mine + other, mine) * inverse[0])
    once = jnp.where(lane >= 2, 1.0, jnp.where(lax.axis_index("core") == 0, 1.0, 0.0))
    target[2:3, :] = jnp.sum(blend * blend * once, axis=0, keepdims=True)


def piece_squares(*args):
    return pl.pallas_call(
        square_kernel,
        out_shape=jax.ShapeDtypeStruct((8, 128), F32),
        in_specs=[SMEM] + [VMEM] * 6,
        out_specs=VMEM,
        compiler_params=LIGHT,
    )(*args)


def sum_over(value, *axes):
    for axis in axes:
        back, on, far = around(value, axis)
        value = (value + far) + (on + back)
    return value


def returned(mine_ref, other_ref):
    mine = mine_ref[...].reshape(128, 2304).astype(F32)
    other = other_ref[...].reshape(128, 2304).astype(F32)
    zero = lax.axis_index("core") == 0
    return jnp.where(zero, mine, other), jnp.where(zero, other, mine)


def update_kernel(kind, row, scalars, totals, w_ref, m_ref, mine_ref, other_ref, w_new, m_new, grad):
    for core, share in enumerate(returned(mine_ref, other_ref)):
        if kind == "rows":
            for i in range(18):
                for j in range(8):
                    rows = slice(core * 288 + i * 16, core * 288 + (i + 1) * 16)
                    grad[rows, j * 128 : (j + 1) * 128] = share[
                        j * 16 : (j + 1) * 16, i * 128 : (i + 1) * 128
                    ]
        else:
            for j in range(share.shape[1] // kind):
                grad[:, (2 * j + core) * kind : (2 * j + core + 1) * kind] = share[
                    :, j * kind : (j + 1) * kind
                ]
    m, w = m_ref[...], w_ref[...]
    mean = grad[...] * scalars[0]
    blend = 0.9 * m + 0.1 * mean
    m_new[...] = 0.5 * m + 0.5 * mean
    square = jnp.sum(totals[row : row + 1, :], axis=1, keepdims=True)
    scale = lax.rsqrt(square / (w.size * 8) + 1e-06)
    w_new[...] = w - scalars[1] * (jnp.tanh(2.0 * blend * scale) + 0.1 * w)


def whole_block(value):
    return pl.BlockSpec(value.shape, lambda i: (0, 0))


def part_block(part):
    return pl.BlockSpec((8, 16, 2304), lambda i: (0, part, 0))


def update(kind, row, part, scalars, totals, weight, moment, mine, other):
    matrix = whole_block(weight)
    return pl.pallas_call(
        functools.partial(update_kernel, kind, row),
        grid=(1,),
        out_shape=[jax.ShapeDtypeStruct(weight.shape, F32)] * 2,
        in_specs=[SMEM, whole_block(totals), matrix, matrix, part_block(part), part_block(part)],
        out_specs=[matrix, matrix],
        scratch_shapes=[pltpu.VMEM(weight.shape, F32)],
        compiler_params=LIGHT,
    )(scalars, totals, weight, moment, mine, other)


def mix_update_kernel(
    scalars, totals, mine, other, in_w, in_m, out_w, out_m, conv_w, conv_m, mixer_w, mixer_m, feed_w, feed_m,
    in_wn, in_mn, out_wn, out_mn, conv_wn, conv_mn, mixer_wn, mixer_mn, feed_wn, feed_mn, grad, wide,
):
    def step(grad, square, count, w_ref, m_ref, w_new, m_new):
        m, w = m_ref[...], w_ref[...]
        mean = grad * scalars[0]
        scale = lax.rsqrt(square / count + 1e-06)
        m_new[...] = 0.5 * m + 0.5 * mean
        move = jnp.tanh(2.0 * (0.9 * m + 0.1 * mean) * scale) + 0.1 * w
        w_new[...] = w - scalars[1] * move

    first, second = returned(mine, other)
    for core, half in enumerate((first, second)):
        for j in range(24):
            grad[:, (2 * j + core) * 64 : (2 * j + core + 1) * 64] = half[:, j * 64 : (j + 1) * 64]
        wide[core * 64 : (core + 1) * 64, :512] = half[:64, 1536:2048]
        wide[core * 64 : (core + 1) * 64, 512:] = half[64:, 1536:2048]
    total = lambda row: jnp.sum(totals[row : row + 1, :], axis=1, keepdims=True)
    step(grad[...], total(0), 1024 * 3072, in_w, in_m, in_wn, in_mn)
    step(wide[...], total(1), 1024 * 1024, out_w, out_m, out_wn, out_mn)
    one, two = first[:, 2048:2176].T, second[:, 2048:2176].T
    lane = lax.broadcasted_iota(jnp.int32, (1, 128), 1)
    among = lambda low, high: jnp.sum(
        jnp.where((lane >= low) & (lane < high), totals[2:3, :], 0.0), axis=1, keepdims=True
    )
    taps = jnp.where(lane < 64, one[2:5], pltpu.roll(two[2:5], 64, 1))
    step(taps, among(2, 5), 3 * 1024, conv_w, conv_m, conv_wn, conv_mn)
    step(one[0:1] + two[0:1], among(0, 1), 1024, mixer_w, mixer_m, mixer_wn, mixer_mn)
    step(one[1:2] + two[1:2], among(1, 2), 1024, feed_w, feed_m, feed_wn, feed_mn)


def mix_update(scalars, totals, first, second, *arrays):
    shapes = [jax.ShapeDtypeStruct(v.shape, F32) for v in arrays]
    return pl.pallas_call(
        mix_update_kernel,
        out_shape=shapes,
        grid=(1,),
        in_specs=[SMEM, whole_block(totals), part_block(3), part_block(3)] + [whole_block(v) for v in arrays],
        out_specs=[whole_block(v) for v in arrays],
        scratch_shapes=[pltpu.VMEM((128, 3072), F32), pltpu.VMEM((128, 1024), F32)],
        compiler_params=LIGHT,
    )(scalars, totals, first, second, *arrays)


def dot(left, right):
    return jnp.dot(left, right, preferred_element_type=F32)


def dot_t(left, right):
    return lax.dot_general(left, right, (((1,), (1,)), ((), ())), preferred_element_type=F32)


def t_dot(left, right):
    return lax.dot_general(left, right, (((0,), (0,)), ((), ())), preferred_element_type=F32)


def root(values):
    return lax.rsqrt(jnp.mean(values * values, axis=-1, keepdims=True) + 1e-05)


def root_back(values, gain, grad):
    r = root(values)
    inner = jnp.mean(grad * gain * values, axis=-1, keepdims=True)
    back = r * grad * gain - values * (r * r * r) * inner
    return back, jnp.sum(grad * values * r, axis=0)


def shards(
    tokens,
    cotangent,
    lengths,
    step_rate,
    in_weight,
    out_weight,
    conv_weight,
    gain_mixer,
    gain_feed,
    gate_weight,
    up_weight,
    down_weight,
    in_moment,
    out_moment,
    conv_moment,
    mixer_moment,
    feed_moment,
    gate_moment,
    up_moment,
    down_moment,
):
    core = lax.axis_index("core")
    group = lax.axis_index(G)
    rate = step_rate[0]
    slots, length, width = tokens.shape
    rows = slots * length
    half = width // 2

    taps = lax.dynamic_slice_in_dim(conv_weight, core * 64, 64, 1)
    taps = jnp.pad(taps, ((0, 0), (0, 64)))
    small = jnp.concatenate([gain_mixer[None], gain_feed[None], taps], 0).T
    small = jnp.pad(small, ((0, 0), (0, 123)))
    mix_part = mix_share(in_weight, out_weight, small)
    gate_part = share(288, gate_weight)
    up_part = share(288, up_weight)
    down_part = lax.dynamic_slice_in_dim(down_weight, core * 288, 288, 0).astype(BF16)

    up_quarter = lax.dynamic_slice_in_dim(up_part, lax.axis_index("y") * 32, 32, 0)
    up_quarters = spread(up_quarter, G, 8).reshape(8, 32, 2304)
    piece = lax.axis_index(CHIPS)
    sixteen = lambda value: lax.dynamic_slice_in_dim(value, piece * 16, 16, 0)
    down_moments = lax.dynamic_slice(down_moment, (core * 288, piece * 128), (288, 128))
    down_moments = down_moments.reshape(18, 16, 128).transpose(1, 0, 2).reshape(16, 2304)
    feed_moments = jnp.concatenate(
        [down_moments, share(288, sixteen(up_moment), F32), share(288, sixteen(gate_moment), F32)], 0
    )
    out_moments = lax.dynamic_slice(
        out_moment, (core * 64 + piece % 4 * 16, piece // 4 * half), (16, half)
    )
    tap_moments = lax.dynamic_slice(conv_moment, (0, core * 64 + piece % 4 * 16), (3, 16))
    tap_moments = jnp.where(piece < 4, tap_moments, 0.0)
    small_moments = jnp.concatenate(
        [sixteen(mixer_moment)[None], sixteen(feed_moment)[None], tap_moments], 0
    ).T
    small_moments = jnp.pad(small_moments, ((0, 0), (0, 123)))
    mix_moments = jnp.concatenate(
        [share(64, sixteen(in_moment), F32), out_moments, small_moments], 1
    )
    mix_z = around(mix_part, "z")
    own = tokens.reshape(rows, width)
    rim = from_behind(after(tokens[:, length - 2 :], *mix_z), 1).reshape(2 * slots, width)
    positions = group * length + jnp.arange(length, dtype=jnp.int32)
    valid = (positions[None, :] < lengths[:, None]).reshape(rows, 1)
    branch_own = jnp.where(valid, cotangent.reshape(rows, width), 0).astype(BF16)
    swapped = swap(own), swap(rim), swap(branch_own)

    down_other = across(down_part)
    gate_part, up_quarters, down_other, *both = lax.optimization_barrier(
        (gate_part, up_quarters, down_other, *swapped, *mix_z)
    )
    swapped, mix_z = both[:3], both[3:]
    pad = jnp.zeros((8, width), BF16)
    chip = jnp.concatenate([own, swapped[0], rim, swapped[1], pad], 0)
    branch = jnp.concatenate([branch_own, swapped[2]], 0)
    total_length = after(jnp.sum(lengths).astype(F32), mix_z[0])
    counts = jnp.broadcast_to(total_length, (16, 128))
    count = jnp.sum(lax.all_to_all(counts, DP, 0, 0, tiled=True)[:, 0])
    inverse = jnp.reshape(1.0 / count, (1,))
    mix_x = other_x((mix_part, *mix_z))
    gate_z = around(gate_part, "z")
    down_pair = jnp.concatenate([down_part, down_other])
    down_pair, inverse, up_quarters, *both = lax.optimization_barrier(
        (down_pair, inverse, up_quarters, mix_x, *gate_z)
    )
    mix_x, gate_z = both[0], both[1:]
    gate_x = other_x((gate_part, *gate_z))
    up_near = ring(up_quarters, "y", 1), ring(up_quarters, "y", -1)
    down_z = ring(down_pair, "z", 1), ring(down_pair, "z", -1)
    in_full, out_full, small_full = place_mix((mix_part, *mix_z, mix_x))

    gains = small_full[:, :, :2].reshape(width, 2).astype(F32)
    mixer_gain, feed_gain = gains[:, 0][None], gains[:, 1][None]
    kernel = small_full[:, :64, 2:5].reshape(half, 3).astype(F32).T

    normed_turned, gated_turned, projected, conv_sum, partial, peer = conv_forward(
        chip, in_full, mixer_gain, kernel, out_full
    )
    peer, feed_moments, mix_moments, gate_x, *both = lax.optimization_barrier(
        (peer, feed_moments, mix_moments, gate_x, *down_z, *up_near)
    )
    down_z, up_near = both[:2], both[2:]
    top, bottom = pl.ds(0, 288), pl.ds(288, 288)
    low, high = pl.ds(0, 4), pl.ds(4, 4)
    all_of = lambda z, x: (slice(None),)
    halves = place(
        (*down_z, *up_near),
        [(288, 1024), (288, 1024), (4, 32, 2304), (4, 32, 2304)],
        [(0, (top,), 0, all_of), (1, (bottom,), 1, all_of), (2, (low,), 2, all_of), (3, (high,), 3, all_of)],
    )
    down_far = ring(halves[0], "z", 1), ring(halves[1], "z", -1)
    up_far = ring(halves[2], "y", 1), ring(halves[3], "y", -1)
    up_set = place_quarters((up_quarters, *up_near, *up_far))
    gate_set = place_whole((gate_part, *gate_z, gate_x))
    down_set = place_pair(down_pair, *down_z, *down_far)
    inputs_own = own.astype(F32)
    middle = inputs_own + (partial + swap(peer))
    normed_own = (middle * root(middle) * feed_gain).astype(BF16)
    partials, gate_dots, up_dots, down_dots = feed_forward(
        normed_own, swap(normed_own), branch, gate_set, up_set, down_set
    )

    grad_total, grad_out, sum_feed = norm_back(
        middle, partials[2], swap(partials[3]), feed_gain, branch[:rows]
    )
    partial_in, *mix_dots = conv_back(
        grad_out,
        swap(grad_out),
        out_full,
        projected,
        conv_sum,
        gated_turned,
        normed_turned,
        chip,
        in_full,
        kernel,
        sum_feed,
    )
    mine = lax.axis_index("xl")
    down_here = x_sum(*down_dots, mix_dots[0])
    up_here = x_sum(*up_dots, mix_dots[0])
    mix_here = x_sum(*mix_dots)
    down_part = ring_sum(down_here.reshape(4, 128, 2304), "z")
    gate_pieces = after(lax.all_to_all(gate_dots, "y", 0, 0, tiled=True), mix_dots[0])
    gate_here = jnp.sum(gate_pieces.astype(F32), axis=0).astype(BF16)
    gate_blocks = gate_here.reshape(4, 2, 32, 2304)
    gate_here = x_sum(pick(gate_blocks, 1 - mine, 1), pick(gate_blocks, mine, 1))
    mix_wide = jnp.pad(mix_here.reshape(4, 128, 2176), ((0, 0), (0, 0), (0, 128)))
    last_picks = ring_picks(jnp.concatenate([mix_wide, gate_here], 1), "z")
    up_part = ring_sum(up_here.reshape(4, 128, 2304), "z", *last_picks[1:])
    feed_part = jnp.concatenate([down_part.reshape(8, 16, 2304), up_part.reshape(8, 16, 2304)], 1)
    feed_pieces = lax.all_to_all(feed_part, CHIPS, 0, 0, tiled=True)
    feed_piece = jnp.sum(feed_pieces.astype(F32), axis=0).astype(BF16)
    last_part = near_far_sum(last_picks, "z", feed_part, feed_pieces)
    mix_part, gate_halves = last_part(slice(0, 128)), last_part(slice(128, 160)).reshape(2, 16, 2304)
    half_index = lax.axis_index("xh")
    gate_away = lax.ppermute(pick(gate_halves, 1 - half_index, 0), "xh", [(0, 1), (1, 0)])
    gate_piece = add(pick(gate_halves, half_index, 0), gate_away)
    output = middle + (partials[0] + swap(after(partials[1], mix_part)))
    block_out = output.astype(BF16).reshape(slots, length, width)
    split = 2 * rows + 2 * slots
    here_in = jnp.concatenate([partial_in[:rows], partial_in[2 * rows : split]], 0)
    there_in = jnp.concatenate([partial_in[rows : 2 * rows], partial_in[split : split + 2 * slots]], 0)
    grad_normed = here_in + swap(after(there_in, mix_part))
    inputs_rim = jnp.concatenate([inputs_own, rim.astype(F32)], 0)
    grad_inputs, _ = root_back(inputs_rim, mixer_gain, grad_normed)

    mix_piece = piece_sum(after(mix_part, feed_pieces).reshape(8, 16, 2304), block_out, grad_inputs)
    squares = piece_squares(
        inverse,
        feed_piece,
        gate_piece,
        mix_piece,
        swap(mix_piece[:, 2048:2176]),
        feed_moments,
        mix_moments,
    )
    squares = sum_over(squares + swap(squares), "z")
    pieces = jnp.concatenate([feed_piece, gate_piece, mix_piece], 0)
    back_mine = after(spread(pieces, CHIPS, 8), squares).reshape(8, 64, 2304)
    back_other = swap(back_mine)
    squares = sum_over(after(squares, back_mine), X)
    rim_inputs = from_behind(after(grad_inputs[rows:], squares).reshape(slots, 2, width), -1)
    grad_tokens = (grad_total + grad_inputs[:rows]).reshape(slots, length, width)
    grad_tokens = grad_tokens + jnp.pad(rim_inputs, ((0, 0), (length - 2, 0), (0, 0)))
    grad_tokens = grad_tokens.astype(BF16)
    totals = sum_over(squares, "y")

    scalars = jnp.stack([inverse[0], rate])
    down_new = update("rows", 5, 0, scalars, totals, down_weight, down_moment, back_mine, back_other)
    up_new = update(288, 4, 1, scalars, totals, up_weight, up_moment, back_mine, back_other)
    gate_new = update(288, 3, 2, scalars, totals, gate_weight, gate_moment, back_mine, back_other)
    news = mix_update(
        scalars,
        totals,
        back_mine,
        back_other,
        in_weight,
        in_moment,
        out_weight,
        out_moment,
        conv_weight,
        conv_moment,
        gain_mixer[None],
        mixer_moment[None],
        gain_feed[None],
        feed_moment[None],
    )
    in_new, out_new, conv_new = news[0:2], news[2:4], news[4:6]
    mixer_new, feed_new = [v[0] for v in news[6:8]], [v[0] for v in news[8:10]]
    news = (in_new, out_new, conv_new, mixer_new, feed_new, gate_new, up_new, down_new)
    return (block_out, grad_tokens, *[new[0] for new in news], *[new[1] for new in news])


def solution(mesh):
    fine = Mesh(mesh.devices.reshape(4, 2, 2, 4, 2), ("y", "xh", "core", "z", "xl"))
    rows = P(G, None)
    flat = P(G)
    taps = P(None, G)
    slots = P(DP, G, None)
    weights = (rows, rows, taps, flat, flat, rows, rows, rows)
    return jax.shard_map(
        shards,
        mesh=fine,
        in_specs=(slots, slots, P(DP), P(), *weights, *weights),
        out_specs=(slots, slots, *weights, *weights),
        check_vma=False,
    )
```

```python
import functools

import jax
import jax.numpy as jnp
from jax import lax
from jax.experimental import pallas as pl
from jax.experimental.pallas import tpu as pltpu
from jax.sharding import Mesh
from jax.sharding import PartitionSpec as P

BF16 = jnp.bfloat16
F32 = jnp.float32
X = ("xh", "xl")
G = ("z", "xl")
DP = ("y", "xh", "core")
CHIPS = ("y", "xh")
VMEM = pl.BlockSpec(memory_space=pltpu.VMEM)
SMEM = pl.BlockSpec(memory_space=pltpu.SMEM)
ANY = pl.BlockSpec(memory_space=pl.ANY)
PARAMS = pltpu.CompilerParams(vmem_limit_bytes=48 * 1024 * 1024)
LIGHT = pltpu.CompilerParams(vmem_limit_bytes=20 * 1024 * 1024)
WIDE = pltpu.CompilerParams(vmem_limit_bytes=58 * 1024 * 1024)


def ring(value, axis, by):
    return lax.ppermute(value, axis, [(i, (i + by) % 4) for i in range(4)])


def swap(value):
    return lax.ppermute(value, "core", [(0, 1), (1, 0)])


def across(value):
    at = lambda x, core: (x % 4 // 2) * 4 + core * 2 + x % 2
    pairs = [(at(x, core), at(x + 2 * core - 1, core)) for x in range(4) for core in range(2)]
    return lax.ppermute(value, ("xh", "core", "xl"), pairs)


def from_behind(value, by):
    pairs = [(i, i + by) for i in range(8) if 0 <= i + by < 8]
    return lax.ppermute(value, G, pairs)


def pick(value, index, axis):
    return lax.dynamic_index_in_dim(value, index, axis, keepdims=False)


def after(value, *others):
    return lax.optimization_barrier((value, *others))[0]


def share_kernel(widths, *refs):
    sources, target = refs[:-1], refs[-1]
    for core in range(2):

        @pl.when(lax.axis_index("core") == core)
        def _():
            at = 0
            for source, width in zip(sources, widths):
                for j in range(source.shape[1] // (2 * width)):
                    columns = source[:, (2 * j + core) * width : (2 * j + core + 1) * width]
                    target[:, at : at + width] = columns.astype(target.dtype)
                    at += width


def share(width, source, kind=BF16):
    rows, columns = source.shape
    return pl.pallas_call(
        functools.partial(share_kernel, (width,)),
        out_shape=jax.ShapeDtypeStruct((rows, columns // 2), kind),
        in_specs=[VMEM],
        out_specs=VMEM,
        compiler_params=PARAMS,
    )(source)


def mix_kernel(in_ref, out_ref, small_ref, target):
    for core in range(2):

        @pl.when(lax.axis_index("core") == core)
        def _():
            for j in range(24):
                columns = in_ref[:, (2 * j + core) * 64 : (2 * j + core + 1) * 64]
                target[:, j * 64 : (j + 1) * 64] = columns.astype(BF16)
            rows = out_ref[core * 64 : (core + 1) * 64, :].astype(BF16)
            target[:64, 1536:2048] = rows[:, :512]
            target[64:, 1536:2048] = rows[:, 512:]
            target[:, 2048:] = small_ref[...].astype(BF16)


def mix_share(in_weight, out_weight, small):
    return pl.pallas_call(
        mix_kernel,
        out_shape=jax.ShapeDtypeStruct((128, 2176), BF16),
        in_specs=[VMEM] * 3,
        out_specs=VMEM,
        compiler_params=PARAMS,
    )(in_weight, out_weight, small)


def copies_of(parts, wholes, sems, moves):
    z, x = lax.axis_index("z"), lax.axis_index("xl")
    return [
        pltpu.make_async_copy(parts[part].at[source], wholes[whole].at[where(z, x)], sems.at[number])
        for number, (part, source, whole, where) in enumerate(moves)
    ]


def place_kernel(n_in, n_out, moves, *refs):
    parts, wholes, sems = refs[:n_in], refs[n_in : n_in + n_out], refs[-1]
    copies = copies_of(parts, wholes, sems, moves)
    for copy in copies:
        copy.start()
    for copy in copies:
        copy.wait()


def place(parts, shapes, moves):
    return pl.pallas_call(
        functools.partial(place_kernel, len(parts), len(shapes), moves),
        out_shape=[jax.ShapeDtypeStruct(shape, BF16) for shape in shapes],
        in_specs=[ANY] * len(parts),
        out_specs=[VMEM] * len(shapes),
        scratch_shapes=[pltpu.SemaphoreType.DMA((len(moves),))],
        compiler_params=PARAMS,
    )(*parts)


def block(dz, dx, *rest):
    def where(z, x):
        return (lax.rem(z + dz, 4), x if dx == 0 else 1 - x) + rest

    return where


def around(part, axis):
    return [ring(part, axis, by) for by in (1, -1, 2)]


def other_x(pieces):
    shape = (4,) + pieces[0].shape
    (stack,) = place(pieces, [shape], [(i, (), 0, (lambda z, x, i=i: (i,))) for i in range(4)])
    return across(stack)


BLOCKS = (
    (0, (), 0, 0),
    (1, (), 3, 0),
    (2, (), 1, 0),
    (3, (), 2, 0),
    (4, (0,), 0, 1),
    (4, (1,), 3, 1),
    (4, (2,), 1, 1),
    (4, (3,), 2, 1),
)


def place_whole(pieces):
    rows, columns = pieces[0].shape
    moves = [(part, lead, 0, block(dz, dx)) for part, lead, dz, dx in BLOCKS]
    return pieces, (4, 2, rows, columns), moves


def place_pair(pair, left, right, low, high):
    rows, columns = low.shape
    here, there = pl.ds(0, rows), pl.ds(rows, rows)
    moves = [(part, (here,), 0, block(dz, 0)) for part, dz in ((0, 0), (1, 3), (2, 1))]
    moves += [(part, (there,), 0, block(dz, 1)) for part, dz in ((0, 0), (1, 3), (2, 1))]
    moves += [(3, (), 0, block(2, 0)), (4, (), 0, block(2, 1))]
    return (pair, left, right, low, high), (4, 2, rows, columns), moves


def place_mix(pieces):
    moves = []
    ins, outs, smalls = pl.ds(0, 1536), pl.ds(1536, 512), pl.ds(2048, 128)
    top, bottom, full = pl.ds(0, 64), pl.ds(64, 64), pl.ds(0, 128)
    for part, lead, dz, dx in BLOCKS:
        moves.append((part, lead + (full, ins), 0, block(dz, dx)))
        moves.append((part, lead + (top, outs), 1, block(dz, dx, top, pl.ds(0, 512))))
        moves.append((part, lead + (bottom, outs), 1, block(dz, dx, top, pl.ds(512, 512))))
        moves.append((part, lead + (full, smalls), 2, block(dz, dx)))
    shapes = [(4, 2, 128, 1536), (4, 2, 64, 1024), (4, 2, 128, 128)]
    in_full, out_full, small = place(pieces, shapes, moves)
    return in_full.reshape(1024, 1536), out_full.reshape(512, 1024), small.reshape(8, 128, 128)


def place_quarters(pieces):
    _, rows, columns = pieces[0].shape

    def quarter(owners, by):
        def where(z, x):
            at = pl.multiple_of(lax.rem(lax.axis_index("y") + by, 4) * rows, rows)
            return owners, pl.ds(at, rows)

        return where

    every, low, high = pl.ds(0, 8), pl.ds(0, 4), pl.ds(4, 4)
    order = ((every, 0), (every, 3), (every, 1), (low, 2), (high, 2))
    moves = [(part, (), 0, quarter(*place)) for part, place in enumerate(order)]
    return pieces, (8, 4 * rows, columns), moves


def add(first, *others):
    total = first.astype(F32)
    for other in others:
        total = total + other.astype(F32)
    return total.astype(BF16)


def turned(value):
    return lax.optimization_barrier(value.T)


def ring_sum(blocks, axis, *pins):
    me = lax.axis_index(axis)
    here, on, back, far = [pick(blocks, (me + by) % 4, 0) for by in (0, 1, 3, 2)]
    arrived = (ring(on, axis, 1), ring(back, axis, -1), ring(far, axis, 2))
    return add(here, *[after(part, *pins) for part in arrived])


def ring_picks(blocks, axis):
    me = lax.axis_index(axis)
    return [pick(blocks, (me + by) % 4, 0) for by in (0, 1, 3, 2)]


def near_far_sum(picks, axis, near_pin, far_pin):
    here, on, back, far = picks
    near = here.astype(F32) + after(ring(on, axis, 1), near_pin).astype(F32)
    near = near + after(ring(back, axis, -1), near_pin).astype(F32)
    far = after(ring(far, axis, 2), far_pin).astype(F32)
    return lambda rows: (near[rows] + far[rows]).astype(BF16)


def x_sum(away, here, *pins):
    return add(here, after(across(away), *pins))


def pair_sum(part, axis, by, *pins):
    pairs = [(i, i ^ by) for i in range(lax.axis_size(axis))]
    return add(part, after(lax.ppermute(part, axis, pairs), *pins))


def to_owners(blocks):
    return lax.all_to_all(blocks, ("z", "xl", "y"), 0, 0, tiled=True)


def owner_sum(pieces):
    return pair_sum(jnp.sum(pieces.astype(F32), axis=0).astype(BF16), "xh", 1)


def piece_sum(part, *pins):
    pieces = after(lax.all_to_all(part, CHIPS, 0, 0, tiled=True), *pins)
    return jnp.sum(pieces.astype(F32), axis=0).astype(BF16)


def spread(part, axes, count):
    return lax.all_to_all(jnp.broadcast_to(part[None], (count,) + part.shape), axes, 0, 0, tiled=True)


def chip_sum(part):
    return pair_sum(pair_sum(pair_sum(part, "y", 1), "y", 2), "xh", 1)


def shifted(product, slot):
    main = product[slot * 128 : (slot + 1) * 128]
    rim = product[512 + 2 * slot : 514 + 2 * slot]
    row = lax.broadcasted_iota(jnp.int32, main.shape, 0)
    one = jnp.where(row == 0, rim[1:2], pltpu.roll(main, 1, 0))
    two = pltpu.roll(main, 2, 0)
    two = jnp.where(row == 0, rim[0:1], jnp.where(row == 1, rim[1:2], two))
    return main, one, two


def conv_kernel(
    chip, in_ref, gain, taps, out_ref, normed_turned, gated_turned, projected, conv_sum, partial, peer, normed, gated
):
    inputs = chip[...].astype(F32)
    normed[...] = (inputs * root(inputs) * gain[...]).astype(BF16)
    for j in range(3):
        columns = slice(j * 512, (j + 1) * 512)
        projected[:, columns] = dot(normed[...], in_ref[:, columns])
    product = (projected[:, :512] * projected[:, 1024:]).astype(BF16).astype(F32)
    for slot in range(4):
        rows = slice(slot * 128, (slot + 1) * 128)
        main, one, two = shifted(product, slot)
        conv = taps[0:1] * two + taps[1:2] * one + taps[2:3] * main
        conv_sum[rows, :] = conv
        gated[rows, :] = (projected[rows, 512:1024] * conv).astype(BF16)
    partial[...] = dot(gated[:256, :], out_ref[...])
    peer[...] = dot(gated[256:, :], out_ref[...])
    normed_turned[...] = normed[...].T
    gated_turned[...] = gated[...].T


def conv_forward(*args):
    return pl.pallas_call(
        conv_kernel,
        out_shape=[
            jax.ShapeDtypeStruct((1024, 528), BF16),
            jax.ShapeDtypeStruct((512, 512), BF16),
            jax.ShapeDtypeStruct((528, 1536), F32),
            jax.ShapeDtypeStruct((512, 512), F32),
            jax.ShapeDtypeStruct((256, 1024), F32),
            jax.ShapeDtypeStruct((256, 1024), F32),
        ],
        in_specs=[VMEM] * 5,
        out_specs=[VMEM] * 6,
        scratch_shapes=[pltpu.VMEM((528, 1024), BF16), pltpu.VMEM((512, 512), BF16)],
        compiler_params=PARAMS,
    )(*args)


def conv_back_kernel(
    grad_mine, grad_other, out_ref, projected, conv_sum, gated_turned, normed_turned, chip, in_ref, taps, sum_feed,
    partial, away, own, grad, block, grad_out,
):
    grad_out[:256, :] = grad_mine[...]
    grad_out[256:, :] = grad_other[...]
    gated_back = dot_t(grad_out[...], out_ref[...])
    grad_conv = (gated_back * projected[:512, 512:1024]).astype(BF16).astype(F32)
    grad[:512, 512:1024] = (gated_back * conv_sum[...]).astype(BF16)
    product = (projected[:, :512] * projected[:, 1024:]).astype(BF16).astype(F32)
    sums = [jnp.zeros((1, 512), F32)] * 3
    rim = []
    for slot in range(4):
        rows = slice(slot * 128, (slot + 1) * 128)
        back = grad_conv[rows]
        row = lax.broadcasted_iota(jnp.int32, back.shape, 0)
        one = jnp.where(row == 127, 0.0, pltpu.roll(back, 127, 0))
        two = jnp.where(row >= 126, 0.0, pltpu.roll(back, 126, 0))
        grad_product = taps[0:1] * two + taps[1:2] * one + taps[2:3] * back
        grad[rows, :512] = (grad_product * projected[rows, 1024:]).astype(BF16)
        grad[rows, 1024:] = (grad_product * projected[rows, :512]).astype(BF16)
        rim.append(taps[0:1] * back[0:1])
        rim.append(taps[0:1] * back[1:2] + taps[1:2] * back[0:1])
        main, behind, further = shifted(product, slot)
        for j, value in enumerate((further, behind, main)):
            sums[j] = sums[j] + jnp.sum(back * value, axis=0, keepdims=True)
    rim = jnp.concatenate(rim + [jnp.zeros((8, 512), F32)], 0)
    grad[512:, :512] = (rim * projected[512:, 1024:]).astype(BF16)
    grad[512:, 512:1024] = jnp.zeros((16, 512), BF16)
    grad[512:, 1024:] = (rim * projected[512:, :512]).astype(BF16)
    partial[...] = dot_t(grad[...], in_ref[...])
    inputs = chip[...].astype(F32)
    sum_mixer = jnp.sum(partial[...] * inputs * root(inputs), axis=0, keepdims=True)
    zeros = jnp.zeros((1, 64), F32)
    wide = [
        jnp.concatenate([part for g in range(8) for part in (total[:, g * 64 : (g + 1) * 64], zeros)], 1)
        for total in sums
    ]
    small = jnp.concatenate([sum_mixer, sum_feed[...], *wide, jnp.zeros((123, 1024), F32)], 0).T
    x = lax.axis_index("xl")
    for z in range(4):
        columns = slice(z * 256, (z + 1) * 256)
        block[:, :1536] = dot(normed_turned[columns, :], grad[...]).astype(BF16)
        total = dot(gated_turned[z * 128 : (z + 1) * 128, :], grad_out[...]).astype(BF16)
        for part in range(4):
            corner = total[(part // 2) * 64 : (part // 2 + 1) * 64, (part % 2) * 512 : (part % 2 + 1) * 512]
            block[part * 64 : (part + 1) * 64, 1536:2048] = corner
        block[:, 2048:] = small[columns].astype(BF16)
        cut(block, x, 128, z, away, own)


def conv_back(*args):
    return pl.pallas_call(
        conv_back_kernel,
        out_shape=[
            jax.ShapeDtypeStruct((528, 1024), F32),
            jax.ShapeDtypeStruct((512, 2176), BF16),
            jax.ShapeDtypeStruct((512, 2176), BF16),
        ],
        in_specs=[VMEM] * 11,
        out_specs=[VMEM] * 3,
        scratch_shapes=[
            pltpu.VMEM((528, 1536), BF16),
            pltpu.VMEM((256, 2176), BF16),
            pltpu.VMEM((512, 1024), BF16),
        ],
        compiler_params=WIDE,
    )(*args)


def cut(block, x, rows, z, away, own):
    other = pl.multiple_of((1 - x) * rows, 32)
    mine = pl.multiple_of(x * rows, 32)
    away[z * rows : (z + 1) * rows, :] = block[pl.ds(other, rows), :]
    own[z * rows : (z + 1) * rows, :] = block[pl.ds(mine, rows), :]


def feed_kernel(sets, mine, other, branch, *refs):
    n_in = sum(count for count, _ in sets)
    parts, refs = refs[:n_in], refs[n_in:]
    out_mine, out_other, in_mine, in_other, gate_rows, up_away, up_own, down_away, down_own = refs[:9]
    normed, turned, gate_pre, up_pre, hidden, grad_gate, grad_up, block, tall = refs[9:18]
    wholes, sems = refs[18:21], refs[21:24]
    step = pl.program_id(0)
    x = lax.axis_index("xl")
    copies, at = [], 0
    for (count, moves), whole, sem in zip(sets, wholes, sems):
        copies.append(copies_of(parts[at : at + count], (whole,), sem, moves))
        at += count

    def arrived(which):
        @pl.when(step == 0)
        def _():
            for copy in copies[which]:
                copy.wait()

    columns = pl.ds(pl.multiple_of(step * 1152, 128), 1152)

    @pl.when(step == 0)
    def _():
        for which in copies:
            for copy in which:
                copy.start()
        for ref in (out_mine, out_other, in_mine, in_other):
            ref[...] = jnp.zeros_like(ref)
        normed[:256, :] = mine[...]
        normed[256:, :] = other[...]
        turned[...] = normed[...].T

    arrived(0)
    gate = wholes[0][:, :, :, columns].reshape(1024, 1152)
    gate_pre[...] = dot(normed[...], gate)
    arrived(1)
    up = wholes[1][:, :, columns].reshape(1024, 1152)
    up_pre[...] = dot(normed[...], up)
    arrived(2)
    down = wholes[2][pl.ds(2 * step, 2)].reshape(1152, 1024)
    grad_hid = dot_t(branch[...], down)
    for part in range(4):
        rows = slice(part * 128, (part + 1) * 128)
        grad_hidden = grad_hid[rows, :]
        sigmoid = jax.nn.sigmoid(gate_pre[rows, :])
        silu = gate_pre[rows, :] * sigmoid
        hidden[rows, :] = (silu * up_pre[rows, :]).astype(BF16)
        grad_up[rows, :] = (grad_hidden * silu).astype(BF16)
        slope = grad_hidden * up_pre[rows, :] * sigmoid * (1.0 + gate_pre[rows, :] * (1.0 - sigmoid))
        grad_gate[rows, :] = slope.astype(BF16)
    for rows, out_part, in_part in ((slice(0, 256), out_mine, in_mine), (slice(256, 512), out_other, in_other)):
        out_part[...] += dot(hidden[rows, :], down)
        in_part[...] += dot_t(grad_gate[rows, :], gate) + dot_t(grad_up[rows, :], up)
    tall[...] = t_dot(hidden[...], branch[...]).astype(BF16)
    for part in range(2):
        for target, source in ((down_away, 2 * part + 1 - x), (down_own, 2 * part + x)):
            for i in range(18):
                at = pl.multiple_of(source * 288 + i * 16, 16)
                rows = tall[pl.ds(at, 16), :]
                for j in range(8):
                    target[part * 128 + j * 16 : part * 128 + (j + 1) * 16, i * 128 : (i + 1) * 128] = rows[
                        :, j * 128 : (j + 1) * 128
                    ]

    for z in range(4):
        rows = turned[z * 256 : (z + 1) * 256, :]
        block[...] = dot(rows, grad_gate[...]).astype(BF16)
        for source in range(2):
            for y in range(4):
                at = z * 64 + source * 32
                gate_rows[y, at : at + 32, :] = block[source * 128 + y * 32 : source * 128 + (y + 1) * 32, :]
        block[...] = dot(rows, grad_up[...]).astype(BF16)
        cut(block, x, 128, z, up_away, up_own)


def feed_forward(mine, other, branch, *weights):
    sets = [(len(pieces), moves) for pieces, _, moves in weights]
    parts = [piece for pieces, _, _ in weights for piece in pieces]
    whole = lambda *shape: pl.BlockSpec(shape, lambda i: (0, 0), pipeline_mode=pl.Buffered(1))
    total = lambda *shape: pl.BlockSpec(shape, lambda i: (0, 0))
    columns = lambda rows: pl.BlockSpec((rows, 1152), lambda i: (0, i))
    outs = pl.pallas_call(
        functools.partial(feed_kernel, sets),
        grid=(2,),
        out_shape=[
            *[jax.ShapeDtypeStruct((256, 1024), F32)] * 4,
            jax.ShapeDtypeStruct((4, 256, 2304), BF16),
            *[jax.ShapeDtypeStruct((512, 2304), BF16)] * 4,
        ],
        in_specs=[
            whole(256, 1024),
            whole(256, 1024),
            whole(512, 1024),
            *[ANY] * len(parts),
        ],
        out_specs=[
            *[total(256, 1024)] * 4,
            pl.BlockSpec((4, 256, 1152), lambda i: (0, 0, i)),
            *[columns(512)] * 2,
            *[pl.BlockSpec((256, 2304), lambda i: (i, 0))] * 2,
        ],
        scratch_shapes=[
            pltpu.VMEM((512, 1024), BF16),
            pltpu.VMEM((1024, 512), BF16),
            *[pltpu.VMEM((512, 1152), F32)] * 2,
            *[pltpu.VMEM((512, 1152), BF16)] * 3,
            pltpu.VMEM((256, 1152), BF16),
            pltpu.VMEM((1152, 1024), BF16),
            *[pltpu.VMEM(shape, BF16) for _, shape, _ in weights],
            *[pltpu.SemaphoreType.DMA((len(moves),)) for _, _, moves in weights],
        ],
        compiler_params=WIDE,
    )(mine, other, branch, *parts)
    return outs[:4], outs[4], outs[5:7], outs[7:9]


def norm_back_kernel(middle, here, there, gain, branch, grad_total, grad_out, sum_gain):
    values, grad = middle[...], here[...] + there[...]
    back, total = root_back(values, gain[...], grad)
    total_grad = branch[...].astype(F32) + back
    grad_total[...] = total_grad
    grad_out[...] = total_grad.astype(BF16)
    sum_gain[...] = total[None]


def norm_back(*args):
    return pl.pallas_call(
        norm_back_kernel,
        out_shape=[
            jax.ShapeDtypeStruct((256, 1024), F32),
            jax.ShapeDtypeStruct((256, 1024), BF16),
            jax.ShapeDtypeStruct((1, 1024), F32),
        ],
        in_specs=[VMEM] * 5,
        out_specs=[VMEM] * 3,
        compiler_params=PARAMS,
    )(*args)


def square_kernel(inverse, feed, gate, mix, small, feed_moment, mix_moment, target):
    target[...] = jnp.zeros_like(target)

    def fold(row, grad, moment):
        blend = 0.9 * moment + 0.1 * (grad.astype(F32) * inverse[0])
        square = jnp.sum(blend * blend, axis=0, keepdims=True)
        total = square[:, :128]
        for j in range(1, square.shape[1] // 128):
            total = total + square[:, j * 128 : (j + 1) * 128]
        target[row : row + 1, :] = total

    fold(0, mix[:, :1536], mix_moment[:, :1536])
    fold(1, mix[:, 1536:2048], mix_moment[:, 1536:2048])
    fold(3, gate[...], feed_moment[32:, :])
    fold(4, feed[16:, :], feed_moment[16:32, :])
    fold(5, feed[:16, :], feed_moment[:16, :])
    mine, other = mix[:, 2048:2176].astype(F32), small[...].astype(F32)
    lane = lax.broadcasted_iota(jnp.int32, mine.shape, 1)
    blend = 0.9 * mix_moment[:, 2048:] + 0.1 * (jnp.where(lane < 2, mine + other, mine) * inverse[0])
    once = jnp.where(lane >= 2, 1.0, jnp.where(lax.axis_index("core") == 0, 1.0, 0.0))
    target[2:3, :] = jnp.sum(blend * blend * once, axis=0, keepdims=True)


def piece_squares(*args):
    return pl.pallas_call(
        square_kernel,
        out_shape=jax.ShapeDtypeStruct((8, 128), F32),
        in_specs=[SMEM] + [VMEM] * 6,
        out_specs=VMEM,
        compiler_params=LIGHT,
    )(*args)


def sum_over(value, *axes):
    for axis in axes:
        back, on, far = around(value, axis)
        value = (value + far) + (on + back)
    return value


def returned(mine_ref, other_ref):
    mine, other = mine_ref[...].astype(F32), other_ref[...].astype(F32)
    zero = lax.axis_index("core") == 0
    return jnp.where(zero, mine, other), jnp.where(zero, other, mine)


def update_kernel(kind, row, scalars, totals, w_ref, m_ref, mine_ref, other_ref, w_new, m_new, grad):
    for core, share in enumerate(returned(mine_ref, other_ref)):
        if kind == "rows":
            for i in range(18):
                for j in range(8):
                    rows = slice(core * 288 + i * 16, core * 288 + (i + 1) * 16)
                    grad[rows, j * 128 : (j + 1) * 128] = share[
                        j * 16 : (j + 1) * 16, i * 128 : (i + 1) * 128
                    ]
        else:
            for j in range(share.shape[1] // kind):
                grad[:, (2 * j + core) * kind : (2 * j + core + 1) * kind] = share[
                    :, j * kind : (j + 1) * kind
                ]
    m, w = m_ref[...], w_ref[...]
    mean = grad[...] * scalars[0]
    blend = 0.9 * m + 0.1 * mean
    m_new[...] = 0.5 * m + 0.5 * mean
    square = jnp.sum(totals[row : row + 1, :], axis=1, keepdims=True)
    scale = lax.rsqrt(square / (w.size * 8) + 1e-06)
    w_new[...] = w - scalars[1] * (jnp.tanh(2.0 * blend * scale) + 0.1 * w)


def update(kind, row, scalars, totals, weight, moment, mine, other):
    return pl.pallas_call(
        functools.partial(update_kernel, kind, row),
        out_shape=[jax.ShapeDtypeStruct(weight.shape, F32)] * 2,
        in_specs=[SMEM] + [VMEM] * 5,
        out_specs=[VMEM, VMEM],
        scratch_shapes=[pltpu.VMEM(weight.shape, F32)],
        compiler_params=PARAMS,
    )(scalars, totals, weight, moment, mine, other)


def mix_update_kernel(
    scalars, totals, mine, other, in_w, in_m, out_w, out_m, conv_w, conv_m, mixer_w, mixer_m, feed_w, feed_m,
    in_wn, in_mn, out_wn, out_mn, conv_wn, conv_mn, mixer_wn, mixer_mn, feed_wn, feed_mn, grad, wide,
):
    def step(grad, square, count, w_ref, m_ref, w_new, m_new):
        m, w = m_ref[...], w_ref[...]
        mean = grad * scalars[0]
        scale = lax.rsqrt(square / count + 1e-06)
        m_new[...] = 0.5 * m + 0.5 * mean
        move = jnp.tanh(2.0 * (0.9 * m + 0.1 * mean) * scale) + 0.1 * w
        w_new[...] = w - scalars[1] * move

    first, second = returned(mine, other)
    for core, half in enumerate((first, second)):
        for j in range(24):
            grad[:, (2 * j + core) * 64 : (2 * j + core + 1) * 64] = half[:, j * 64 : (j + 1) * 64]
        wide[core * 64 : (core + 1) * 64, :512] = half[:64, 1536:2048]
        wide[core * 64 : (core + 1) * 64, 512:] = half[64:, 1536:2048]
    total = lambda row: jnp.sum(totals[row : row + 1, :], axis=1, keepdims=True)
    step(grad[...], total(0), 1024 * 3072, in_w, in_m, in_wn, in_mn)
    step(wide[...], total(1), 1024 * 1024, out_w, out_m, out_wn, out_mn)
    one, two = first[:, 2048:2176].T, second[:, 2048:2176].T
    lane = lax.broadcasted_iota(jnp.int32, (1, 128), 1)
    among = lambda low, high: jnp.sum(
        jnp.where((lane >= low) & (lane < high), totals[2:3, :], 0.0), axis=1, keepdims=True
    )
    taps = jnp.where(lane < 64, one[2:5], pltpu.roll(two[2:5], 64, 1))
    step(taps, among(2, 5), 3 * 1024, conv_w, conv_m, conv_wn, conv_mn)
    step(one[0:1] + two[0:1], among(0, 1), 1024, mixer_w, mixer_m, mixer_wn, mixer_mn)
    step(one[1:2] + two[1:2], among(1, 2), 1024, feed_w, feed_m, feed_wn, feed_mn)


def mix_update(scalars, totals, first, second, *arrays):
    shapes = [jax.ShapeDtypeStruct(v.shape, F32) for v in arrays]
    return pl.pallas_call(
        mix_update_kernel,
        out_shape=shapes,
        in_specs=[SMEM] + [VMEM] * (3 + len(arrays)),
        out_specs=[VMEM] * len(arrays),
        scratch_shapes=[pltpu.VMEM((128, 3072), F32), pltpu.VMEM((128, 1024), F32)],
        compiler_params=PARAMS,
    )(scalars, totals, first, second, *arrays)


def dot(left, right):
    return jnp.dot(left, right, preferred_element_type=F32)


def dot_t(left, right):
    return lax.dot_general(left, right, (((1,), (1,)), ((), ())), preferred_element_type=F32)


def t_dot(left, right):
    return lax.dot_general(left, right, (((0,), (0,)), ((), ())), preferred_element_type=F32)


def root(values):
    return lax.rsqrt(jnp.mean(values * values, axis=-1, keepdims=True) + 1e-05)


def root_back(values, gain, grad):
    r = root(values)
    inner = jnp.mean(grad * gain * values, axis=-1, keepdims=True)
    back = r * grad * gain - values * (r * r * r) * inner
    return back, jnp.sum(grad * values * r, axis=0)


def shards(
    tokens,
    cotangent,
    lengths,
    step_rate,
    in_weight,
    out_weight,
    conv_weight,
    gain_mixer,
    gain_feed,
    gate_weight,
    up_weight,
    down_weight,
    in_moment,
    out_moment,
    conv_moment,
    mixer_moment,
    feed_moment,
    gate_moment,
    up_moment,
    down_moment,
):
    core = lax.axis_index("core")
    group = lax.axis_index(G)
    rate = step_rate[0]
    slots, length, width = tokens.shape
    rows = slots * length
    half = width // 2

    taps = lax.dynamic_slice_in_dim(conv_weight, core * 64, 64, 1)
    taps = jnp.pad(taps, ((0, 0), (0, 64)))
    small = jnp.concatenate([gain_mixer[None], gain_feed[None], taps], 0).T
    small = jnp.pad(small, ((0, 0), (0, 123)))
    mix_part = mix_share(in_weight, out_weight, small)
    gate_part = share(288, gate_weight)
    up_part = share(288, up_weight)
    down_part = lax.dynamic_slice_in_dim(down_weight, core * 288, 288, 0).astype(BF16)

    up_quarter = lax.dynamic_slice_in_dim(up_part, lax.axis_index("y") * 32, 32, 0)
    up_quarters = spread(up_quarter, G, 8).reshape(8, 32, 2304)
    piece = lax.axis_index(CHIPS)
    sixteen = lambda value: lax.dynamic_slice_in_dim(value, piece * 16, 16, 0)
    down_moments = lax.dynamic_slice(down_moment, (core * 288, piece * 128), (288, 128))
    down_moments = down_moments.reshape(18, 16, 128).transpose(1, 0, 2).reshape(16, 2304)
    feed_moments = jnp.concatenate(
        [down_moments, share(288, sixteen(up_moment), F32), share(288, sixteen(gate_moment), F32)], 0
    )
    out_moments = lax.dynamic_slice(
        out_moment, (core * 64 + piece % 4 * 16, piece // 4 * half), (16, half)
    )
    tap_moments = lax.dynamic_slice(conv_moment, (0, core * 64 + piece % 4 * 16), (3, 16))
    tap_moments = jnp.where(piece < 4, tap_moments, 0.0)
    small_moments = jnp.concatenate(
        [sixteen(mixer_moment)[None], sixteen(feed_moment)[None], tap_moments], 0
    ).T
    small_moments = jnp.pad(small_moments, ((0, 0), (0, 123)))
    mix_moments = jnp.concatenate(
        [share(64, sixteen(in_moment), F32), out_moments, small_moments], 1
    )
    mix_z = around(mix_part, "z")
    own = tokens.reshape(rows, width)
    rim = from_behind(after(tokens[:, length - 2 :], *mix_z), 1).reshape(2 * slots, width)
    positions = group * length + jnp.arange(length, dtype=jnp.int32)
    valid = (positions[None, :] < lengths[:, None]).reshape(rows, 1)
    branch_own = jnp.where(valid, cotangent.reshape(rows, width), 0).astype(BF16)
    swapped = swap(own), swap(rim), swap(branch_own)

    down_other = across(down_part)
    gate_part, up_quarters, down_other, *both = lax.optimization_barrier(
        (gate_part, up_quarters, down_other, *swapped, *mix_z)
    )
    swapped, mix_z = both[:3], both[3:]
    pad = jnp.zeros((8, width), BF16)
    chip = jnp.concatenate([own, swapped[0], rim, swapped[1], pad], 0)
    branch = jnp.concatenate([branch_own, swapped[2]], 0)
    total_length = after(jnp.sum(lengths).astype(F32), mix_z[0])
    counts = jnp.broadcast_to(total_length, (16, 128))
    count = jnp.sum(lax.all_to_all(counts, DP, 0, 0, tiled=True)[:, 0])
    inverse = jnp.reshape(1.0 / count, (1,))
    mix_x = other_x((mix_part, *mix_z))
    gate_z = around(gate_part, "z")
    down_pair = jnp.concatenate([down_part, down_other])
    down_pair, inverse, up_quarters, *both = lax.optimization_barrier(
        (down_pair, inverse, up_quarters, mix_x, *gate_z)
    )
    mix_x, gate_z = both[0], both[1:]
    gate_x = other_x((gate_part, *gate_z))
    up_near = ring(up_quarters, "y", 1), ring(up_quarters, "y", -1)
    down_z = ring(down_pair, "z", 1), ring(down_pair, "z", -1)
    in_full, out_full, small_full = place_mix((mix_part, *mix_z, mix_x))

    gains = small_full[:, :, :2].reshape(width, 2).astype(F32)
    mixer_gain, feed_gain = gains[:, 0][None], gains[:, 1][None]
    kernel = small_full[:, :64, 2:5].reshape(half, 3).astype(F32).T

    normed_turned, gated_turned, projected, conv_sum, partial, peer = conv_forward(
        chip, in_full, mixer_gain, kernel, out_full
    )
    peer, feed_moments, mix_moments, gate_x, *both = lax.optimization_barrier(
        (peer, feed_moments, mix_moments, gate_x, *down_z, *up_near)
    )
    down_z, up_near = both[:2], both[2:]
    top, bottom = pl.ds(0, 288), pl.ds(288, 288)
    low, high = pl.ds(0, 4), pl.ds(4, 4)
    all_of = lambda z, x: (slice(None),)
    halves = place(
        (*down_z, *up_near),
        [(288, 1024), (288, 1024), (4, 32, 2304), (4, 32, 2304)],
        [(0, (top,), 0, all_of), (1, (bottom,), 1, all_of), (2, (low,), 2, all_of), (3, (high,), 3, all_of)],
    )
    down_far = ring(halves[0], "z", 1), ring(halves[1], "z", -1)
    up_far = ring(halves[2], "y", 1), ring(halves[3], "y", -1)
    up_set = place_quarters((up_quarters, *up_near, *up_far))
    gate_set = place_whole((gate_part, *gate_z, gate_x))
    down_set = place_pair(down_pair, *down_z, *down_far)
    inputs_own = own.astype(F32)
    middle = inputs_own + (partial + swap(peer))
    normed_own = (middle * root(middle) * feed_gain).astype(BF16)
    partials, gate_dots, up_dots, down_dots = feed_forward(
        normed_own, swap(normed_own), branch, gate_set, up_set, down_set
    )

    grad_total, grad_out, sum_feed = norm_back(
        middle, partials[2], swap(partials[3]), feed_gain, branch[:rows]
    )
    partial_in, *mix_dots = conv_back(
        grad_out,
        swap(grad_out),
        out_full,
        projected,
        conv_sum,
        gated_turned,
        normed_turned,
        chip,
        in_full,
        kernel,
        sum_feed,
    )
    mine = lax.axis_index("xl")
    down_here = x_sum(*down_dots, mix_dots[0])
    up_here = x_sum(*up_dots, mix_dots[0])
    mix_here = x_sum(*mix_dots)
    down_part = ring_sum(down_here.reshape(4, 128, 2304), "z")
    gate_pieces = after(lax.all_to_all(gate_dots, "y", 0, 0, tiled=True), mix_dots[0])
    gate_here = jnp.sum(gate_pieces.astype(F32), axis=0).astype(BF16)
    gate_blocks = gate_here.reshape(4, 2, 32, 2304)
    gate_here = x_sum(pick(gate_blocks, 1 - mine, 1), pick(gate_blocks, mine, 1))
    mix_wide = jnp.pad(mix_here.reshape(4, 128, 2176), ((0, 0), (0, 0), (0, 128)))
    last_picks = ring_picks(jnp.concatenate([mix_wide, gate_here], 1), "z")
    up_part = ring_sum(up_here.reshape(4, 128, 2304), "z", *last_picks[1:])
    feed_part = jnp.concatenate([down_part.reshape(8, 16, 2304), up_part.reshape(8, 16, 2304)], 1)
    feed_pieces = lax.all_to_all(feed_part, CHIPS, 0, 0, tiled=True)
    feed_piece = jnp.sum(feed_pieces.astype(F32), axis=0).astype(BF16)
    last_part = near_far_sum(last_picks, "z", feed_part, feed_pieces)
    mix_part, gate_halves = last_part(slice(0, 128)), last_part(slice(128, 160)).reshape(2, 16, 2304)
    half_index = lax.axis_index("xh")
    gate_away = lax.ppermute(pick(gate_halves, 1 - half_index, 0), "xh", [(0, 1), (1, 0)])
    gate_piece = add(pick(gate_halves, half_index, 0), gate_away)
    output = middle + (partials[0] + swap(after(partials[1], mix_part)))
    block_out = output.astype(BF16).reshape(slots, length, width)
    split = 2 * rows + 2 * slots
    here_in = jnp.concatenate([partial_in[:rows], partial_in[2 * rows : split]], 0)
    there_in = jnp.concatenate([partial_in[rows : 2 * rows], partial_in[split : split + 2 * slots]], 0)
    grad_normed = here_in + swap(after(there_in, mix_part))
    inputs_rim = jnp.concatenate([inputs_own, rim.astype(F32)], 0)
    grad_inputs, _ = root_back(inputs_rim, mixer_gain, grad_normed)

    mix_piece = piece_sum(after(mix_part, feed_pieces).reshape(8, 16, 2304), block_out, grad_inputs)
    squares = piece_squares(
        inverse,
        feed_piece,
        gate_piece,
        mix_piece,
        swap(mix_piece[:, 2048:2176]),
        feed_moments,
        mix_moments,
    )
    squares = sum_over(squares + swap(squares), "z")
    pieces = jnp.concatenate([feed_piece, gate_piece, mix_piece], 0)
    back_mine = after(spread(pieces, CHIPS, 8), squares).reshape(8, 64, 2304)
    back_other = swap(back_mine)
    squares = sum_over(after(squares, back_mine), X)
    rim_inputs = from_behind(after(grad_inputs[rows:], squares).reshape(slots, 2, width), -1)
    grad_tokens = (grad_total + grad_inputs[:rows]).reshape(slots, length, width)
    grad_tokens = grad_tokens + jnp.pad(rim_inputs, ((0, 0), (length - 2, 0), (0, 0)))
    grad_tokens = grad_tokens.astype(BF16)
    totals = sum_over(squares, "y")

    scalars = jnp.stack([inverse[0], rate])
    shares = [
        [v[:, at : at + 16].reshape(128, 2304) for v in (back_mine, back_other)] for at in (0, 16, 32, 48)
    ]
    down_new = update("rows", 5, scalars, totals, down_weight, down_moment, *shares[0])
    up_new = update(288, 4, scalars, totals, up_weight, up_moment, *shares[1])
    gate_new = update(288, 3, scalars, totals, gate_weight, gate_moment, *shares[2])
    news = mix_update(
        scalars,
        totals,
        *shares[3],
        in_weight,
        in_moment,
        out_weight,
        out_moment,
        conv_weight,
        conv_moment,
        gain_mixer[None],
        mixer_moment[None],
        gain_feed[None],
        feed_moment[None],
    )
    in_new, out_new, conv_new = news[0:2], news[2:4], news[4:6]
    mixer_new, feed_new = [v[0] for v in news[6:8]], [v[0] for v in news[8:10]]
    news = (in_new, out_new, conv_new, mixer_new, feed_new, gate_new, up_new, down_new)
    return (block_out, grad_tokens, *[new[0] for new in news], *[new[1] for new in news])


def solution(mesh):
    fine = Mesh(mesh.devices.reshape(4, 2, 2, 4, 2), ("y", "xh", "core", "z", "xl"))
    rows = P(G, None)
    flat = P(G)
    taps = P(None, G)
    slots = P(DP, G, None)
    weights = (rows, rows, taps, flat, flat, rows, rows, rows)
    return jax.shard_map(
        shards,
        mesh=fine,
        in_specs=(slots, slots, P(DP), P(), *weights, *weights),
        out_specs=(slots, slots, *weights, *weights),
        check_vma=False,
    )
```

```python
import functools

import jax
import jax.numpy as jnp
from jax import lax
from jax.experimental import pallas as pl
from jax.experimental.pallas import tpu as pltpu
from jax.sharding import Mesh
from jax.sharding import PartitionSpec as P

BF16 = jnp.bfloat16
F32 = jnp.float32
X = ("xh", "xl")
G = ("z", "xl")
DP = ("y", "xh", "core")
CHIPS = ("y", "xh")
VMEM = pl.BlockSpec(memory_space=pltpu.VMEM)
SMEM = pl.BlockSpec(memory_space=pltpu.SMEM)
ANY = pl.BlockSpec(memory_space=pl.ANY)
PARAMS = pltpu.CompilerParams(vmem_limit_bytes=48 * 1024 * 1024)
LIGHT = pltpu.CompilerParams(vmem_limit_bytes=20 * 1024 * 1024)
WIDE = pltpu.CompilerParams(vmem_limit_bytes=58 * 1024 * 1024)


def ring(value, axis, by):
    return lax.ppermute(value, axis, [(i, (i + by) % 4) for i in range(4)])


def swap(value):
    return lax.ppermute(value, "core", [(0, 1), (1, 0)])


def across(value):
    at = lambda x, core: (x % 4 // 2) * 4 + core * 2 + x % 2
    pairs = [(at(x, core), at(x + 2 * core - 1, core)) for x in range(4) for core in range(2)]
    return lax.ppermute(value, ("xh", "core", "xl"), pairs)


def from_behind(value, by):
    pairs = [(i, i + by) for i in range(8) if 0 <= i + by < 8]
    return lax.ppermute(value, G, pairs)


def pick(value, index, axis):
    return lax.dynamic_index_in_dim(value, index, axis, keepdims=False)


def after(value, *others):
    return lax.optimization_barrier((value, *others))[0]


def share_kernel(widths, *refs):
    sources, target = refs[:-1], refs[-1]
    for core in range(2):

        @pl.when(lax.axis_index("core") == core)
        def _():
            at = 0
            for source, width in zip(sources, widths):
                for j in range(source.shape[1] // (2 * width)):
                    columns = source[:, (2 * j + core) * width : (2 * j + core + 1) * width]
                    target[:, at : at + width] = columns.astype(target.dtype)
                    at += width


def share(width, source, kind=BF16):
    rows, columns = source.shape
    return pl.pallas_call(
        functools.partial(share_kernel, (width,)),
        out_shape=jax.ShapeDtypeStruct((rows, columns // 2), kind),
        in_specs=[VMEM],
        out_specs=VMEM,
        compiler_params=PARAMS,
    )(source)


def mix_kernel(in_ref, out_ref, small_ref, target):
    for core in range(2):

        @pl.when(lax.axis_index("core") == core)
        def _():
            for j in range(24):
                columns = in_ref[:, (2 * j + core) * 64 : (2 * j + core + 1) * 64]
                target[:, j * 64 : (j + 1) * 64] = columns.astype(BF16)
            rows = out_ref[core * 64 : (core + 1) * 64, :].astype(BF16)
            target[:64, 1536:2048] = rows[:, :512]
            target[64:, 1536:2048] = rows[:, 512:]
            target[:, 2048:] = small_ref[...].astype(BF16)


def mix_share(in_weight, out_weight, small):
    return pl.pallas_call(
        mix_kernel,
        out_shape=jax.ShapeDtypeStruct((128, 2176), BF16),
        in_specs=[VMEM] * 3,
        out_specs=VMEM,
        compiler_params=PARAMS,
    )(in_weight, out_weight, small)


def copies_of(parts, wholes, sems, moves):
    z, x = lax.axis_index("z"), lax.axis_index("xl")
    return [
        pltpu.make_async_copy(parts[part].at[source], wholes[whole].at[where(z, x)], sems.at[number])
        for number, (part, source, whole, where) in enumerate(moves)
    ]


def place_kernel(n_in, n_out, moves, *refs):
    parts, wholes, sems = refs[:n_in], refs[n_in : n_in + n_out], refs[-1]
    copies = copies_of(parts, wholes, sems, moves)
    for copy in copies:
        copy.start()
    for copy in copies:
        copy.wait()


def place(parts, shapes, moves):
    return pl.pallas_call(
        functools.partial(place_kernel, len(parts), len(shapes), moves),
        out_shape=[jax.ShapeDtypeStruct(shape, BF16) for shape in shapes],
        in_specs=[ANY] * len(parts),
        out_specs=[VMEM] * len(shapes),
        scratch_shapes=[pltpu.SemaphoreType.DMA((len(moves),))],
        compiler_params=PARAMS,
    )(*parts)


def block(dz, dx, *rest):
    def where(z, x):
        return (lax.rem(z + dz, 4), x if dx == 0 else 1 - x) + rest

    return where


def around(part, axis):
    return [ring(part, axis, by) for by in (1, -1, 2)]


def other_x(pieces):
    shape = (4,) + pieces[0].shape
    (stack,) = place(pieces, [shape], [(i, (), 0, (lambda z, x, i=i: (i,))) for i in range(4)])
    return across(stack)


BLOCKS = (
    (0, (), 0, 0),
    (1, (), 3, 0),
    (2, (), 1, 0),
    (3, (), 2, 0),
    (4, (0,), 0, 1),
    (4, (1,), 3, 1),
    (4, (2,), 1, 1),
    (4, (3,), 2, 1),
)


def place_whole(pieces):
    rows, columns = pieces[0].shape
    moves = [(part, lead, 0, block(dz, dx)) for part, lead, dz, dx in BLOCKS]
    return pieces, (4, 2, rows, columns), moves


def place_pair(pair, left, right, low, high):
    rows, columns = low.shape
    here, there = pl.ds(0, rows), pl.ds(rows, rows)
    moves = [(part, (here,), 0, block(dz, 0)) for part, dz in ((0, 0), (1, 3), (2, 1))]
    moves += [(part, (there,), 0, block(dz, 1)) for part, dz in ((0, 0), (1, 3), (2, 1))]
    moves += [(3, (), 0, block(2, 0)), (4, (), 0, block(2, 1))]
    return (pair, left, right, low, high), (4, 2, rows, columns), moves


def place_mix(pieces):
    moves = []
    ins, outs, smalls = pl.ds(0, 1536), pl.ds(1536, 512), pl.ds(2048, 128)
    top, bottom, full = pl.ds(0, 64), pl.ds(64, 64), pl.ds(0, 128)
    for part, lead, dz, dx in BLOCKS:
        moves.append((part, lead + (full, ins), 0, block(dz, dx)))
        moves.append((part, lead + (top, outs), 1, block(dz, dx, top, pl.ds(0, 512))))
        moves.append((part, lead + (bottom, outs), 1, block(dz, dx, top, pl.ds(512, 512))))
        moves.append((part, lead + (full, smalls), 2, block(dz, dx)))
    shapes = [(4, 2, 128, 1536), (4, 2, 64, 1024), (4, 2, 128, 128)]
    in_full, out_full, small = place(pieces, shapes, moves)
    return in_full.reshape(1024, 1536), out_full.reshape(512, 1024), small.reshape(8, 128, 128)


def place_quarters(pieces):
    _, rows, columns = pieces[0].shape

    def quarter(owners, by):
        def where(z, x):
            at = pl.multiple_of(lax.rem(lax.axis_index("y") + by, 4) * rows, rows)
            return owners, pl.ds(at, rows)

        return where

    every, low, high = pl.ds(0, 8), pl.ds(0, 4), pl.ds(4, 4)
    order = ((every, 0), (every, 3), (every, 1), (low, 2), (high, 2))
    moves = [(part, (), 0, quarter(*place)) for part, place in enumerate(order)]
    return pieces, (8, 4 * rows, columns), moves


def add(first, *others):
    total = first.astype(F32)
    for other in others:
        total = total + other.astype(F32)
    return total.astype(BF16)


def turned(value):
    return lax.optimization_barrier(value.T)


def ring_sum(blocks, axis, *pins):
    me = lax.axis_index(axis)
    here, on, back, far = [pick(blocks, (me + by) % 4, 0) for by in (0, 1, 3, 2)]
    arrived = (ring(on, axis, 1), ring(back, axis, -1), ring(far, axis, 2))
    return add(here, *[after(part, *pins) for part in arrived])


def ring_picks(blocks, axis):
    me = lax.axis_index(axis)
    return [pick(blocks, (me + by) % 4, 0) for by in (0, 1, 3, 2)]


def near_far_sum(picks, axis, near_pin, far_pin):
    here, on, back, far = picks
    near = here.astype(F32) + after(ring(on, axis, 1), near_pin).astype(F32)
    near = near + after(ring(back, axis, -1), near_pin).astype(F32)
    far = after(ring(far, axis, 2), far_pin).astype(F32)
    return lambda rows: (near[rows] + far[rows]).astype(BF16)


def x_sum(away, here, *pins):
    return add(here, after(across(away), *pins))


def pair_sum(part, axis, by, *pins):
    pairs = [(i, i ^ by) for i in range(lax.axis_size(axis))]
    return add(part, after(lax.ppermute(part, axis, pairs), *pins))


def to_owners(blocks):
    return lax.all_to_all(blocks, ("z", "xl", "y"), 0, 0, tiled=True)


def owner_sum(pieces):
    return pair_sum(jnp.sum(pieces.astype(F32), axis=0).astype(BF16), "xh", 1)


def piece_sum(part, *pins):
    pieces = after(lax.all_to_all(part, CHIPS, 0, 0, tiled=True), *pins)
    return jnp.sum(pieces.astype(F32), axis=0).astype(BF16)


def spread(part, axes, count):
    return lax.all_to_all(jnp.broadcast_to(part[None], (count,) + part.shape), axes, 0, 0, tiled=True)


def chip_sum(part):
    return pair_sum(pair_sum(pair_sum(part, "y", 1), "y", 2), "xh", 1)


def shifted(product, slot):
    main = product[slot * 128 : (slot + 1) * 128]
    rim = product[512 + 2 * slot : 514 + 2 * slot]
    row = lax.broadcasted_iota(jnp.int32, main.shape, 0)
    one = jnp.where(row == 0, rim[1:2], pltpu.roll(main, 1, 0))
    two = pltpu.roll(main, 2, 0)
    two = jnp.where(row == 0, rim[0:1], jnp.where(row == 1, rim[1:2], two))
    return main, one, two


def conv_kernel(
    chip, in_ref, gain, taps, out_ref, normed_turned, gated_turned, projected, conv_sum, partial, peer, normed, gated
):
    inputs = chip[...].astype(F32)
    normed[...] = (inputs * root(inputs) * gain[...]).astype(BF16)
    for j in range(3):
        columns = slice(j * 512, (j + 1) * 512)
        projected[:, columns] = dot(normed[...], in_ref[:, columns])
    product = (projected[:, :512] * projected[:, 1024:]).astype(BF16).astype(F32)
    for slot in range(4):
        rows = slice(slot * 128, (slot + 1) * 128)
        main, one, two = shifted(product, slot)
        conv = taps[0:1] * two + taps[1:2] * one + taps[2:3] * main
        conv_sum[rows, :] = conv
        gated[rows, :] = (projected[rows, 512:1024] * conv).astype(BF16)
    partial[...] = dot(gated[:256, :], out_ref[...])
    peer[...] = dot(gated[256:, :], out_ref[...])
    normed_turned[...] = normed[...].T
    gated_turned[...] = gated[...].T


def conv_forward(*args):
    return pl.pallas_call(
        conv_kernel,
        out_shape=[
            jax.ShapeDtypeStruct((1024, 528), BF16),
            jax.ShapeDtypeStruct((512, 512), BF16),
            jax.ShapeDtypeStruct((528, 1536), F32),
            jax.ShapeDtypeStruct((512, 512), F32),
            jax.ShapeDtypeStruct((256, 1024), F32),
            jax.ShapeDtypeStruct((256, 1024), F32),
        ],
        in_specs=[VMEM] * 5,
        out_specs=[VMEM] * 6,
        scratch_shapes=[pltpu.VMEM((528, 1024), BF16), pltpu.VMEM((512, 512), BF16)],
        compiler_params=PARAMS,
    )(*args)


def conv_back_kernel(
    grad_mine, grad_other, out_ref, projected, conv_sum, gated_turned, normed_turned, chip, in_ref, taps, sum_feed,
    partial, away, own, grad, block, grad_out,
):
    grad_out[:256, :] = grad_mine[...]
    grad_out[256:, :] = grad_other[...]
    gated_back = dot_t(grad_out[...], out_ref[...])
    grad_conv = (gated_back * projected[:512, 512:1024]).astype(BF16).astype(F32)
    grad[:512, 512:1024] = (gated_back * conv_sum[...]).astype(BF16)
    product = (projected[:, :512] * projected[:, 1024:]).astype(BF16).astype(F32)
    sums = [jnp.zeros((1, 512), F32)] * 3
    rim = []
    for slot in range(4):
        rows = slice(slot * 128, (slot + 1) * 128)
        back = grad_conv[rows]
        row = lax.broadcasted_iota(jnp.int32, back.shape, 0)
        one = jnp.where(row == 127, 0.0, pltpu.roll(back, 127, 0))
        two = jnp.where(row >= 126, 0.0, pltpu.roll(back, 126, 0))
        grad_product = taps[0:1] * two + taps[1:2] * one + taps[2:3] * back
        grad[rows, :512] = (grad_product * projected[rows, 1024:]).astype(BF16)
        grad[rows, 1024:] = (grad_product * projected[rows, :512]).astype(BF16)
        rim.append(taps[0:1] * back[0:1])
        rim.append(taps[0:1] * back[1:2] + taps[1:2] * back[0:1])
        main, behind, further = shifted(product, slot)
        for j, value in enumerate((further, behind, main)):
            sums[j] = sums[j] + jnp.sum(back * value, axis=0, keepdims=True)
    rim = jnp.concatenate(rim + [jnp.zeros((8, 512), F32)], 0)
    grad[512:, :512] = (rim * projected[512:, 1024:]).astype(BF16)
    grad[512:, 512:1024] = jnp.zeros((16, 512), BF16)
    grad[512:, 1024:] = (rim * projected[512:, :512]).astype(BF16)
    partial[...] = dot_t(grad[...], in_ref[...])
    inputs = chip[...].astype(F32)
    sum_mixer = jnp.sum(partial[...] * inputs * root(inputs), axis=0, keepdims=True)
    zeros = jnp.zeros((1, 64), F32)
    wide = [
        jnp.concatenate([part for g in range(8) for part in (total[:, g * 64 : (g + 1) * 64], zeros)], 1)
        for total in sums
    ]
    small = jnp.concatenate([sum_mixer, sum_feed[...], *wide, jnp.zeros((123, 1024), F32)], 0).T
    x = lax.axis_index("xl")
    for z in range(4):
        columns = slice(z * 256, (z + 1) * 256)
        block[:, :1536] = dot(normed_turned[columns, :], grad[...]).astype(BF16)
        total = dot(gated_turned[z * 128 : (z + 1) * 128, :], grad_out[...]).astype(BF16)
        for part in range(4):
            corner = total[(part // 2) * 64 : (part // 2 + 1) * 64, (part % 2) * 512 : (part % 2 + 1) * 512]
            block[part * 64 : (part + 1) * 64, 1536:2048] = corner
        block[:, 2048:] = small[columns].astype(BF16)
        cut(block, x, 128, z, away, own)


def conv_back(*args):
    return pl.pallas_call(
        conv_back_kernel,
        out_shape=[
            jax.ShapeDtypeStruct((528, 1024), F32),
            jax.ShapeDtypeStruct((512, 2176), BF16),
            jax.ShapeDtypeStruct((512, 2176), BF16),
        ],
        in_specs=[VMEM] * 11,
        out_specs=[VMEM] * 3,
        scratch_shapes=[
            pltpu.VMEM((528, 1536), BF16),
            pltpu.VMEM((256, 2176), BF16),
            pltpu.VMEM((512, 1024), BF16),
        ],
        compiler_params=WIDE,
    )(*args)


def cut(block, x, rows, z, away, own):
    other = pl.multiple_of((1 - x) * rows, 32)
    mine = pl.multiple_of(x * rows, 32)
    away[z * rows : (z + 1) * rows, :] = block[pl.ds(other, rows), :]
    own[z * rows : (z + 1) * rows, :] = block[pl.ds(mine, rows), :]


def feed_kernel(sets, mine, other, branch, *refs):
    n_in = sum(count for count, _ in sets)
    parts, refs = refs[:n_in], refs[n_in:]
    out_mine, out_other, in_mine, in_other, gate_rows, up_away, up_own, down_away, down_own = refs[:9]
    normed, turned, gate_pre, up_pre, hidden, grad_gate, grad_up, block, tall = refs[9:18]
    wholes, sems = refs[18:21], refs[21:24]
    step = pl.program_id(0)
    x = lax.axis_index("xl")
    copies, at = [], 0
    for (count, moves), whole, sem in zip(sets, wholes, sems):
        copies.append(copies_of(parts[at : at + count], (whole,), sem, moves))
        at += count

    def arrived(which):
        @pl.when(step == 0)
        def _():
            for copy in copies[which]:
                copy.wait()

    columns = pl.ds(pl.multiple_of(step * 1152, 128), 1152)

    @pl.when(step == 0)
    def _():
        for which in copies:
            for copy in which:
                copy.start()
        for ref in (out_mine, out_other, in_mine, in_other):
            ref[...] = jnp.zeros_like(ref)
        normed[:256, :] = mine[...]
        normed[256:, :] = other[...]
        turned[...] = normed[...].T

    arrived(0)
    gate = wholes[0][:, :, :, columns].reshape(1024, 1152)
    gate_pre[...] = dot(normed[...], gate)
    arrived(1)
    up = wholes[1][:, :, columns].reshape(1024, 1152)
    up_pre[...] = dot(normed[...], up)
    arrived(2)
    down = wholes[2][pl.ds(2 * step, 2)].reshape(1152, 1024)
    grad_hid = dot_t(branch[...], down)
    for part in range(4):
        rows = slice(part * 128, (part + 1) * 128)
        grad_hidden = grad_hid[rows, :]
        sigmoid = jax.nn.sigmoid(gate_pre[rows, :])
        silu = gate_pre[rows, :] * sigmoid
        hidden[rows, :] = (silu * up_pre[rows, :]).astype(BF16)
        grad_up[rows, :] = (grad_hidden * silu).astype(BF16)
        slope = grad_hidden * up_pre[rows, :] * sigmoid * (1.0 + gate_pre[rows, :] * (1.0 - sigmoid))
        grad_gate[rows, :] = slope.astype(BF16)
    for rows, out_part, in_part in ((slice(0, 256), out_mine, in_mine), (slice(256, 512), out_other, in_other)):
        out_part[...] += dot(hidden[rows, :], down)
        in_part[...] += dot_t(grad_gate[rows, :], gate) + dot_t(grad_up[rows, :], up)
    tall[...] = t_dot(hidden[...], branch[...]).astype(BF16)
    for part in range(2):
        for target, source in ((down_away, 2 * part + 1 - x), (down_own, 2 * part + x)):
            for i in range(18):
                at = pl.multiple_of(source * 288 + i * 16, 16)
                rows = tall[pl.ds(at, 16), :]
                for j in range(8):
                    target[part * 128 + j * 16 : part * 128 + (j + 1) * 16, i * 128 : (i + 1) * 128] = rows[
                        :, j * 128 : (j + 1) * 128
                    ]

    for z in range(4):
        rows = turned[z * 256 : (z + 1) * 256, :]
        block[...] = dot(rows, grad_gate[...]).astype(BF16)
        for source in range(2):
            for y in range(4):
                at = z * 64 + source * 32
                gate_rows[y, at : at + 32, :] = block[source * 128 + y * 32 : source * 128 + (y + 1) * 32, :]
        block[...] = dot(rows, grad_up[...]).astype(BF16)
        cut(block, x, 128, z, up_away, up_own)


def feed_forward(mine, other, branch, *weights):
    sets = [(len(pieces), moves) for pieces, _, moves in weights]
    parts = [piece for pieces, _, _ in weights for piece in pieces]
    whole = lambda *shape: pl.BlockSpec(shape, lambda i: (0, 0), pipeline_mode=pl.Buffered(1))
    total = lambda *shape: pl.BlockSpec(shape, lambda i: (0, 0))
    columns = lambda rows: pl.BlockSpec((rows, 1152), lambda i: (0, i))
    outs = pl.pallas_call(
        functools.partial(feed_kernel, sets),
        grid=(2,),
        out_shape=[
            *[jax.ShapeDtypeStruct((256, 1024), F32)] * 4,
            jax.ShapeDtypeStruct((4, 256, 2304), BF16),
            *[jax.ShapeDtypeStruct((512, 2304), BF16)] * 4,
        ],
        in_specs=[
            whole(256, 1024),
            whole(256, 1024),
            whole(512, 1024),
            *[ANY] * len(parts),
        ],
        out_specs=[
            *[total(256, 1024)] * 4,
            pl.BlockSpec((4, 256, 1152), lambda i: (0, 0, i)),
            *[columns(512)] * 2,
            *[pl.BlockSpec((256, 2304), lambda i: (i, 0))] * 2,
        ],
        scratch_shapes=[
            pltpu.VMEM((512, 1024), BF16),
            pltpu.VMEM((1024, 512), BF16),
            *[pltpu.VMEM((512, 1152), F32)] * 2,
            *[pltpu.VMEM((512, 1152), BF16)] * 3,
            pltpu.VMEM((256, 1152), BF16),
            pltpu.VMEM((1152, 1024), BF16),
            *[pltpu.VMEM(shape, BF16) for _, shape, _ in weights],
            *[pltpu.SemaphoreType.DMA((len(moves),)) for _, _, moves in weights],
        ],
        compiler_params=WIDE,
    )(mine, other, branch, *parts)
    return outs[:4], outs[4], outs[5:7], outs[7:9]


def norm_back_kernel(middle, here, there, gain, branch, grad_total, grad_out, sum_gain):
    values, grad = middle[...], here[...] + there[...]
    back, total = root_back(values, gain[...], grad)
    total_grad = branch[...].astype(F32) + back
    grad_total[...] = total_grad
    grad_out[...] = total_grad.astype(BF16)
    sum_gain[...] = total[None]


def norm_back(*args):
    return pl.pallas_call(
        norm_back_kernel,
        out_shape=[
            jax.ShapeDtypeStruct((256, 1024), F32),
            jax.ShapeDtypeStruct((256, 1024), BF16),
            jax.ShapeDtypeStruct((1, 1024), F32),
        ],
        in_specs=[VMEM] * 5,
        out_specs=[VMEM] * 3,
        compiler_params=PARAMS,
    )(*args)


def square_kernel(inverse, feed, gate, mix, small, feed_moment, mix_moment, target):
    target[...] = jnp.zeros_like(target)

    def fold(row, grad, moment):
        blend = 0.9 * moment + 0.1 * (grad.astype(F32) * inverse[0])
        square = jnp.sum(blend * blend, axis=0, keepdims=True)
        total = square[:, :128]
        for j in range(1, square.shape[1] // 128):
            total = total + square[:, j * 128 : (j + 1) * 128]
        target[row : row + 1, :] = total

    fold(0, mix[:, :1536], mix_moment[:, :1536])
    fold(1, mix[:, 1536:2048], mix_moment[:, 1536:2048])
    fold(3, gate[...], feed_moment[32:, :])
    fold(4, feed[16:, :], feed_moment[16:32, :])
    fold(5, feed[:16, :], feed_moment[:16, :])
    mine, other = mix[:, 2048:2176].astype(F32), small[...].astype(F32)
    lane = lax.broadcasted_iota(jnp.int32, mine.shape, 1)
    blend = 0.9 * mix_moment[:, 2048:] + 0.1 * (jnp.where(lane < 2, mine + other, mine) * inverse[0])
    once = jnp.where(lane >= 2, 1.0, jnp.where(lax.axis_index("core") == 0, 1.0, 0.0))
    target[2:3, :] = jnp.sum(blend * blend * once, axis=0, keepdims=True)


def piece_squares(*args):
    return pl.pallas_call(
        square_kernel,
        out_shape=jax.ShapeDtypeStruct((8, 128), F32),
        in_specs=[SMEM] + [VMEM] * 6,
        out_specs=VMEM,
        compiler_params=LIGHT,
    )(*args)


def sum_over(value, *axes):
    for axis in axes:
        back, on, far = around(value, axis)
        value = (value + far) + (on + back)
    return value


def returned(mine_ref, other_ref):
    mine, other = mine_ref[...].astype(F32), other_ref[...].astype(F32)
    zero = lax.axis_index("core") == 0
    return jnp.where(zero, mine, other), jnp.where(zero, other, mine)


def update_kernel(kind, row, scalars, totals, w_ref, m_ref, mine_ref, other_ref, w_new, m_new, grad):
    for core, share in enumerate(returned(mine_ref, other_ref)):
        if kind == "rows":
            for i in range(18):
                for j in range(8):
                    rows = slice(core * 288 + i * 16, core * 288 + (i + 1) * 16)
                    grad[rows, j * 128 : (j + 1) * 128] = share[
                        j * 16 : (j + 1) * 16, i * 128 : (i + 1) * 128
                    ]
        else:
            for j in range(share.shape[1] // kind):
                grad[:, (2 * j + core) * kind : (2 * j + core + 1) * kind] = share[
                    :, j * kind : (j + 1) * kind
                ]
    m, w = m_ref[...], w_ref[...]
    mean = grad[...] * scalars[0]
    blend = 0.9 * m + 0.1 * mean
    m_new[...] = 0.5 * m + 0.5 * mean
    square = jnp.sum(totals[row : row + 1, :], axis=1, keepdims=True)
    scale = lax.rsqrt(square / (w.size * 8) + 1e-06)
    w_new[...] = w - scalars[1] * (jnp.tanh(2.0 * blend * scale) + 0.1 * w)


def update(kind, row, scalars, totals, weight, moment, mine, other):
    return pl.pallas_call(
        functools.partial(update_kernel, kind, row),
        out_shape=[jax.ShapeDtypeStruct(weight.shape, F32)] * 2,
        in_specs=[SMEM] + [VMEM] * 5,
        out_specs=[VMEM, VMEM],
        scratch_shapes=[pltpu.VMEM(weight.shape, F32)],
        compiler_params=PARAMS,
    )(scalars, totals, weight, moment, mine, other)


def mix_update_kernel(
    scalars, totals, mine, other, in_w, in_m, out_w, out_m, conv_w, conv_m, mixer_w, mixer_m, feed_w, feed_m,
    in_wn, in_mn, out_wn, out_mn, conv_wn, conv_mn, mixer_wn, mixer_mn, feed_wn, feed_mn, grad, wide,
):
    def step(grad, square, count, w_ref, m_ref, w_new, m_new):
        m, w = m_ref[...], w_ref[...]
        mean = grad * scalars[0]
        scale = lax.rsqrt(square / count + 1e-06)
        m_new[...] = 0.5 * m + 0.5 * mean
        move = jnp.tanh(2.0 * (0.9 * m + 0.1 * mean) * scale) + 0.1 * w
        w_new[...] = w - scalars[1] * move

    first, second = returned(mine, other)
    for core, half in enumerate((first, second)):
        for j in range(24):
            grad[:, (2 * j + core) * 64 : (2 * j + core + 1) * 64] = half[:, j * 64 : (j + 1) * 64]
        wide[core * 64 : (core + 1) * 64, :512] = half[:64, 1536:2048]
        wide[core * 64 : (core + 1) * 64, 512:] = half[64:, 1536:2048]
    total = lambda row: jnp.sum(totals[row : row + 1, :], axis=1, keepdims=True)
    step(grad[...], total(0), 1024 * 3072, in_w, in_m, in_wn, in_mn)
    step(wide[...], total(1), 1024 * 1024, out_w, out_m, out_wn, out_mn)
    one, two = first[:, 2048:2176].T, second[:, 2048:2176].T
    lane = lax.broadcasted_iota(jnp.int32, (1, 128), 1)
    among = lambda low, high: jnp.sum(
        jnp.where((lane >= low) & (lane < high), totals[2:3, :], 0.0), axis=1, keepdims=True
    )
    taps = jnp.where(lane < 64, one[2:5], pltpu.roll(two[2:5], 64, 1))
    step(taps, among(2, 5), 3 * 1024, conv_w, conv_m, conv_wn, conv_mn)
    step(one[0:1] + two[0:1], among(0, 1), 1024, mixer_w, mixer_m, mixer_wn, mixer_mn)
    step(one[1:2] + two[1:2], among(1, 2), 1024, feed_w, feed_m, feed_wn, feed_mn)


def mix_update(scalars, totals, first, second, *arrays):
    shapes = [jax.ShapeDtypeStruct(v.shape, F32) for v in arrays]
    return pl.pallas_call(
        mix_update_kernel,
        out_shape=shapes,
        in_specs=[SMEM] + [VMEM] * (3 + len(arrays)),
        out_specs=[VMEM] * len(arrays),
        scratch_shapes=[pltpu.VMEM((128, 3072), F32), pltpu.VMEM((128, 1024), F32)],
        compiler_params=PARAMS,
    )(scalars, totals, first, second, *arrays)


def dot(left, right):
    return jnp.dot(left, right, preferred_element_type=F32)


def dot_t(left, right):
    return lax.dot_general(left, right, (((1,), (1,)), ((), ())), preferred_element_type=F32)


def t_dot(left, right):
    return lax.dot_general(left, right, (((0,), (0,)), ((), ())), preferred_element_type=F32)


def root(values):
    return lax.rsqrt(jnp.mean(values * values, axis=-1, keepdims=True) + 1e-05)


def root_back(values, gain, grad):
    r = root(values)
    inner = jnp.mean(grad * gain * values, axis=-1, keepdims=True)
    back = r * grad * gain - values * (r * r * r) * inner
    return back, jnp.sum(grad * values * r, axis=0)


def shards(
    tokens,
    cotangent,
    lengths,
    step_rate,
    in_weight,
    out_weight,
    conv_weight,
    gain_mixer,
    gain_feed,
    gate_weight,
    up_weight,
    down_weight,
    in_moment,
    out_moment,
    conv_moment,
    mixer_moment,
    feed_moment,
    gate_moment,
    up_moment,
    down_moment,
):
    core = lax.axis_index("core")
    group = lax.axis_index(G)
    rate = step_rate[0]
    slots, length, width = tokens.shape
    rows = slots * length
    half = width // 2

    taps = lax.dynamic_slice_in_dim(conv_weight, core * 64, 64, 1)
    taps = jnp.pad(taps, ((0, 0), (0, 64)))
    small = jnp.concatenate([gain_mixer[None], gain_feed[None], taps], 0).T
    small = jnp.pad(small, ((0, 0), (0, 123)))
    mix_part = mix_share(in_weight, out_weight, small)
    gate_part = share(288, gate_weight)
    up_part = share(288, up_weight)
    down_part = lax.dynamic_slice_in_dim(down_weight, core * 288, 288, 0).astype(BF16)

    up_quarter = lax.dynamic_slice_in_dim(up_part, lax.axis_index("y") * 32, 32, 0)
    up_quarters = spread(up_quarter, G, 8).reshape(8, 32, 2304)
    piece = lax.axis_index(CHIPS)
    sixteen = lambda value: lax.dynamic_slice_in_dim(value, piece * 16, 16, 0)
    down_moments = lax.dynamic_slice(down_moment, (core * 288, piece * 128), (288, 128))
    down_moments = down_moments.reshape(18, 16, 128).transpose(1, 0, 2).reshape(16, 2304)
    feed_moments = jnp.concatenate(
        [down_moments, share(288, sixteen(up_moment), F32), share(288, sixteen(gate_moment), F32)], 0
    )
    out_moments = lax.dynamic_slice(
        out_moment, (core * 64 + piece % 4 * 16, piece // 4 * half), (16, half)
    )
    tap_moments = lax.dynamic_slice(conv_moment, (0, core * 64 + piece % 4 * 16), (3, 16))
    tap_moments = jnp.where(piece < 4, tap_moments, 0.0)
    small_moments = jnp.concatenate(
        [sixteen(mixer_moment)[None], sixteen(feed_moment)[None], tap_moments], 0
    ).T
    small_moments = jnp.pad(small_moments, ((0, 0), (0, 123)))
    mix_moments = jnp.concatenate(
        [share(64, sixteen(in_moment), F32), out_moments, small_moments], 1
    )
    mix_z = around(mix_part, "z")
    own = tokens.reshape(rows, width)
    rim = from_behind(after(tokens[:, length - 2 :], mix_z[0], mix_z[1]), 1).reshape(2 * slots, width)
    positions = group * length + jnp.arange(length, dtype=jnp.int32)
    valid = (positions[None, :] < lengths[:, None]).reshape(rows, 1)
    branch_own = jnp.where(valid, cotangent.reshape(rows, width), 0).astype(BF16)
    swapped = swap(own), swap(rim), swap(branch_own)

    down_other = across(down_part)
    gate_part, up_quarters, down_other, *both = lax.optimization_barrier(
        (gate_part, up_quarters, down_other, *swapped, *mix_z)
    )
    swapped, mix_z = both[:3], both[3:]
    pad = jnp.zeros((8, width), BF16)
    chip = jnp.concatenate([own, swapped[0], rim, swapped[1], pad], 0)
    branch = jnp.concatenate([branch_own, swapped[2]], 0)
    total_length = after(jnp.sum(lengths).astype(F32), mix_z[0])
    counts = jnp.broadcast_to(total_length, (16, 128))
    count = jnp.sum(lax.all_to_all(counts, DP, 0, 0, tiled=True)[:, 0])
    inverse = jnp.reshape(1.0 / count, (1,))
    mix_x = other_x((mix_part, *mix_z))
    gate_z = around(gate_part, "z")
    down_pair = jnp.concatenate([down_part, down_other])
    down_pair, inverse, up_quarters, *both = lax.optimization_barrier(
        (down_pair, inverse, up_quarters, mix_x, *gate_z)
    )
    mix_x, gate_z = both[0], both[1:]
    gate_x = other_x((gate_part, *gate_z))
    up_near = ring(up_quarters, "y", 1), ring(up_quarters, "y", -1)
    down_z = ring(down_pair, "z", 1), ring(down_pair, "z", -1)
    in_full, out_full, small_full = place_mix((mix_part, *mix_z, mix_x))

    gains = small_full[:, :, :2].reshape(width, 2).astype(F32)
    mixer_gain, feed_gain = gains[:, 0][None], gains[:, 1][None]
    kernel = small_full[:, :64, 2:5].reshape(half, 3).astype(F32).T

    normed_turned, gated_turned, projected, conv_sum, partial, peer = conv_forward(
        chip, in_full, mixer_gain, kernel, out_full
    )
    peer, feed_moments, mix_moments, gate_x, *both = lax.optimization_barrier(
        (peer, feed_moments, mix_moments, gate_x, *down_z, *up_near)
    )
    down_z, up_near = both[:2], both[2:]
    top, bottom = pl.ds(0, 288), pl.ds(288, 288)
    low, high = pl.ds(0, 4), pl.ds(4, 4)
    all_of = lambda z, x: (slice(None),)
    halves = place(
        (*down_z, *up_near),
        [(288, 1024), (288, 1024), (4, 32, 2304), (4, 32, 2304)],
        [(0, (top,), 0, all_of), (1, (bottom,), 1, all_of), (2, (low,), 2, all_of), (3, (high,), 3, all_of)],
    )
    down_far = ring(halves[0], "z", 1), ring(halves[1], "z", -1)
    up_far = ring(halves[2], "y", 1), ring(halves[3], "y", -1)
    up_set = place_quarters((up_quarters, *up_near, *up_far))
    gate_set = place_whole((gate_part, *gate_z, gate_x))
    down_set = place_pair(down_pair, *down_z, *down_far)
    inputs_own = own.astype(F32)
    middle = inputs_own + (partial + swap(peer))
    normed_own = (middle * root(middle) * feed_gain).astype(BF16)
    partials, gate_dots, up_dots, down_dots = feed_forward(
        normed_own, swap(normed_own), branch, gate_set, up_set, down_set
    )

    grad_total, grad_out, sum_feed = norm_back(
        middle, partials[2], swap(partials[3]), feed_gain, branch[:rows]
    )
    partial_in, *mix_dots = conv_back(
        grad_out,
        swap(grad_out),
        out_full,
        projected,
        conv_sum,
        gated_turned,
        normed_turned,
        chip,
        in_full,
        kernel,
        sum_feed,
    )
    mine = lax.axis_index("xl")
    down_here = x_sum(*down_dots, mix_dots[0])
    up_here = x_sum(*up_dots, mix_dots[0])
    mix_here = x_sum(*mix_dots)
    down_part = ring_sum(down_here.reshape(4, 128, 2304), "z")
    gate_pieces = after(lax.all_to_all(gate_dots, "y", 0, 0, tiled=True), mix_dots[0])
    gate_here = jnp.sum(gate_pieces.astype(F32), axis=0).astype(BF16)
    gate_blocks = gate_here.reshape(4, 2, 32, 2304)
    gate_here = x_sum(pick(gate_blocks, 1 - mine, 1), pick(gate_blocks, mine, 1))
    mix_wide = jnp.pad(mix_here.reshape(4, 128, 2176), ((0, 0), (0, 0), (0, 128)))
    last_picks = ring_picks(jnp.concatenate([mix_wide, gate_here], 1), "z")
    up_part = ring_sum(up_here.reshape(4, 128, 2304), "z", *last_picks[1:])
    feed_part = jnp.concatenate([down_part.reshape(8, 16, 2304), up_part.reshape(8, 16, 2304)], 1)
    feed_pieces = lax.all_to_all(feed_part, CHIPS, 0, 0, tiled=True)
    feed_piece = jnp.sum(feed_pieces.astype(F32), axis=0).astype(BF16)
    last_part = near_far_sum(last_picks, "z", feed_part, feed_pieces)
    mix_part, gate_halves = last_part(slice(0, 128)), last_part(slice(128, 160)).reshape(2, 16, 2304)
    half_index = lax.axis_index("xh")
    gate_away = lax.ppermute(pick(gate_halves, 1 - half_index, 0), "xh", [(0, 1), (1, 0)])
    gate_piece = add(pick(gate_halves, half_index, 0), gate_away)
    output = middle + (partials[0] + swap(after(partials[1], mix_part)))
    block_out = output.astype(BF16).reshape(slots, length, width)
    split = 2 * rows + 2 * slots
    here_in = jnp.concatenate([partial_in[:rows], partial_in[2 * rows : split]], 0)
    there_in = jnp.concatenate([partial_in[rows : 2 * rows], partial_in[split : split + 2 * slots]], 0)
    grad_normed = here_in + swap(after(there_in, mix_part))
    inputs_rim = jnp.concatenate([inputs_own, rim.astype(F32)], 0)
    grad_inputs, _ = root_back(inputs_rim, mixer_gain, grad_normed)

    mix_piece = piece_sum(after(mix_part, feed_pieces).reshape(8, 16, 2304), block_out, grad_inputs)
    squares = piece_squares(
        inverse,
        feed_piece,
        gate_piece,
        mix_piece,
        swap(mix_piece[:, 2048:2176]),
        feed_moments,
        mix_moments,
    )
    squares = sum_over(squares + swap(squares), "z")
    pieces = jnp.concatenate([feed_piece, gate_piece, mix_piece], 0)
    back_mine = after(spread(pieces, CHIPS, 8), squares).reshape(8, 64, 2304)
    back_other = swap(back_mine)
    squares = sum_over(after(squares, back_mine), X)
    rim_inputs = from_behind(after(grad_inputs[rows:], squares).reshape(slots, 2, width), -1)
    grad_tokens = (grad_total + grad_inputs[:rows]).reshape(slots, length, width)
    grad_tokens = grad_tokens + jnp.pad(rim_inputs, ((0, 0), (length - 2, 0), (0, 0)))
    grad_tokens = grad_tokens.astype(BF16)
    totals = sum_over(squares, "y")

    scalars = jnp.stack([inverse[0], rate])
    shares = [
        [v[:, at : at + 16].reshape(128, 2304) for v in (back_mine, back_other)] for at in (0, 16, 32, 48)
    ]
    down_new = update("rows", 5, scalars, totals, down_weight, down_moment, *shares[0])
    up_new = update(288, 4, scalars, totals, up_weight, up_moment, *shares[1])
    gate_new = update(288, 3, scalars, totals, gate_weight, gate_moment, *shares[2])
    news = mix_update(
        scalars,
        totals,
        *shares[3],
        in_weight,
        in_moment,
        out_weight,
        out_moment,
        conv_weight,
        conv_moment,
        gain_mixer[None],
        mixer_moment[None],
        gain_feed[None],
        feed_moment[None],
    )
    in_new, out_new, conv_new = news[0:2], news[2:4], news[4:6]
    mixer_new, feed_new = [v[0] for v in news[6:8]], [v[0] for v in news[8:10]]
    news = (in_new, out_new, conv_new, mixer_new, feed_new, gate_new, up_new, down_new)
    return (block_out, grad_tokens, *[new[0] for new in news], *[new[1] for new in news])


def solution(mesh):
    fine = Mesh(mesh.devices.reshape(4, 2, 2, 4, 2), ("y", "xh", "core", "z", "xl"))
    rows = P(G, None)
    flat = P(G)
    taps = P(None, G)
    slots = P(DP, G, None)
    weights = (rows, rows, taps, flat, flat, rows, rows, rows)
    return jax.shard_map(
        shards,
        mesh=fine,
        in_specs=(slots, slots, P(DP), P(), *weights, *weights),
        out_specs=(slots, slots, *weights, *weights),
        check_vma=False,
    )
```
